32 devices in a mesh: dp: 16 (over z, y, x), ctx: 2 (over core).
Axes of the slice: x: 2, y: 2, z: 4, core: 2. Of those that a mesh axis runs over, the one named last changes fastest.
Arguments:
- queries: bfloat16 [16, 512, 1024], P('dp', 'ctx'), may hold values from -7 to 7
- key_states: bfloat16 [16, 512, 1024], P('dp', 'ctx'), may hold values from -7 to 7
- value_states: bfloat16 [16, 512, 1024], P('dp', 'ctx'), may hold values from -6 to 6
- token_order: int32 [16, 512], P('dp', 'ctx'), may hold values from 0 to 511, each once within a row
- block_pattern: int32 [16, 4, 4], P('dp'), may hold values from -1 to 3, as said below
- out_weight: bfloat16 [1024, 2048], P('dp'), may hold values from -0.1875 to 0.1875
- out_grad: bfloat16 [16, 512, 2048], P('dp', 'ctx'), may hold values from -6 to 6
Outputs:
- layer_out: bfloat16 [16, 512, 2048], P('dp', 'ctx')
- query_grad: bfloat16 [16, 512, 1024], P('dp', 'ctx')
- key_grad: bfloat16 [16, 512, 1024], P('dp', 'ctx')
- value_grad: bfloat16 [16, 512, 1024], P('dp', 'ctx')
- weight_grad: float32 [1024, 2048], P('dp')
The draws below stay inside these ranges and needn't reach their ends.
Inputs may be any that keep to these rules, and one draw needn't show every extreme that they name: `block_pattern`: row b of a session lists key blocks of the same session, each within 2 blocks of b, none twice; slot 0 holds b itself, used slots come before the slots that hold -1, and a row is full whenever 4 blocks lie within that reach.
All inputs are finite; a program needn't handle non-finite values.
Results may differ from the reference program's by a relative error of at most 0.012.
Values may be sent and summed in bfloat16 or wider, within the bound.
No kernel may reach another device: no remote copies, remote signals or barrier semaphores. Data moves between devices by JAX's collectives and lax.ppermute only.
A program may use at most 128 MiB of HBM per device.

```python
import math
import jax
import jax.numpy as jnp
from jax import lax

D = 2048
H = 8
HD = 128
BLK = 128
KB = 4
HW = 1024
BATCH = 16
SEQ = 512
NB = 4
BDEV = 2


def drawn_pair(key):
    draw_shape = (BATCH, SEQ, H, HD)
    query_vals = jnp.clip(jax.random.normal(jax.random.fold_in(key, 1), draw_shape, jnp.float32), -4.0, 4.0)
    key_vals = jnp.clip(jax.random.normal(jax.random.fold_in(key, 2), draw_shape, jnp.float32), -4.0, 4.0)
    return (query_vals.reshape(BATCH, SEQ, H * HD), key_vals.reshape(BATCH, SEQ, H * HD))


def draw_queries(key, part):
    return drawn_pair(key)[0].astype(jnp.bfloat16)


def draw_key_states(key, part):
    return drawn_pair(key)[1].astype(jnp.bfloat16)


def draw_block_pattern(key, part):
    span_width = 2 * BDEV + 1
    offsets = jnp.arange(span_width) - BDEV
    blocks = jnp.arange(NB)[:, None] + offsets[None, :]
    inside = (blocks >= 0) & (blocks < NB)
    noise_ints = jax.random.randint(key, (BATCH, NB, span_width), 0, 1 << 20)
    score_ints = noise_ints * 64 + jnp.arange(span_width)
    score_ints = jnp.where(offsets == 0, 1 << 30, score_ints)
    score_ints = jnp.where(inside, score_ints, -1 - jnp.arange(span_width))
    top_slots = lax.top_k(score_ints, KB)[1]
    chosen = jnp.take_along_axis(jnp.broadcast_to(blocks, (BATCH, NB, span_width)), top_slots, axis=-1)
    usable = jnp.take_along_axis(jnp.broadcast_to(inside, (BATCH, NB, span_width)), top_slots, axis=-1)
    return jnp.where(usable, chosen, -1).astype(jnp.int32)


def block_levels(stream_key, shape, cuts, low, top_value):
    def one(axis_at, parts):
        draws = jax.random.uniform(jax.random.fold_in(jax.random.fold_in(stream_key, 6), axis_at), (parts,), jnp.float32, low / len(cuts), top_value / len(cuts))
        return jnp.repeat(jnp.exp(draws), shape[axis_at] // parts).reshape((-1,) + (1,) * (len(shape) - axis_at - 1))

    level = one(*cuts[0])
    for cut in cuts[1:]:
        level = level * one(*cut)
    return level


def gaussian(stream_key, extent, spread, bound, pieces=(), held_as=jnp.bfloat16):
    level = block_levels(stream_key, extent, pieces, -0.22, 0.18) if pieces else 1.0
    drawn = jax.random.normal(stream_key, extent, jnp.float32) * spread * level
    return jnp.minimum(jnp.maximum(drawn, -bound), bound).astype(held_as)


def setup_inputs(seed: int = 0) -> dict:
    streams_of = jax.random.split(jax.random.key(seed), 8)
    queries = draw_queries(jax.random.fold_in(streams_of[7], 71), 0)
    key_states = draw_key_states(jax.random.fold_in(streams_of[7], 71), 0)
    value_states = gaussian(streams_of[2], (BATCH, SEQ, HW), 1.0, 6.0, ((0, 16), (1, 2)))
    token_order = jax.vmap(lambda own: jax.random.permutation(own, SEQ))(jax.random.split(streams_of[3], BATCH)).reshape((BATCH, SEQ)).astype(jnp.int32)
    block_pattern = draw_block_pattern(jax.random.fold_in(streams_of[7], 71), 0)
    out_weight = gaussian(streams_of[5], (HW, D), HW ** -0.5, 0.1875, ((0, 16),))
    out_grad = gaussian(streams_of[6], (BATCH, SEQ, D), 1.0, 6.0, ((0, 16), (1, 2)))
    return dict(queries=queries, key_states=key_states, value_states=value_states, token_order=token_order, block_pattern=block_pattern, out_weight=out_weight, out_grad=out_grad)


def rope_tables(positions):
    coords = jnp.stack([positions % 8, positions // 8 % 8, positions // 64 % 4, positions // 256], axis=1).astype(jnp.float32)
    per_axis = HD // 16
    frequency = 100.0 ** (-jnp.arange(per_axis, dtype=jnp.float32) / per_axis)
    angle = (coords[:, :, None] * frequency[None, None, :]).reshape(positions.shape[0], 4 * per_axis)
    return (jnp.cos(angle), jnp.sin(angle))

def rotate_heads(heads, cosine, sine_vals, direction):
    quarter = HD // 4
    first_part = heads[..., :quarter]
    second_part = heads[..., quarter:2 * quarter]
    cos_rows = cosine[:, None, :]
    sin_rows = direction * sine_vals[:, None, :]
    return jnp.concatenate([first_part * cos_rows - second_part * sin_rows, second_part * cos_rows + first_part * sin_rows, heads[..., 2 * quarter:]], axis=-1)

def block_sets(table, slots):
    return jnp.take(table, slots, axis=0).reshape(KB * BLK, H, HD)

def session_pass(queries, key_states, value_states, token_order, block_pattern, out_grad, out_weight):
    cosine, sine_vals = rope_tables(token_order)
    rot_query = rotate_heads(queries.astype(jnp.float32).reshape(SEQ, H, HD), cosine, sine_vals, 1.0).astype(jnp.bfloat16)
    rot_keys = rotate_heads(key_states.astype(jnp.float32).reshape(SEQ, H, HD), cosine, sine_vals, 1.0).astype(jnp.bfloat16)
    query_table = rot_query.reshape(NB, BLK, H, HD)
    key_table = rot_keys.reshape(NB, BLK, H, HD)
    value_table = value_states.reshape(NB, BLK, H, HD)
    slot_valid = block_pattern >= 0
    slot_index = jnp.where(slot_valid, block_pattern, 0).astype(jnp.int32)
    score_scale = 1.0 / math.sqrt(HD)

    def block_scores(query_block, slots, valid):
        key_set = block_sets(key_table, slots)
        scores = jnp.einsum('qhd,khd->hqk', query_block.astype(jnp.float32), key_set.astype(jnp.float32)) * score_scale
        key_mask = jnp.repeat(valid, BLK)
        return (jnp.where(key_mask[None, None, :], scores, -jnp.inf), key_set)

    def forward_block(items):
        query_block, slots, valid = items
        scores, key_set = block_scores(query_block, slots, valid)
        value_set = block_sets(value_table, slots)
        row_peak = lax.optimization_barrier(jnp.max(scores, axis=-1))
        row_total = lax.optimization_barrier(jnp.sum(jnp.exp(scores - row_peak[..., None]), axis=-1))
        log_total = row_peak + jnp.log(row_total)
        soft_probs = jnp.exp(scores - log_total[..., None]).astype(jnp.bfloat16)
        block_out = jnp.einsum('hqk,khd->qhd', soft_probs.astype(jnp.float32), value_set.astype(jnp.float32)).astype(jnp.bfloat16)
        return (block_out, log_total)
    block_outs, log_totals = lax.map(forward_block, (query_table, slot_index, slot_valid))
    attn = block_outs.reshape(SEQ, HW)
    layer_out = jnp.dot(attn, out_weight, preferred_element_type=jnp.float32).astype(jnp.bfloat16)
    attn_grad = jnp.dot(out_grad, out_weight.T, preferred_element_type=jnp.float32).astype(jnp.bfloat16)
    weight_term = jnp.dot(attn.T, out_grad, preferred_element_type=jnp.float32)
    grad_dot = lax.optimization_barrier(jnp.sum((attn_grad.astype(jnp.float32) * attn.astype(jnp.float32)).reshape(SEQ, H, HD), axis=-1))
    grad_dot = grad_dot.reshape(NB, BLK, H).transpose(0, 2, 1)
    grad_table = attn_grad.reshape(NB, BLK, H, HD)

    def backward_block(running, items):
        key_sum, value_sum = running
        query_block, slots, valid, log_total, block_dot, grad_block = items
        scores, key_set = block_scores(query_block, slots, valid)
        value_set = block_sets(value_table, slots)
        exact_probs = jnp.exp(scores - log_total[..., None])
        soft_probs = exact_probs.astype(jnp.bfloat16)
        value_part = jnp.einsum('hqk,qhd->khd', soft_probs.astype(jnp.float32), grad_block.astype(jnp.float32))
        prob_grad = jnp.einsum('qhd,khd->hqk', grad_block.astype(jnp.float32), value_set.astype(jnp.float32))
        score_grad = (exact_probs * (prob_grad - block_dot[..., None]) * score_scale).astype(jnp.bfloat16)
        query_part = jnp.einsum('hqk,khd->qhd', score_grad.astype(jnp.float32), key_set.astype(jnp.float32))
        key_part = jnp.einsum('hqk,qhd->khd', score_grad.astype(jnp.float32), query_block.astype(jnp.float32))
        keep = valid.astype(jnp.float32)[:, None, None, None]
        key_sum = key_sum.at[slots].add(key_part.reshape(KB, BLK, H, HD) * keep)
        value_sum = value_sum.at[slots].add(value_part.reshape(KB, BLK, H, HD) * keep)
        return ((key_sum, value_sum), query_part)
    empty = jnp.zeros((NB, BLK, H, HD), jnp.float32)
    (key_sum, value_sum), query_parts = lax.scan(backward_block, (empty, empty), (query_table, slot_index, slot_valid, log_totals, grad_dot, grad_table))
    query_grad = rotate_heads(query_parts.reshape(SEQ, H, HD), cosine, sine_vals, -1.0).reshape(SEQ, HW).astype(jnp.bfloat16)
    key_grad = rotate_heads(key_sum.reshape(SEQ, H, HD), cosine, sine_vals, -1.0).reshape(SEQ, HW).astype(jnp.bfloat16)
    value_grad = value_sum.reshape(SEQ, HW).astype(jnp.bfloat16)
    return (layer_out, query_grad, key_grad, value_grad, weight_term)

def reference(queries, key_states, value_states, token_order, block_pattern, out_weight, out_grad):

    def one_session(running, items):
        outputs = session_pass(items[0], items[1], items[2], items[3], items[4], items[5], out_weight)
        return (running + outputs[4], (outputs[0], outputs[1], outputs[2], outputs[3]))
    start_sum = jnp.zeros((HW, D), jnp.float32)
    weight_sum, stacked = lax.scan(one_session, start_sum, (queries, key_states, value_states, token_order, block_pattern, out_grad))
    return (stacked[0], stacked[1], stacked[2], stacked[3], weight_sum / BATCH)
```

```python
import itertools
import math

import jax
import jax.numpy as jnp
import numpy as np
from jax import lax
from jax.experimental import pallas as pl
from jax.experimental.pallas import tpu as pltpu
from jax.sharding import PartitionSpec as P

H = 8
HD = 128
BLK = 128
KB = 4


def padded(shard, sides, width):
    for axis, dim in sides:
        devices, length = (lax.axis_size(axis), shard.shape[dim])
        up = [(i, (i + 1) % devices) for i in range(devices - 1)]
        down = [(j, i) for i, j in up]
        last = lax.slice_in_dim(shard, length - width, length, axis=dim)
        leading = lax.slice_in_dim(shard, 0, width, axis=dim)
        before = lax.ppermute(last, axis, up)
        after = lax.ppermute(leading, axis, down)
        shard = jnp.concatenate([before, shard, after], axis=dim)
    return shard


def from_behind(block, axis, distance):
    devices = range(lax.axis_size(axis))
    route = [(i - distance, i) for i in devices if i - distance in devices]
    return lax.ppermute(block, axis, route)


def rope_tables(positions):
    coords = jnp.stack(
        [positions % 8, positions // 8 % 8, positions // 64 % 4, positions // 256], axis=1
    ).astype(jnp.float32)
    per_axis = HD // 16
    frequency = 100.0 ** (-jnp.arange(per_axis, dtype=jnp.float32) / per_axis)
    angle = (coords[:, :, None] * frequency[None, None, :]).reshape(
        positions.shape[0], 4 * per_axis
    )
    return (jnp.cos(angle), jnp.sin(angle))


def rotate_heads(heads, cosine, sine_vals, direction):
    quarter = HD // 4
    first_part = heads[..., :quarter]
    second_part = heads[..., quarter : 2 * quarter]
    cos_rows = cosine[:, None, :]
    sin_rows = direction * sine_vals[:, None, :]
    return jnp.concatenate(
        [
            first_part * cos_rows - second_part * sin_rows,
            second_part * cos_rows + first_part * sin_rows,
            heads[..., 2 * quarter :],
        ],
        axis=-1,
    )


def attend_forward(query_blocks, key_sets, value_sets, key_mask, score_scale):
    scores = (
        jnp.einsum("nqhd,nkhd->nhqk", query_blocks, key_sets, preferred_element_type=jnp.float32)
        * score_scale
    )
    scores = jnp.where(key_mask[:, None, None, :], scores, -jnp.inf)
    row_peak = jnp.max(scores, axis=-1)
    row_total = jnp.sum(jnp.exp(scores - row_peak[..., None]), axis=-1)
    log_total = row_peak + jnp.log(row_total)
    soft_probs = jnp.exp(scores - log_total[..., None]).astype(jnp.bfloat16)
    block_out = jnp.einsum(
        "nhqk,nkhd->nqhd", soft_probs, value_sets, preferred_element_type=jnp.float32
    ).astype(jnp.bfloat16)
    return (block_out, log_total)


def attend_backward(
    query_blocks,
    key_sets,
    value_sets,
    key_mask,
    log_total,
    grad_dot,
    grad_blocks,
    score_scale,
    key_form,
):
    scores = (
        jnp.einsum(
            "nqhd," + key_form + "->nhqk",
            query_blocks,
            key_sets,
            preferred_element_type=jnp.float32,
        )
        * score_scale
    )
    scores = jnp.where(key_mask[:, None, None, :], scores, -jnp.inf)
    exact_probs = jnp.exp(scores - log_total[..., None])
    soft_probs = exact_probs.astype(jnp.bfloat16)
    value_part = jnp.einsum(
        "nhqk,nqhd->" + key_form, soft_probs, grad_blocks, preferred_element_type=jnp.float32
    )
    prob_grad = jnp.einsum(
        "nqhd," + key_form + "->nhqk", grad_blocks, value_sets, preferred_element_type=jnp.float32
    )
    score_grad = (exact_probs * (prob_grad - grad_dot[..., None]) * score_scale).astype(
        jnp.bfloat16
    )
    query_part = jnp.einsum(
        "nhqk," + key_form + "->nqhd", score_grad, key_sets, preferred_element_type=jnp.float32
    )
    key_part = jnp.einsum(
        "nhqk,nqhd->" + key_form, score_grad, query_blocks, preferred_element_type=jnp.float32
    )
    return (query_part, key_part, value_part)


def shards(queries, key_states, value_states, token_order, block_pattern, out_weight, out_grad):
    row_count = queries.shape[1]
    feature_width = queries.shape[2]
    local_blocks = row_count // BLK
    shard_index = lax.axis_index("ctx")
    score_scale = 1.0 / math.sqrt(HD)
    cosine, sine_vals = rope_tables(token_order[0])
    rot_query = rotate_heads(
        queries[0].astype(jnp.float32).reshape(row_count, H, HD), cosine, sine_vals, 1.0
    ).astype(jnp.bfloat16)
    rot_keys = rotate_heads(
        key_states[0].astype(jnp.float32).reshape(row_count, H, HD), cosine, sine_vals, 1.0
    ).astype(jnp.bfloat16)
    stacked = jnp.stack([rot_keys.reshape(row_count, feature_width), value_states[0]], axis=1)
    extended = padded(stacked, (("ctx", 0),), row_count)
    ext_blocks = extended.reshape(3 * local_blocks, BLK, 2, H, HD)
    pattern_rows = block_pattern[0]
    first_block = shard_index * local_blocks
    my_pattern = lax.dynamic_slice_in_dim(pattern_rows, first_block, local_blocks, 0)
    slot_valid = my_pattern >= 0
    slot_local = jnp.where(slot_valid, my_pattern - first_block + local_blocks, 0)
    gathered = jnp.take(ext_blocks, slot_local, axis=0)
    key_sets = gathered[:, :, :, 0].reshape(local_blocks, KB * BLK, H, HD)
    value_sets = gathered[:, :, :, 1].reshape(local_blocks, KB * BLK, H, HD)
    key_mask = jnp.repeat(slot_valid, BLK, axis=1)
    query_blocks = rot_query.reshape(local_blocks, BLK, H, HD)
    block_out, log_total = attend_forward(query_blocks, key_sets, value_sets, key_mask, score_scale)
    attn = block_out.reshape(row_count, feature_width)
    grad_rows = out_grad[0]
    forward_weight = lax.all_gather(out_weight, "dp", axis=0, tiled=True)
    layer_out = jnp.dot(attn, forward_weight, preferred_element_type=jnp.float32).astype(
        jnp.bfloat16
    )
    attn_grad = lax.dot_general(
        grad_rows,
        lax.all_gather(out_weight, "dp", axis=0, tiled=True),
        (((1,), (1,)), ((), ())),
        preferred_element_type=jnp.float32,
    ).astype(jnp.bfloat16)
    batch_count = lax.axis_size("dp")
    local_grad = lax.psum_scatter(
        lax.dot_general(
            attn, grad_rows, (((0,), (0,)), ((), ())), preferred_element_type=jnp.float32
        )
        / batch_count,
        "dp",
        scatter_dimension=0,
        tiled=True,
    )
    weight_grad = lax.psum(local_grad, "ctx")
    dot_rows = jnp.sum(
        (attn_grad.astype(jnp.float32) * attn.astype(jnp.float32)).reshape(row_count, H, HD),
        axis=-1,
    )
    grad_dot = dot_rows.reshape(local_blocks, BLK, H).transpose(0, 2, 1)
    grad_blocks = attn_grad.reshape(local_blocks, BLK, H, HD)
    query_part, key_part, value_part = attend_backward(
        query_blocks,
        key_sets,
        value_sets,
        key_mask,
        log_total,
        grad_dot,
        grad_blocks,
        score_scale,
        "nkhd",
    )
    query_grad = (
        rotate_heads(query_part.reshape(row_count, H, HD), cosine, sine_vals, -1.0)
        .reshape(row_count, feature_width)
        .astype(jnp.bfloat16)
    )
    keep = slot_valid.reshape(local_blocks * KB).astype(jnp.float32)[:, None, None, None, None]
    both_parts = (
        jnp.stack(
            [
                key_part.reshape(local_blocks * KB, BLK, H, HD),
                value_part.reshape(local_blocks * KB, BLK, H, HD),
            ],
            axis=2,
        )
        * keep
    )
    accumulated = (
        jnp.zeros((3 * local_blocks, BLK, 2, H, HD), jnp.float32)
        .at[slot_local.reshape(-1)]
        .add(both_parts)
    )
    accumulated = accumulated.reshape(3 * row_count, 2, feature_width)
    own_part = accumulated[row_count : 2 * row_count]
    from_right = from_behind(accumulated[:row_count], "ctx", -1)
    from_left = from_behind(accumulated[2 * row_count :], "ctx", 1)
    summed = own_part + from_right + from_left
    key_total = summed[:, 0]
    value_total = summed[:, 1]
    key_grad = (
        rotate_heads(key_total.reshape(row_count, H, HD), cosine, sine_vals, -1.0)
        .reshape(row_count, feature_width)
        .astype(jnp.bfloat16)
    )
    value_grad = value_total.astype(jnp.bfloat16)
    return (layer_out[None], query_grad[None], key_grad[None], value_grad[None], weight_grad)

def chip_moves(rule):
    pairs = []
    for z, y, x, core in itertools.product(range(4), range(2), range(2), range(2)):
        target = rule(z, y, x, core)
        if target is not None:
            tz, ty, tx, tcore = target
            pairs.append((((z * 2 + y) * 2 + x) * 2 + core, ((tz * 2 + ty) * 2 + tx) * 2 + tcore))
    return pairs


def swap_x(z, y, x, core):
    return (z, y, 1 - x, core)


def swap_y(z, y, x, core):
    return (z, 1 - y, x, core)


def move(array, rule):
    return lax.ppermute(array, ("dp", "ctx"), chip_moves(rule))


def swap_core(array):
    return lax.ppermute(array, "ctx", [(0, 1), (1, 0)])


def gather_first(z, y, x, core):
    return (z ^ 2, y, x, core) if z // 2 == core else (z ^ 1, y, x, 1 - core)


def gather_second(z, y, x, core):
    return (z ^ 3, y, x, core) if z // 2 == core else None


def gather_near(z, y, x, core):
    return swap_y(z, y, x, core) if core == 0 else swap_x(z, y, x, core)


def gather_far(z, y, x, core):
    return swap_x(z, y, x, core) if core == 0 else swap_y(z, y, x, core)


def scatter_first(z, y, x, core):
    return (z ^ 1, y, x, 1 - core) if z // 2 == core else (z ^ 2, y, x, core)


def scatter_second(z, y, x, core):
    return None if z // 2 == core else (z ^ 3, y, x, core)


def dot_nt(a, b):
    return lax.dot_general(a, b, (((1,), (1,)), ((), ())), preferred_element_type=jnp.float32)


def dot_tn(a, b):
    return lax.dot_general(a, b, (((0,), (0,)), ((), ())), preferred_element_type=jnp.float32)


def dot_nn(a, b):
    return jnp.dot(a, b, preferred_element_type=jnp.float32)


def rope_rows(order):
    lane = np.arange(HD)
    entry = lane % (HD // 4)
    axis_of, step = entry // (HD // 16), entry % (HD // 16)
    rotated = lane < HD // 2
    shift = np.array([0, 3, 6, 8], np.int32)[axis_of]
    keep = np.array([7, 7, 3, -1], np.int32)[axis_of]
    per_axis = HD // 16
    frequency = 100.0 ** (-jnp.arange(per_axis, dtype=jnp.float32) / per_axis)
    lane_frequency = jnp.where(rotated, jnp.tile(frequency, HD // per_axis), 0.0)
    coords = jnp.bitwise_and(jnp.right_shift(order[:, None], shift[None, :]), keep[None, :])
    angle = coords.astype(jnp.float32) * lane_frequency[None, :]
    sign = np.where(lane < HD // 4, -1.0, 1.0).astype(np.float32)
    return jnp.cos(angle), jnp.sin(angle) * sign[None, :]


def rotate(x, cos_ref, sin_ref, direction):
    quarter = HD // 4
    lane = lax.broadcasted_iota(jnp.int32, x.shape, 1)
    other = jnp.where(
        lane < quarter, pltpu.roll(x, HD - quarter, 1), pltpu.roll(x, quarter, 1)
    )
    return x * cos_ref[...] + direction * (other * sin_ref[...])


def block_bias(info, row_block, width):
    core = info[0]
    lane_block = lax.broadcasted_iota(jnp.int32, (1, width), 1) // BLK
    bias = jnp.full((1, width), -jnp.inf, jnp.float32)
    query_block = (row_block + 2 * core) % 4
    for key_local in range(4):
        key_block = (key_local + 2 * core) % 4
        listed = jnp.int32(0)
        for slot in range(KB):
            listed = listed + jnp.where(info[4 + query_block * KB + slot] == key_block, 1, 0)
        bias = jnp.where((lane_block == key_local) & (listed > 0), 0.0, bias)
    return bias


def forward_kernel(info, q, k, v, r, cos, sin, rot_q, rot_k, attn, lse):
    head = pl.program_id(0)
    tokens = cos.shape[0]
    half = tokens // 2
    scale = 1.0 / math.sqrt(HD)
    xq = jnp.concatenate([q[...], r[0]], axis=0).astype(jnp.float32)
    rot_q[...] = rotate(xq, cos, sin, 1.0).astype(jnp.bfloat16)
    xk = jnp.concatenate([k[...], r[1]], axis=0).astype(jnp.float32)
    rot_k[...] = rotate(xk, cos, sin, 1.0).astype(jnp.bfloat16)
    keys = rot_k[...]
    values = jnp.concatenate([v[...], r[2]], axis=0)
    lane = lax.broadcasted_iota(jnp.int32, (BLK, HD), 1)
    for b in range(tokens // BLK):
        rows = slice(b * BLK, (b + 1) * BLK)
        scores = dot_nt(rot_q[rows, :], keys) * scale + block_bias(info, b, tokens)
        peak = jnp.max(scores, axis=1, keepdims=True)
        raised = jnp.exp(scores - peak)
        total = jnp.sum(raised, axis=1, keepdims=True)
        probs = (raised * (1.0 / total)).astype(jnp.bfloat16)
        attn[rows, :] = dot_nn(probs, values).astype(jnp.bfloat16)
        log_total = peak + jnp.log(total)
        lse[rows, :] = jnp.where(lane == head, log_total, lse[rows, :])


def weight_grad_kernel(info, attn, own, other, send, keep):
    core, z, y, x = info[0], info[1], info[2], info[3]
    half = own.shape[0]
    part = dot_tn(attn[0:half, :], own[...]) + dot_tn(attn[half:, :], other[...])
    piece = send.shape[2]
    for low in range(2):
        for head_y in range(2):
            for head_x in range(2):
                start = ((low * 2 + head_y) * 2 + head_x) * piece
                rows = part[start : start + piece, :]
                z_rel = low ^ (z & 1)
                first = jnp.where(core == 0, head_x ^ x, head_y ^ y)
                sub = jnp.where(core == 0, head_y ^ y, head_x ^ x)

                @pl.when(first == 1)
                def _():
                    send[sub, z_rel] = rows.astype(send.dtype)

                @pl.when(first == 0)
                def _():
                    keep[sub, z_rel] = rows


def projection_kernel(info, attn, own, other, near, far, out_own, out_send, grad, weight):
    core, z, y, x = info[0], info[1], info[2], info[3]
    piece = near.shape[2]
    for e3, ref in enumerate((near, far)):
        for e2 in range(2):
            y_at = jnp.where(core == 0, y ^ e2, y ^ e3)
            x_at = jnp.where(core == 0, x ^ e3, x ^ e2)
            for low in range(2):
                start = pl.multiple_of(((low * 2 + y_at) * 2 + x_at) * piece, piece)
                weight[pl.ds(start, piece), :] = ref[e2, low]
    half = own.shape[0]
    out_send[...] = dot_nn(attn[half:, :], weight[...]).astype(out_send.dtype)
    out_own[...] = dot_nn(attn[0:half, :], weight[...])
    grad[0:half, :] = dot_nt(own[...], weight[...]).astype(grad.dtype)
    grad[half:, :] = dot_nt(other[...], weight[...]).astype(grad.dtype)


def backward_kernel(
    info, rot_q, rot_k, v, r, attn, grad, lse, cos, sin, own, send, key_sum, value_sum, query_sum
):
    head = pl.program_id(0)
    tokens = cos.shape[0]
    half = tokens // 2
    scale = 1.0 / math.sqrt(HD)
    keys = rot_k[...]
    values = jnp.concatenate([v[...], r[0]], axis=0)
    lane = lax.broadcasted_iota(jnp.int32, (BLK, HD), 1)
    for b in range(tokens // BLK):
        rows = slice(b * BLK, (b + 1) * BLK)
        queries = rot_q[rows, :]
        grads = grad[rows, :]
        log_total = jnp.sum(jnp.where(lane == head, lse[rows, :], 0.0), axis=1, keepdims=True)
        dots = jnp.sum(
            grads.astype(jnp.float32) * attn[rows, :].astype(jnp.float32), axis=1, keepdims=True
        )
        scores = dot_nt(queries, keys) * scale + block_bias(info, b, tokens)
        exact = jnp.exp(scores - log_total)
        prob_grad = dot_nt(grads, values)
        score_grad = (exact * (prob_grad - dots) * scale).astype(jnp.bfloat16)
        value_part = dot_tn(exact.astype(jnp.bfloat16), grads)
        key_part = dot_tn(score_grad, queries)
        query_sum[rows, :] = dot_nn(score_grad, keys)
        if b == 0:
            key_sum[...] = key_part
            value_sum[...] = value_part
        else:
            key_sum[...] += key_part
            value_sum[...] += value_part
    outs = (
        rotate(query_sum[...], cos, sin, -1.0),
        rotate(key_sum[...], cos, sin, -1.0),
        value_sum[...],
    )
    for i, out in enumerate(outs):
        out = out.astype(jnp.bfloat16)
        own[i] = out[0:half, :]
        send[i] = out[half:, :]


def chip_shards(queries, key_states, value_states, token_order, block_pattern, out_weight, out_grad):
    rows, width = queries.shape[1:]
    model = out_grad.shape[2]
    tokens, mine = 2 * rows, width // 2
    heads = mine // HD
    owned = out_weight.shape[0]
    core = lax.axis_index("ctx")
    dp = lax.axis_index("dp")
    z, y, x = dp // 4, dp // 2 % 2, dp % 2
    at_home = z // 2 == core
    odd = z % 2 == 1
    params = pltpu.CompilerParams(vmem_limit_bytes=56 * 1024 * 1024)
    bf16 = jnp.bfloat16

    first = move(out_weight, gather_first)
    second = move(out_weight, gather_second)

    order_other = swap_core(token_order[0])
    start_other = (1 - core) * mine
    pack = jnp.stack(
        [
            lax.dynamic_slice_in_dim(a[0], start_other, mine, axis=1)
            for a in (queries, key_states, value_states)
        ]
    )
    received = swap_core(pack)
    dy_own = out_grad[0]
    dy_other = swap_core(dy_own)

    order = jnp.concatenate([token_order[0], order_other])
    cos, sin = rope_rows(order)
    info = jnp.concatenate([jnp.stack([core, z, y, x]), block_pattern[0].reshape(-1)]).astype(
        jnp.int32
    )

    def whole(*shape):
        return pl.BlockSpec(shape, lambda *_: (0,) * len(shape))

    own_head = pl.BlockSpec((None, rows, HD), lambda h, info: (0, 0, info[0] * heads + h))
    by_head = pl.BlockSpec((tokens, HD), lambda h, info: (0, h))
    rot_q, rot_k, attn, lse = pl.pallas_call(
        forward_kernel,
        grid_spec=pltpu.PrefetchScalarGridSpec(
            num_scalar_prefetch=1,
            grid=(heads,),
            in_specs=[
                own_head,
                own_head,
                own_head,
                pl.BlockSpec((3, rows, HD), lambda h, info: (0, 0, h)),
                whole(tokens, HD),
                whole(tokens, HD),
            ],
            out_specs=[by_head, by_head, by_head, whole(tokens, HD)],
        ),
        out_shape=[jax.ShapeDtypeStruct((tokens, mine), bf16)] * 3
        + [jax.ShapeDtypeStruct((tokens, HD), jnp.float32)],
        compiler_params=params,
        name="forward",
    )(info, queries, key_states, value_states, received, cos, sin)

    piece = (2, 2, owned, model)
    send, keep = pl.pallas_call(
        weight_grad_kernel,
        grid_spec=pltpu.PrefetchScalarGridSpec(
            num_scalar_prefetch=1,
            grid=(1,),
            in_specs=[whole(tokens, mine), whole(rows, model), whole(rows, model)],
            out_specs=[whole(*piece), whole(*piece)],
        ),
        out_shape=[
            jax.ShapeDtypeStruct(piece, bf16),
            jax.ShapeDtypeStruct(piece, jnp.float32),
        ],
        compiler_params=params,
        name="weight_grad",
    )(info, attn, dy_own, dy_other)
    got = move(send, gather_far).astype(jnp.float32)
    second_send = (keep[1] + got[1]).astype(bf16)
    kept = keep[0] + got[0]
    kept = kept + move(second_send, gather_near).astype(jnp.float32)
    to_first = jnp.where(at_home, kept[1], kept[0]).astype(bf16)
    to_second = kept[1].astype(bf16)
    from_first = move(to_first, scatter_first).astype(jnp.float32)
    from_second = move(to_second, scatter_second).astype(jnp.float32)
    share = jnp.where(at_home, kept[0] + from_first + from_second, from_first)
    weight_grad = (share + swap_core(share)) * (1.0 / lax.axis_size("dp"))

    a = jnp.where(at_home, out_weight, first)
    b = jnp.where(at_home, first, second)
    near = jnp.where(odd, jnp.stack([b, a]), jnp.stack([a, b]))
    near = jnp.stack([near, move(near, gather_near)])
    far = move(near, gather_far)

    out_own, out_send, grad = pl.pallas_call(
        projection_kernel,
        grid_spec=pltpu.PrefetchScalarGridSpec(
            num_scalar_prefetch=1,
            grid=(1,),
            in_specs=[
                whole(tokens, mine),
                whole(rows, model),
                whole(rows, model),
                whole(*piece),
                whole(*piece),
            ],
            out_specs=[whole(rows, model), whole(rows, model), whole(tokens, mine)],
            scratch_shapes=[pltpu.VMEM((mine, model), bf16)],
        ),
        out_shape=[
            jax.ShapeDtypeStruct((rows, model), jnp.float32),
            jax.ShapeDtypeStruct((rows, model), bf16),
            jax.ShapeDtypeStruct((tokens, mine), bf16),
        ],
        compiler_params=params,
        name="projection",
    )(info, attn, dy_own, dy_other, near, far)
    layer_out = (out_own + swap_core(out_send).astype(jnp.float32)).astype(bf16)

    grads_own, grads_send = pl.pallas_call(
        backward_kernel,
        grid_spec=pltpu.PrefetchScalarGridSpec(
            num_scalar_prefetch=1,
            grid=(heads,),
            in_specs=[
                by_head,
                by_head,
                own_head,
                pl.BlockSpec((1, rows, HD), lambda h, info: (2, 0, h)),
                by_head,
                by_head,
                whole(tokens, HD),
                whole(tokens, HD),
                whole(tokens, HD),
            ],
            out_specs=[pl.BlockSpec((3, rows, HD), lambda h, info: (0, 0, h))] * 2,
            scratch_shapes=[pltpu.VMEM((tokens, HD), jnp.float32)] * 3,
        ),
        out_shape=[jax.ShapeDtypeStruct((3, rows, mine), bf16)] * 2,
        compiler_params=params,
        name="backward",
    )(info, rot_q, rot_k, value_states, received, attn, grad, lse, cos, sin)
    grads_other = swap_core(grads_send)
    on_left = core == 0
    outs = [
        jnp.concatenate(
            [
                jnp.where(on_left, grads_own[i], grads_other[i]),
                jnp.where(on_left, grads_other[i], grads_own[i]),
            ],
            axis=1,
        )[None]
        for i in range(3)
    ]
    return (layer_out[None], *outs, weight_grad)


def solution(mesh):
    in_specs = (
        P("dp", "ctx", None),
        P("dp", "ctx", None),
        P("dp", "ctx", None),
        P("dp", "ctx"),
        P("dp", None, None),
        P("dp", None),
        P("dp", "ctx", None),
    )
    out_specs = (
        P("dp", "ctx", None),
        P("dp", "ctx", None),
        P("dp", "ctx", None),
        P("dp", "ctx", None),
        P("dp", None),
    )
    body = chip_shards if (mesh.shape["dp"], mesh.shape["ctx"]) == (16, 2) else shards
    return jax.shard_map(body, mesh=mesh, in_specs=in_specs, out_specs=out_specs, check_vma=False)
```

```python
import functools
import itertools
import math

import jax
import jax.numpy as jnp
import numpy as np
from jax import lax
from jax.experimental import pallas as pl
from jax.experimental.pallas import tpu as pltpu
from jax.sharding import PartitionSpec as P

H = 8
HD = 128
BLK = 128
KB = 4
SUM_CHUNKS = 2


def padded(shard, sides, width):
    for axis, dim in sides:
        devices, length = (lax.axis_size(axis), shard.shape[dim])
        up = [(i, (i + 1) % devices) for i in range(devices - 1)]
        down = [(j, i) for i, j in up]
        last = lax.slice_in_dim(shard, length - width, length, axis=dim)
        leading = lax.slice_in_dim(shard, 0, width, axis=dim)
        before = lax.ppermute(last, axis, up)
        after = lax.ppermute(leading, axis, down)
        shard = jnp.concatenate([before, shard, after], axis=dim)
    return shard


def from_behind(block, axis, distance):
    devices = range(lax.axis_size(axis))
    route = [(i - distance, i) for i in devices if i - distance in devices]
    return lax.ppermute(block, axis, route)


def rope_tables(positions):
    coords = jnp.stack(
        [positions % 8, positions // 8 % 8, positions // 64 % 4, positions // 256], axis=1
    ).astype(jnp.float32)
    per_axis = HD // 16
    frequency = 100.0 ** (-jnp.arange(per_axis, dtype=jnp.float32) / per_axis)
    angle = (coords[:, :, None] * frequency[None, None, :]).reshape(
        positions.shape[0], 4 * per_axis
    )
    return (jnp.cos(angle), jnp.sin(angle))


def rotate_heads(heads, cosine, sine_vals, direction):
    quarter = HD // 4
    first_part = heads[..., :quarter]
    second_part = heads[..., quarter : 2 * quarter]
    cos_rows = cosine[:, None, :]
    sin_rows = direction * sine_vals[:, None, :]
    return jnp.concatenate(
        [
            first_part * cos_rows - second_part * sin_rows,
            second_part * cos_rows + first_part * sin_rows,
            heads[..., 2 * quarter :],
        ],
        axis=-1,
    )


def attend_forward(query_blocks, key_sets, value_sets, key_mask, score_scale):
    scores = (
        jnp.einsum("nqhd,nkhd->nhqk", query_blocks, key_sets, preferred_element_type=jnp.float32)
        * score_scale
    )
    scores = jnp.where(key_mask[:, None, None, :], scores, -jnp.inf)
    row_peak = jnp.max(scores, axis=-1)
    row_total = jnp.sum(jnp.exp(scores - row_peak[..., None]), axis=-1)
    log_total = row_peak + jnp.log(row_total)
    soft_probs = jnp.exp(scores - log_total[..., None]).astype(jnp.bfloat16)
    block_out = jnp.einsum(
        "nhqk,nkhd->nqhd", soft_probs, value_sets, preferred_element_type=jnp.float32
    ).astype(jnp.bfloat16)
    return (block_out, log_total)


def attend_backward(
    query_blocks,
    key_sets,
    value_sets,
    key_mask,
    log_total,
    grad_dot,
    grad_blocks,
    score_scale,
    key_form,
):
    scores = (
        jnp.einsum(
            "nqhd," + key_form + "->nhqk",
            query_blocks,
            key_sets,
            preferred_element_type=jnp.float32,
        )
        * score_scale
    )
    scores = jnp.where(key_mask[:, None, None, :], scores, -jnp.inf)
    exact_probs = jnp.exp(scores - log_total[..., None])
    soft_probs = exact_probs.astype(jnp.bfloat16)
    value_part = jnp.einsum(
        "nhqk,nqhd->" + key_form, soft_probs, grad_blocks, preferred_element_type=jnp.float32
    )
    prob_grad = jnp.einsum(
        "nqhd," + key_form + "->nhqk", grad_blocks, value_sets, preferred_element_type=jnp.float32
    )
    score_grad = (exact_probs * (prob_grad - grad_dot[..., None]) * score_scale).astype(
        jnp.bfloat16
    )
    query_part = jnp.einsum(
        "nhqk," + key_form + "->nqhd", score_grad, key_sets, preferred_element_type=jnp.float32
    )
    key_part = jnp.einsum(
        "nhqk,nqhd->" + key_form, score_grad, query_blocks, preferred_element_type=jnp.float32
    )
    return (query_part, key_part, value_part)


def shards(queries, key_states, value_states, token_order, block_pattern, out_weight, out_grad):
    row_count = queries.shape[1]
    feature_width = queries.shape[2]
    local_blocks = row_count // BLK
    shard_index = lax.axis_index("ctx")
    score_scale = 1.0 / math.sqrt(HD)
    cosine, sine_vals = rope_tables(token_order[0])
    rot_query = rotate_heads(
        queries[0].astype(jnp.float32).reshape(row_count, H, HD), cosine, sine_vals, 1.0
    ).astype(jnp.bfloat16)
    rot_keys = rotate_heads(
        key_states[0].astype(jnp.float32).reshape(row_count, H, HD), cosine, sine_vals, 1.0
    ).astype(jnp.bfloat16)
    stacked = jnp.stack([rot_keys.reshape(row_count, feature_width), value_states[0]], axis=1)
    extended = padded(stacked, (("ctx", 0),), row_count)
    ext_blocks = extended.reshape(3 * local_blocks, BLK, 2, H, HD)
    pattern_rows = block_pattern[0]
    first_block = shard_index * local_blocks
    my_pattern = lax.dynamic_slice_in_dim(pattern_rows, first_block, local_blocks, 0)
    slot_valid = my_pattern >= 0
    slot_local = jnp.where(slot_valid, my_pattern - first_block + local_blocks, 0)
    gathered = jnp.take(ext_blocks, slot_local, axis=0)
    key_sets = gathered[:, :, :, 0].reshape(local_blocks, KB * BLK, H, HD)
    value_sets = gathered[:, :, :, 1].reshape(local_blocks, KB * BLK, H, HD)
    key_mask = jnp.repeat(slot_valid, BLK, axis=1)
    query_blocks = rot_query.reshape(local_blocks, BLK, H, HD)
    block_out, log_total = attend_forward(query_blocks, key_sets, value_sets, key_mask, score_scale)
    attn = block_out.reshape(row_count, feature_width)
    grad_rows = out_grad[0]
    forward_weight = lax.all_gather(out_weight, "dp", axis=0, tiled=True)
    layer_out = jnp.dot(attn, forward_weight, preferred_element_type=jnp.float32).astype(
        jnp.bfloat16
    )
    attn_grad = lax.dot_general(
        grad_rows,
        lax.all_gather(out_weight, "dp", axis=0, tiled=True),
        (((1,), (1,)), ((), ())),
        preferred_element_type=jnp.float32,
    ).astype(jnp.bfloat16)
    batch_count = lax.axis_size("dp")
    local_grad = lax.psum_scatter(
        lax.dot_general(
            attn, grad_rows, (((0,), (0,)), ((), ())), preferred_element_type=jnp.float32
        )
        / batch_count,
        "dp",
        scatter_dimension=0,
        tiled=True,
    )
    weight_grad = lax.psum(local_grad, "ctx")
    dot_rows = jnp.sum(
        (attn_grad.astype(jnp.float32) * attn.astype(jnp.float32)).reshape(row_count, H, HD),
        axis=-1,
    )
    grad_dot = dot_rows.reshape(local_blocks, BLK, H).transpose(0, 2, 1)
    grad_blocks = attn_grad.reshape(local_blocks, BLK, H, HD)
    query_part, key_part, value_part = attend_backward(
        query_blocks,
        key_sets,
        value_sets,
        key_mask,
        log_total,
        grad_dot,
        grad_blocks,
        score_scale,
        "nkhd",
    )
    query_grad = (
        rotate_heads(query_part.reshape(row_count, H, HD), cosine, sine_vals, -1.0)
        .reshape(row_count, feature_width)
        .astype(jnp.bfloat16)
    )
    keep = slot_valid.reshape(local_blocks * KB).astype(jnp.float32)[:, None, None, None, None]
    both_parts = (
        jnp.stack(
            [
                key_part.reshape(local_blocks * KB, BLK, H, HD),
                value_part.reshape(local_blocks * KB, BLK, H, HD),
            ],
            axis=2,
        )
        * keep
    )
    accumulated = (
        jnp.zeros((3 * local_blocks, BLK, 2, H, HD), jnp.float32)
        .at[slot_local.reshape(-1)]
        .add(both_parts)
    )
    accumulated = accumulated.reshape(3 * row_count, 2, feature_width)
    own_part = accumulated[row_count : 2 * row_count]
    from_right = from_behind(accumulated[:row_count], "ctx", -1)
    from_left = from_behind(accumulated[2 * row_count :], "ctx", 1)
    summed = own_part + from_right + from_left
    key_total = summed[:, 0]
    value_total = summed[:, 1]
    key_grad = (
        rotate_heads(key_total.reshape(row_count, H, HD), cosine, sine_vals, -1.0)
        .reshape(row_count, feature_width)
        .astype(jnp.bfloat16)
    )
    value_grad = value_total.astype(jnp.bfloat16)
    return (layer_out[None], query_grad[None], key_grad[None], value_grad[None], weight_grad)

def chip_moves(rule):
    pairs = []
    for z, y, x, core in itertools.product(range(4), range(2), range(2), range(2)):
        target = rule(z, y, x, core)
        if target is not None:
            tz, ty, tx, tcore = target
            pairs.append((((z * 2 + y) * 2 + x) * 2 + core, ((tz * 2 + ty) * 2 + tx) * 2 + tcore))
    return pairs


def swap_x(z, y, x, core):
    return (z, y, 1 - x, core)


def swap_y(z, y, x, core):
    return (z, 1 - y, x, core)


def move(array, rule):
    return lax.ppermute(array, ("dp", "ctx"), chip_moves(rule))


def swap_core(array):
    return lax.ppermute(array, "ctx", [(0, 1), (1, 0)])


def gather_first(z, y, x, core):
    return (z ^ 2, y, x, core) if z // 2 == core else (z ^ 1, y, x, 1 - core)


def gather_second(z, y, x, core):
    return (z ^ 3, y, x, core) if z // 2 == core else None


def gather_near(z, y, x, core):
    return swap_y(z, y, x, core) if core == 0 else swap_x(z, y, x, core)


def gather_far(z, y, x, core):
    return swap_x(z, y, x, core) if core == 0 else swap_y(z, y, x, core)


def scatter_first(z, y, x, core):
    return (z ^ 1, y, x, 1 - core) if z // 2 == core else (z ^ 2, y, x, core)


def scatter_second(z, y, x, core):
    return None if z // 2 == core else (z ^ 3, y, x, core)


def dot_nt(a, b):
    return lax.dot_general(a, b, (((1,), (1,)), ((), ())), preferred_element_type=jnp.float32)


def dot_nn(a, b):
    return jnp.dot(a, b, preferred_element_type=jnp.float32)


def rope_table(order):
    per_axis = HD // 16
    shape = (4 * per_axis, order.shape[1])
    row = lax.broadcasted_iota(jnp.int32, shape, 0)
    axis_of, step = row // per_axis, row % per_axis
    coords = jnp.where(
        axis_of == 0,
        order % 8,
        jnp.where(axis_of == 1, order // 8 % 8, jnp.where(axis_of == 2, order // 64 % 4, order // 256)),
    )
    frequency = jnp.zeros(shape, jnp.float32)
    for i in range(per_axis):
        frequency = jnp.where(step == i, jnp.float32(100.0 ** (-i / per_axis)), frequency)
    angle = coords.astype(jnp.float32) * frequency
    return jnp.cos(angle), jnp.sin(angle)


def rotate_rows(x, cos, sin):
    quarter = HD // 4
    f, g, rest = x[0:quarter], x[quarter : 2 * quarter], x[2 * quarter :]
    return jnp.concatenate([f * cos - g * sin, g * cos + f * sin, rest], axis=0).astype(jnp.bfloat16)


def place():
    dp = lax.axis_index("dp")
    return lax.axis_index("ctx"), dp // 4, dp // 2 % 2, dp % 2


def block_bias(pattern, core, bias):
    blocks = bias.shape[0]
    lane_block = lax.broadcasted_iota(jnp.int32, (1, bias.shape[1]), 1) // BLK
    for key_local in range(blocks):
        key_block = (key_local + 2 * core) % blocks
        row = jnp.full(lane_block.shape, -jnp.inf, jnp.float32)
        for query_local in range(blocks):
            query_block = (query_local + 2 * core) % blocks
            listed = jnp.int32(0)
            for slot in range(KB):
                listed = listed + jnp.where(pattern[0, query_block, slot] == key_block, 1, 0)
            row = jnp.where((lane_block == query_local) & (listed > 0), 0.0, row)
        bias[key_local : key_local + 1, :] = row


def scaled_scores(keys, queries_t, bias):
    scores = dot_nn(keys, queries_t) * (math.log2(math.e) / math.sqrt(HD))
    parts = [scores[b * BLK : (b + 1) * BLK, :] + bias[b : b + 1, :] for b in range(bias.shape[0])]
    return jnp.concatenate(parts, axis=0)


def pack_kernel(*refs):
    inputs, out, sems = refs[:3], refs[-2], refs[-1]
    mine = out.shape[2]
    there = pl.ds(pl.multiple_of((1 - place()[0]) * mine, mine), mine)
    copies = [pltpu.make_async_copy(a.at[:, there], out.at[i], sems.at[i]) for i, a in enumerate(inputs)]
    for copy in copies:
        copy.start()
    for copy in copies:
        copy.wait()


def forward_kernel(pattern, near, far, received, *refs):
    inputs = refs[:3]
    rot_q, rot_k, rot_kt, values, attn, attn_t, lse, bias, cos_ref, sin_ref, q, k, v, sems = refs[-14:]
    rows, mine = inputs[0].shape[0], rot_q.shape[0]
    tokens = 2 * rows
    step = 2 * BLK
    core = place()[0]
    here = pl.ds(pl.multiple_of(core * mine, mine), mine)
    copies = []
    for i, (ref, target) in enumerate(zip(inputs, (q, k, v))):
        copies.append(pltpu.make_async_copy(ref.at[:, here], target, sems.at[i]))
        copies[-1].start()
    block_bias(pattern, core, bias)
    cos, sin = rope_table(jnp.concatenate([near[...], far[...]], axis=1))
    cos_ref[...] = cos
    sin_ref[...] = sin
    for copy in copies:
        copy.wait()
    for head in range(mine // HD):
        cols = slice(head * HD, (head + 1) * HD)
        query, key, value = (
            jnp.concatenate([a[:, cols], received[i, :, cols]], axis=0) for i, a in enumerate((q, k, v))
        )
        rot_q[cols, :] = rotate_rows(query.T.astype(jnp.float32), cos, sin)
        keys_t = rotate_rows(key.T.astype(jnp.float32), cos, sin)
        rot_kt[cols, :] = keys_t
        keys = keys_t.T
        rot_k[:, cols] = keys
        values[:, cols] = value
        value_t = value.T
        for part in range(tokens // step):
            at = slice(part * step, (part + 1) * step)
            scores = scaled_scores(keys, rot_q[cols, at], bias[:, at])
            peak = jnp.max(scores, axis=0, keepdims=True)
            raised = jnp.exp2(scores - peak)
            total = jnp.sum(raised, axis=0, keepdims=True)
            mixed = dot_nn(value_t, raised.astype(jnp.bfloat16)) * (1.0 / total)
            mixed = mixed.astype(jnp.bfloat16)
            attn_t[cols, at] = mixed
            attn[at, cols] = mixed.T
            lse[head : head + 1, at] = peak + jnp.log2(total)


def weight_grad_kernel(attn_t, own, other, *refs, chunk):
    send, keep = refs[-2:]
    core, z, y, x = place()
    piece, width = send.shape[2:]
    cols = slice(chunk * width, (chunk + 1) * width)
    tokens = jnp.concatenate([own[:, cols], other[:, cols]], axis=0)
    for block in range(attn_t.shape[0] // (2 * piece)):
        rows = slice(block * 2 * piece, (block + 1) * 2 * piece)
        part = dot_nn(attn_t[rows, :], tokens).astype(send.dtype)
        z_rel = (block // 2) ^ (z & 1)
        for head_x in range(2):
            out = part[head_x * piece : (head_x + 1) * piece, :]
            first = jnp.where(core == 0, head_x ^ x, (block % 2) ^ y)
            sub = jnp.where(core == 0, (block % 2) ^ y, head_x ^ x)

            @pl.when(first == 1)
            def _():
                send[sub, z_rel] = out

            @pl.when(first == 0)
            def _():
                keep[sub, z_rel] = out


def attn_grad_kernel(attn_t, own, other, *refs):
    grad_t, dots, weight = refs[-3:]
    core, z, y, x = place()
    piece = refs[0].shape[1]
    for chunk in range(2):
        for e3 in range(2):
            ref = refs[chunk * 2 + e3]
            for e2 in range(2):
                y_at = jnp.where(core == 0, y ^ e2, y ^ e3)
                x_at = jnp.where(core == 0, x ^ e3, x ^ e2)
                start = (((z % 2 ^ chunk) * 2 + y_at) * 2 + x_at) * piece
                weight[pl.ds(pl.multiple_of(start, piece), piece), :] = ref[e2]
    half = own.shape[0]
    mine = weight.shape[0]
    for t, ref in enumerate((own, other)):
        cols = slice(t * half, (t + 1) * half)
        rounded = dot_nt(weight[...], ref[...]).astype(grad_t.dtype)
        grad_t[:, cols] = rounded
        product = rounded.astype(jnp.float32) * attn_t[:, cols].astype(jnp.float32)
        for head in range(mine // HD):
            dots[head : head + 1, cols] = jnp.sum(
                product[head * HD : (head + 1) * HD], axis=0, keepdims=True
            )


def projection_kernel(attn, weight, *refs):
    out_send, out_own = refs[-2:]
    half = out_own.shape[0]
    for c in range(weight.shape[1] // half):
        cols = slice(c * half, (c + 1) * half)
        part = dot_nn(attn[...], weight[:, cols])
        out_send[:, cols] = part[half:].astype(out_send.dtype)
        out_own[:, cols] = part[:half]


def backward_kernel(rot_q, rot_k, rot_kt, values, grad_t, dots, lse, bias, cos_ref, sin_ref, *refs, heads):
    send, own = refs[-2:]
    tokens = rot_k.shape[0]
    half = tokens // 2
    step = 2 * BLK
    scale = 1.0 / math.sqrt(HD)
    cos, sin = cos_ref[...], -sin_ref[...]
    for at_head, head in enumerate(heads):
        cols = slice(head * HD, (head + 1) * HD)
        out_cols = slice(at_head * HD, (at_head + 1) * HD)
        keys, keys_t, value = rot_k[:, cols], rot_kt[cols, :], values[:, cols]
        key_sum = jnp.zeros((HD, tokens), jnp.float32)
        value_sum = jnp.zeros((HD, tokens), jnp.float32)
        query_parts = []
        for part in range(tokens // step):
            at = slice(part * step, (part + 1) * step)
            queries_t, grads_t = rot_q[cols, at], grad_t[cols, at]
            scores = scaled_scores(keys, queries_t, bias[:, at])
            exact = jnp.exp2(scores - lse[head : head + 1, at])
            prob_grad = dot_nn(value, grads_t)
            score_grad = (exact * (prob_grad - dots[head : head + 1, at])).astype(jnp.bfloat16)
            value_sum = value_sum + dot_nt(grads_t, exact.astype(jnp.bfloat16))
            key_sum = key_sum + dot_nt(queries_t, score_grad)
            query_parts.append(dot_nn(keys_t, score_grad))
        query_sum = jnp.concatenate(query_parts, axis=1)
        outs = (
            rotate_rows(query_sum * scale, cos, sin),
            rotate_rows(key_sum * scale, cos, sin),
            value_sum.astype(jnp.bfloat16),
        )
        for i, out in enumerate(outs):
            out = out.T
            own[i, :, out_cols] = out[0:half, :]
            send[i, :, out_cols] = out[half:, :]


def gather_pick_kernel(home, away, *refs):
    core, z, _, _ = place()
    near = refs[-1]

    @pl.when(z // 2 == core)
    def _():
        near[...] = home[...]

    @pl.when(z // 2 != core)
    def _():
        near[...] = away[...]


def pair_kernel(a, b, *refs):
    refs[-1][0] = a[...]
    refs[-1][1] = b[...]


def second_sum_kernel(keep, got, *refs):
    send, kept = refs[-2:]
    send[...] = (keep[1].astype(jnp.float32) + got[1].astype(jnp.float32)).astype(send.dtype)
    kept[...] = keep[0].astype(jnp.float32) + got[0].astype(jnp.float32)


def z_sum_kernel(kept, got, *refs):
    to_first, to_second, own = refs[-3:]
    core, z, _, _ = place()
    at_home = z // 2 == core
    near = kept[0] + got[0].astype(jnp.float32)
    rest = kept[1] + got[1].astype(jnp.float32)
    own[...] = near
    to_first[...] = jnp.where(at_home, rest, near).astype(to_first.dtype)
    to_second[...] = rest.astype(to_second.dtype)


def share_kernel(own, first, second, *refs):
    core, z, _, _ = place()
    at_home = z // 2 == core
    total = own[...] + first[...].astype(jnp.float32) + second[...].astype(jnp.float32)
    refs[-1][...] = jnp.where(at_home, total, first[...].astype(jnp.float32))


def mean_kernel(*refs, count):
    out = refs[-1]
    width = refs[0].shape[1]
    for i in range(out.shape[1] // width):
        out[:, i * width : (i + 1) * width] = (refs[2 * i][...] + refs[2 * i + 1][...]) * (1.0 / count)


def layer_out_kernel(own, got, *refs):
    out = refs[-1]
    out[...] = (own[...] + got[...].astype(jnp.float32)).astype(out.dtype)


def grads_kernel(*refs):
    outs, parts = refs[-3:], refs[:-3]
    mine = outs[0].shape[1] // 2
    width = parts[0].shape[2]
    for p in range(mine // width):
        for source in range(2):
            start = (place()[0] ^ source) * mine + p * width
            cols = pl.ds(pl.multiple_of(start, HD), width)
            for i in range(3):
                outs[i][:, cols] = parts[2 * p + source][i]


def chip_shards(queries, key_states, value_states, token_order, block_pattern, out_weight, out_grad):
    rows, width = queries.shape[1:]
    model = out_grad.shape[2]
    tokens, mine = 2 * rows, width // 2
    owned = out_weight.shape[0]
    bf16, f32 = jnp.bfloat16, jnp.float32
    in_vmem = pl.BlockSpec(memory_space=pltpu.VMEM)
    in_smem = pl.BlockSpec(memory_space=pltpu.SMEM)
    in_hbm = pl.BlockSpec(memory_space=pltpu.HBM)
    anywhere = pl.BlockSpec(memory_space=pl.ANY)
    done = []

    def call(kernel, name, args, outs, scratch=(), limit=8, specs=None, final=False):
        before = [a for a in done if not any(a is b for b in args)]
        results = pl.pallas_call(
            kernel,
            in_specs=list(specs or [in_vmem] * len(args)) + [anywhere] * len(before),
            out_specs=[in_vmem] * len(outs),
            out_shape=[jax.ShapeDtypeStruct(s, d) for s, d in outs],
            scratch_shapes=scratch,
            compiler_params=pltpu.CompilerParams(vmem_limit_bytes=limit << 20),
            cost_estimate=pl.CostEstimate(flops=1, bytes_accessed=1, transcendentals=0),
            name=name,
        )(*args, *before)
        if not final:
            done[:] = results[:1]
        return results

    q_own, k_own, v_own, dy_own = queries[0], key_states[0], value_states[0], out_grad[0]
    q_in, k_in, v_in = (pltpu.with_memory_space_constraint(a, pltpu.HBM) for a in (q_own, k_own, v_own))
    (pack,) = call(
        pack_kernel,
        "pack",
        (q_in, k_in, v_in),
        [((3, rows, mine), bf16)],
        specs=[in_hbm] * 3,
        scratch=[pltpu.SemaphoreType.DMA((3,))],
        final=True,
    )
    received = swap_core(pack)
    order_far = swap_core(token_order)
    dy_far = swap_core(dy_own)

    first, second = move(out_weight, gather_first), move(out_weight, gather_second)
    z_parts = ((out_weight, first), (first, second))
    chunks = 2

    rot_q, rot_k, rot_kt, values, attn, attn_t, lse, bias, cos, sin = call(
        forward_kernel,
        "forward",
        (block_pattern, token_order, order_far, received, q_in, k_in, v_in),
        [((mine, tokens), bf16), ((tokens, mine), bf16), ((mine, tokens), bf16)]
        + [((tokens, mine), bf16)] * 2
        + [((mine, tokens), bf16), ((mine // HD, tokens), f32), ((tokens // BLK, tokens), f32)]
        + [((HD // 4, tokens), f32)] * 2,
        scratch=[pltpu.VMEM((rows, mine), bf16)] * 3 + [pltpu.SemaphoreType.DMA((3,))],
        limit=24,
        specs=[in_smem] + [in_vmem] * 3 + [in_hbm] * 3,
    )
    sums = SUM_CHUNKS
    cols = model // sums
    near, joined, far = [None] * chunks, [None] * chunks, [None] * chunks
    weights = [None] * (2 * chunks)
    parts, z_sums, pairs, shares = [None] * sums, [None] * sums, [], []
    result = {}

    def weight_grad(i):
        send, keep = call(
            functools.partial(weight_grad_kernel, chunk=i),
            "weight_grad",
            (attn_t, dy_own, dy_far),
            [((2, 2, owned, cols), bf16)] * 2,
            limit=16,
        )
        parts[i] = (keep, move(send, gather_far))

    def gather_near_step(i):
        (near[i],) = call(gather_pick_kernel, "gather_pick", z_parts[i], [((owned, model), bf16)])
        joined[i] = move(near[i], gather_near)

    def gather_far_step(i):
        (pair,) = call(pair_kernel, "pair", (near[i], joined[i]), [((2, owned, model), bf16)])
        weights[2 * i], weights[2 * i + 1] = pair, move(pair, gather_far)

    def second_sum(i):
        send, kept = call(
            second_sum_kernel,
            "second_sum",
            parts[i],
            [((2, owned, cols), bf16), ((2, owned, cols), f32)],
        )
        parts[i] = (kept, move(send, gather_near))

    def z_sum(i):
        to_first, to_second, own = call(
            z_sum_kernel,
            "z_sum",
            parts[i],
            [((owned, cols), bf16)] * 2 + [((owned, cols), f32)],
        )
        z_sums[i] = own, move(to_first, scatter_first), move(to_second, scatter_second)

    def share(i):
        (part,) = call(share_kernel, "share", z_sums[i], [((owned, cols), f32)])
        shares.extend([part, swap_core(part)])

    def attn_grad():
        result["grad"] = call(
            attn_grad_kernel,
            "attn_grad",
            (attn_t, dy_own, dy_far, *weights),
            [((mine, tokens), bf16), ((mine // HD, tokens), f32), ((mine, model), bf16)],
            limit=24,
        )

    def projection():
        out_send, out_own = call(
            projection_kernel,
            "projection",
            (attn, result["grad"][2]),
            [((rows, model), bf16), ((rows, model), f32)],
            limit=16,
        )
        result["out"] = (out_own, swap_core(out_send))

    def backward(heads):
        send, own = call(
            functools.partial(backward_kernel, heads=heads),
            "backward",
            (rot_q, rot_k, rot_kt, values, *result["grad"][:2], lse, bias, cos, sin),
            [((3, rows, len(heads) * HD), bf16)] * 2,
            limit=24,
        )
        pairs.extend([own, swap_core(send)])

    def layer_out():
        (result["layer_out"],) = call(layer_out_kernel, "layer_out", result["out"], [((rows, model), bf16)], final=True)

    def grads():
        result["grads"] = call(grads_kernel, "grads", pairs, [((rows, width), bf16)] * 3, final=True)

    def mean():
        (result["weight_grad"],) = call(
            functools.partial(mean_kernel, count=lax.axis_size("dp")), "mean", shares, [((owned, model), f32)], final=True
        )

    weight_grad(0)
    gather_near_step(0)
    weight_grad(1)
    gather_near_step(1)
    gather_far_step(0)
    second_sum(0)
    gather_far_step(1)
    second_sum(1)
    z_sum(0)
    z_sum(1)
    attn_grad()
    share(0)
    backward((0,1))
    share(1)
    projection()
    backward((2,3))
    grads()
    mean()
    layer_out()
    return (result["layer_out"][None], *[g[None] for g in result["grads"]], result["weight_grad"])


def solution(mesh):
    in_specs = (
        P("dp", "ctx", None),
        P("dp", "ctx", None),
        P("dp", "ctx", None),
        P("dp", "ctx"),
        P("dp", None, None),
        P("dp", None),
        P("dp", "ctx", None),
    )
    out_specs = (
        P("dp", "ctx", None),
        P("dp", "ctx", None),
        P("dp", "ctx", None),
        P("dp", "ctx", None),
        P("dp", None),
    )
    body = chip_shards if (mesh.shape["dp"], mesh.shape["ctx"]) == (16, 2) else shards
    return jax.shard_map(body, mesh=mesh, in_specs=in_specs, out_specs=out_specs, check_vma=False)
```

```python
import functools
import itertools
import math

import jax
import jax.numpy as jnp
import numpy as np
from jax import lax
from jax.experimental import pallas as pl
from jax.experimental.pallas import tpu as pltpu
from jax.sharding import PartitionSpec as P

H = 8
HD = 128
BLK = 128
KB = 4
SUM_CHUNKS = 2


def padded(shard, sides, width):
    for axis, dim in sides:
        devices, length = (lax.axis_size(axis), shard.shape[dim])
        up = [(i, (i + 1) % devices) for i in range(devices - 1)]
        down = [(j, i) for i, j in up]
        last = lax.slice_in_dim(shard, length - width, length, axis=dim)
        leading = lax.slice_in_dim(shard, 0, width, axis=dim)
        before = lax.ppermute(last, axis, up)
        after = lax.ppermute(leading, axis, down)
        shard = jnp.concatenate([before, shard, after], axis=dim)
    return shard


def from_behind(block, axis, distance):
    devices = range(lax.axis_size(axis))
    route = [(i - distance, i) for i in devices if i - distance in devices]
    return lax.ppermute(block, axis, route)


def rope_tables(positions):
    coords = jnp.stack(
        [positions % 8, positions // 8 % 8, positions // 64 % 4, positions // 256], axis=1
    ).astype(jnp.float32)
    per_axis = HD // 16
    frequency = 100.0 ** (-jnp.arange(per_axis, dtype=jnp.float32) / per_axis)
    angle = (coords[:, :, None] * frequency[None, None, :]).reshape(
        positions.shape[0], 4 * per_axis
    )
    return (jnp.cos(angle), jnp.sin(angle))


def rotate_heads(heads, cosine, sine_vals, direction):
    quarter = HD // 4
    first_part = heads[..., :quarter]
    second_part = heads[..., quarter : 2 * quarter]
    cos_rows = cosine[:, None, :]
    sin_rows = direction * sine_vals[:, None, :]
    return jnp.concatenate(
        [
            first_part * cos_rows - second_part * sin_rows,
            second_part * cos_rows + first_part * sin_rows,
            heads[..., 2 * quarter :],
        ],
        axis=-1,
    )


def attend_forward(query_blocks, key_sets, value_sets, key_mask, score_scale):
    scores = (
        jnp.einsum("nqhd,nkhd->nhqk", query_blocks, key_sets, preferred_element_type=jnp.float32)
        * score_scale
    )
    scores = jnp.where(key_mask[:, None, None, :], scores, -jnp.inf)
    row_peak = jnp.max(scores, axis=-1)
    row_total = jnp.sum(jnp.exp(scores - row_peak[..., None]), axis=-1)
    log_total = row_peak + jnp.log(row_total)
    soft_probs = jnp.exp(scores - log_total[..., None]).astype(jnp.bfloat16)
    block_out = jnp.einsum(
        "nhqk,nkhd->nqhd", soft_probs, value_sets, preferred_element_type=jnp.float32
    ).astype(jnp.bfloat16)
    return (block_out, log_total)


def attend_backward(
    query_blocks,
    key_sets,
    value_sets,
    key_mask,
    log_total,
    grad_dot,
    grad_blocks,
    score_scale,
    key_form,
):
    scores = (
        jnp.einsum(
            "nqhd," + key_form + "->nhqk",
            query_blocks,
            key_sets,
            preferred_element_type=jnp.float32,
        )
        * score_scale
    )
    scores = jnp.where(key_mask[:, None, None, :], scores, -jnp.inf)
    exact_probs = jnp.exp(scores - log_total[..., None])
    soft_probs = exact_probs.astype(jnp.bfloat16)
    value_part = jnp.einsum(
        "nhqk,nqhd->" + key_form, soft_probs, grad_blocks, preferred_element_type=jnp.float32
    )
    prob_grad = jnp.einsum(
        "nqhd," + key_form + "->nhqk", grad_blocks, value_sets, preferred_element_type=jnp.float32
    )
    score_grad = (exact_probs * (prob_grad - grad_dot[..., None]) * score_scale).astype(
        jnp.bfloat16
    )
    query_part = jnp.einsum(
        "nhqk," + key_form + "->nqhd", score_grad, key_sets, preferred_element_type=jnp.float32
    )
    key_part = jnp.einsum(
        "nhqk,nqhd->" + key_form, score_grad, query_blocks, preferred_element_type=jnp.float32
    )
    return (query_part, key_part, value_part)


def shards(queries, key_states, value_states, token_order, block_pattern, out_weight, out_grad):
    row_count = queries.shape[1]
    feature_width = queries.shape[2]
    local_blocks = row_count // BLK
    shard_index = lax.axis_index("ctx")
    score_scale = 1.0 / math.sqrt(HD)
    cosine, sine_vals = rope_tables(token_order[0])
    rot_query = rotate_heads(
        queries[0].astype(jnp.float32).reshape(row_count, H, HD), cosine, sine_vals, 1.0
    ).astype(jnp.bfloat16)
    rot_keys = rotate_heads(
        key_states[0].astype(jnp.float32).reshape(row_count, H, HD), cosine, sine_vals, 1.0
    ).astype(jnp.bfloat16)
    stacked = jnp.stack([rot_keys.reshape(row_count, feature_width), value_states[0]], axis=1)
    extended = padded(stacked, (("ctx", 0),), row_count)
    ext_blocks = extended.reshape(3 * local_blocks, BLK, 2, H, HD)
    pattern_rows = block_pattern[0]
    first_block = shard_index * local_blocks
    my_pattern = lax.dynamic_slice_in_dim(pattern_rows, first_block, local_blocks, 0)
    slot_valid = my_pattern >= 0
    slot_local = jnp.where(slot_valid, my_pattern - first_block + local_blocks, 0)
    gathered = jnp.take(ext_blocks, slot_local, axis=0)
    key_sets = gathered[:, :, :, 0].reshape(local_blocks, KB * BLK, H, HD)
    value_sets = gathered[:, :, :, 1].reshape(local_blocks, KB * BLK, H, HD)
    key_mask = jnp.repeat(slot_valid, BLK, axis=1)
    query_blocks = rot_query.reshape(local_blocks, BLK, H, HD)
    block_out, log_total = attend_forward(query_blocks, key_sets, value_sets, key_mask, score_scale)
    attn = block_out.reshape(row_count, feature_width)
    grad_rows = out_grad[0]
    forward_weight = lax.all_gather(out_weight, "dp", axis=0, tiled=True)
    layer_out = jnp.dot(attn, forward_weight, preferred_element_type=jnp.float32).astype(
        jnp.bfloat16
    )
    attn_grad = lax.dot_general(
        grad_rows,
        lax.all_gather(out_weight, "dp", axis=0, tiled=True),
        (((1,), (1,)), ((), ())),
        preferred_element_type=jnp.float32,
    ).astype(jnp.bfloat16)
    batch_count = lax.axis_size("dp")
    local_grad = lax.psum_scatter(
        lax.dot_general(
            attn, grad_rows, (((0,), (0,)), ((), ())), preferred_element_type=jnp.float32
        )
        / batch_count,
        "dp",
        scatter_dimension=0,
        tiled=True,
    )
    weight_grad = lax.psum(local_grad, "ctx")
    dot_rows = jnp.sum(
        (attn_grad.astype(jnp.float32) * attn.astype(jnp.float32)).reshape(row_count, H, HD),
        axis=-1,
    )
    grad_dot = dot_rows.reshape(local_blocks, BLK, H).transpose(0, 2, 1)
    grad_blocks = attn_grad.reshape(local_blocks, BLK, H, HD)
    query_part, key_part, value_part = attend_backward(
        query_blocks,
        key_sets,
        value_sets,
        key_mask,
        log_total,
        grad_dot,
        grad_blocks,
        score_scale,
        "nkhd",
    )
    query_grad = (
        rotate_heads(query_part.reshape(row_count, H, HD), cosine, sine_vals, -1.0)
        .reshape(row_count, feature_width)
        .astype(jnp.bfloat16)
    )
    keep = slot_valid.reshape(local_blocks * KB).astype(jnp.float32)[:, None, None, None, None]
    both_parts = (
        jnp.stack(
            [
                key_part.reshape(local_blocks * KB, BLK, H, HD),
                value_part.reshape(local_blocks * KB, BLK, H, HD),
            ],
            axis=2,
        )
        * keep
    )
    accumulated = (
        jnp.zeros((3 * local_blocks, BLK, 2, H, HD), jnp.float32)
        .at[slot_local.reshape(-1)]
        .add(both_parts)
    )
    accumulated = accumulated.reshape(3 * row_count, 2, feature_width)
    own_part = accumulated[row_count : 2 * row_count]
    from_right = from_behind(accumulated[:row_count], "ctx", -1)
    from_left = from_behind(accumulated[2 * row_count :], "ctx", 1)
    summed = own_part + from_right + from_left
    key_total = summed[:, 0]
    value_total = summed[:, 1]
    key_grad = (
        rotate_heads(key_total.reshape(row_count, H, HD), cosine, sine_vals, -1.0)
        .reshape(row_count, feature_width)
        .astype(jnp.bfloat16)
    )
    value_grad = value_total.astype(jnp.bfloat16)
    return (layer_out[None], query_grad[None], key_grad[None], value_grad[None], weight_grad)

def chip_moves(rule):
    pairs = []
    for z, y, x, core in itertools.product(range(4), range(2), range(2), range(2)):
        target = rule(z, y, x, core)
        if target is not None:
            tz, ty, tx, tcore = target
            pairs.append((((z * 2 + y) * 2 + x) * 2 + core, ((tz * 2 + ty) * 2 + tx) * 2 + tcore))
    return pairs


def swap_x(z, y, x, core):
    return (z, y, 1 - x, core)


def swap_y(z, y, x, core):
    return (z, 1 - y, x, core)


def move(array, rule):
    return lax.ppermute(array, ("dp", "ctx"), chip_moves(rule))


def swap_core(array):
    return lax.ppermute(array, "ctx", [(0, 1), (1, 0)])


def gather_first(z, y, x, core):
    return (z ^ 2, y, x, core) if z // 2 == core else (z ^ 1, y, x, 1 - core)


def gather_second(z, y, x, core):
    return (z ^ 3, y, x, core) if z // 2 == core else None


def gather_near(z, y, x, core):
    return swap_y(z, y, x, core) if core == 0 else swap_x(z, y, x, core)


def gather_far(z, y, x, core):
    return swap_x(z, y, x, core) if core == 0 else swap_y(z, y, x, core)


def scatter_first(z, y, x, core):
    return (z ^ 1, y, x, 1 - core) if z // 2 == core else (z ^ 2, y, x, core)


def scatter_second(z, y, x, core):
    return None if z // 2 == core else (z ^ 3, y, x, core)


def dot_nt(a, b):
    return lax.dot_general(a, b, (((1,), (1,)), ((), ())), preferred_element_type=jnp.float32)


def dot_nn(a, b):
    return jnp.dot(a, b, preferred_element_type=jnp.float32)


def rope_table(order):
    per_axis = HD // 16
    shape = (4 * per_axis, order.shape[1])
    row = lax.broadcasted_iota(jnp.int32, shape, 0)
    axis_of, step = row // per_axis, row % per_axis
    coords = jnp.where(
        axis_of == 0,
        order % 8,
        jnp.where(axis_of == 1, order // 8 % 8, jnp.where(axis_of == 2, order // 64 % 4, order // 256)),
    )
    frequency = jnp.zeros(shape, jnp.float32)
    for i in range(per_axis):
        frequency = jnp.where(step == i, jnp.float32(100.0 ** (-i / per_axis)), frequency)
    angle = coords.astype(jnp.float32) * frequency
    return jnp.cos(angle), jnp.sin(angle)


def rotate_rows(x, cos, sin):
    quarter = HD // 4
    f, g, rest = x[0:quarter], x[quarter : 2 * quarter], x[2 * quarter :]
    return jnp.concatenate([f * cos - g * sin, g * cos + f * sin, rest], axis=0).astype(jnp.bfloat16)


def place():
    dp = lax.axis_index("dp")
    return lax.axis_index("ctx"), dp // 4, dp // 2 % 2, dp % 2


def block_bias(pattern, core, bias):
    blocks = bias.shape[0]
    lane_block = lax.broadcasted_iota(jnp.int32, (1, bias.shape[1]), 1) // BLK
    for key_local in range(blocks):
        key_block = (key_local + 2 * core) % blocks
        row = jnp.full(lane_block.shape, -jnp.inf, jnp.float32)
        for query_local in range(blocks):
            query_block = (query_local + 2 * core) % blocks
            listed = jnp.int32(0)
            for slot in range(KB):
                listed = listed + jnp.where(pattern[0, query_block, slot] == key_block, 1, 0)
            row = jnp.where((lane_block == query_local) & (listed > 0), 0.0, row)
        bias[key_local : key_local + 1, :] = row


def scaled_scores(keys, queries_t, bias):
    scores = dot_nn(keys, queries_t) * (math.log2(math.e) / math.sqrt(HD))
    parts = [scores[b * BLK : (b + 1) * BLK, :] + bias[b : b + 1, :] for b in range(bias.shape[0])]
    return jnp.concatenate(parts, axis=0)


def pack_kernel(*refs):
    inputs, out, own, sems = refs[:3], refs[-3], refs[-2], refs[-1]
    mine = out.shape[2]
    copies = []
    for target, core in ((out, 1 - place()[0]), (own, place()[0])):
        there = pl.ds(pl.multiple_of(core * mine, mine), mine)
        for i, a in enumerate(inputs):
            copies.append(pltpu.make_async_copy(a.at[:, there], target.at[i], sems.at[len(copies)]))
            copies[-1].start()
    for copy in copies:
        copy.wait()


def forward_kernel(pattern, near, far, own, received, *refs):
    rot_q, rot_k, rot_kt, values, attn, attn_t, lse, bias, cos_ref, sin_ref = refs[-10:]
    tokens = 2 * own.shape[1]
    step = BLK
    core, z, _, _ = place()
    block_bias(pattern, core, bias)
    cos, sin = rope_table(jnp.concatenate([near[...], far[...]], axis=1))
    cos_ref[...] = cos
    sin_ref[...] = sin
    for head in range(rot_q.shape[0] // HD):
        cols = slice(head * HD, (head + 1) * HD)
        taken = (head // 2 ^ z % 2) * 2 + head % 2
        taken = pl.ds(pl.multiple_of(taken * HD, HD), HD)
        query, key, value = (
            jnp.concatenate([own[i, :, taken], received[i, :, taken]], axis=0) for i in range(3)
        )
        rot_q[cols, :] = rotate_rows(query.T.astype(jnp.float32), cos, sin)
        keys_t = rotate_rows(key.T.astype(jnp.float32), cos, sin)
        rot_kt[cols, :] = keys_t
        keys = keys_t.T
        rot_k[:, cols] = keys
        values[:, cols] = value
        value_t = value.T
        for part in range(tokens // step):
            at = slice(part * step, (part + 1) * step)
            scores = scaled_scores(keys, rot_q[cols, at], bias[:, at])
            peak = jnp.max(scores, axis=0, keepdims=True)
            raised = jnp.exp2(scores - peak)
            total = jnp.sum(raised, axis=0, keepdims=True)
            mixed = dot_nn(value_t, raised.astype(jnp.bfloat16)) * (1.0 / total)
            mixed = mixed.astype(jnp.bfloat16)
            attn_t[cols, at] = mixed
            attn[at, cols] = mixed.T
            lse[head : head + 1, at] = peak + jnp.log2(total)


def weight_grad_kernel(attn_t, own, other, *refs, chunk):
    send, keep = refs[-2:]
    core, _, y, x = place()
    piece, width = send.shape[2:]
    cols = slice(chunk * width, (chunk + 1) * width)
    tokens = jnp.concatenate([own[:, cols], other[:, cols]], axis=0)
    for block in range(attn_t.shape[0] // (2 * piece)):
        rows = slice(block * 2 * piece, (block + 1) * 2 * piece)
        part = dot_nn(attn_t[rows, :], tokens).astype(send.dtype)
        z_rel = block // 2
        for head_x in range(2):
            out = part[head_x * piece : (head_x + 1) * piece, :]
            first = jnp.where(core == 0, head_x ^ x, (block % 2) ^ y)
            sub = jnp.where(core == 0, (block % 2) ^ y, head_x ^ x)

            @pl.when(first == 1)
            def _():
                send[sub, z_rel] = out

            @pl.when(first == 0)
            def _():
                keep[sub, z_rel] = out


def attn_grad_kernel(attn_t, own, other, near, far, *refs, pair):
    grad_t, dots, weight = refs[-3:]
    core, _, y, x = place()
    piece = near.shape[1]
    for e3, ref in enumerate((near, far)):
        for e2 in range(2):
            y_at = jnp.where(core == 0, y ^ e2, y ^ e3)
            x_at = jnp.where(core == 0, x ^ e3, x ^ e2)
            start = (y_at * 2 + x_at) * piece
            weight[pl.ds(pl.multiple_of(start, piece), piece), :] = ref[e2]
    size = weight.shape[0]
    tokens = jnp.concatenate([own[...], other[...]], axis=0)
    rounded = dot_nt(weight[...], tokens).astype(grad_t.dtype)
    grad_t[...] = rounded
    product = rounded.astype(jnp.float32) * attn_t[pair * size : (pair + 1) * size, :].astype(jnp.float32)
    for head in range(size // HD):
        dots[head : head + 1, :] = jnp.sum(product[head * HD : (head + 1) * HD], axis=0, keepdims=True)


def projection_kernel(attn, low, high, *refs):
    out_send, out_own = refs[-2:]
    half = out_own.shape[0]
    for c in range(low.shape[1] // half):
        cols = slice(c * half, (c + 1) * half)
        part = dot_nn(attn[...], jnp.concatenate([low[:, cols], high[:, cols]], axis=0))
        out_send[:, cols] = part[half:].astype(out_send.dtype)
        out_own[:, cols] = part[:half]


def backward_kernel(rot_q, rot_k, rot_kt, values, grad_t, dots, lse, bias, cos_ref, sin_ref, *refs, pair):
    send, own = refs[-2:]
    tokens = rot_k.shape[0]
    half = tokens // 2
    step = 2 * BLK
    scale = 1.0 / math.sqrt(HD)
    cos, sin = cos_ref[...], -sin_ref[...]
    for at_head in range(2):
        head = pair * 2 + at_head
        cols = slice(head * HD, (head + 1) * HD)
        out_cols = slice(at_head * HD, (at_head + 1) * HD)
        keys, keys_t, value = rot_k[:, cols], rot_kt[cols, :], values[:, cols]
        key_sum = jnp.zeros((HD, tokens), jnp.float32)
        value_sum = jnp.zeros((HD, tokens), jnp.float32)
        query_parts = []
        for part in range(tokens // step):
            at = slice(part * step, (part + 1) * step)
            queries_t, grads_t = rot_q[cols, at], grad_t[out_cols, at]
            scores = scaled_scores(keys, queries_t, bias[:, at])
            exact = jnp.exp2(scores - lse[head : head + 1, at])
            prob_grad = dot_nn(value, grads_t)
            score_grad = (exact * (prob_grad - dots[at_head : at_head + 1, at])).astype(jnp.bfloat16)
            value_sum = value_sum + dot_nt(grads_t, exact.astype(jnp.bfloat16))
            key_sum = key_sum + dot_nt(queries_t, score_grad)
            query_parts.append(dot_nn(keys_t, score_grad))
        query_sum = jnp.concatenate(query_parts, axis=1)
        outs = (
            rotate_rows(query_sum * scale, cos, sin),
            rotate_rows(key_sum * scale, cos, sin),
            value_sum.astype(jnp.bfloat16),
        )
        for i, out in enumerate(outs):
            out = out.T
            own[i, :, out_cols] = out[0:half, :]
            send[i, :, out_cols] = out[half:, :]


def gather_pick_kernel(home, away, *refs):
    core, z, _, _ = place()
    near = refs[-1]

    @pl.when(z // 2 == core)
    def _():
        near[...] = home[...]

    @pl.when(z // 2 != core)
    def _():
        near[...] = away[...]


def pair_kernel(a, b, *refs):
    refs[-1][0] = a[...]
    refs[-1][1] = b[...]


def second_sum_kernel(keep, got, *refs):
    send, kept = refs[-2:]
    send[...] = (keep[1].astype(jnp.float32) + got[1].astype(jnp.float32)).astype(send.dtype)
    kept[...] = keep[0].astype(jnp.float32) + got[0].astype(jnp.float32)


def z_sum_kernel(kept, got, *refs):
    to_first, to_second, own = refs[-3:]
    core, z, _, _ = place()
    at_home = z // 2 == core
    near = kept[0] + got[0].astype(jnp.float32)
    rest = kept[1] + got[1].astype(jnp.float32)
    own[...] = near
    to_first[...] = jnp.where(at_home, rest, near).astype(to_first.dtype)
    to_second[...] = rest.astype(to_second.dtype)


def share_kernel(own, first, second, *refs):
    core, z, _, _ = place()
    at_home = z // 2 == core
    total = own[...] + first[...].astype(jnp.float32) + second[...].astype(jnp.float32)
    refs[-1][...] = jnp.where(at_home, total, first[...].astype(jnp.float32))


def finish_kernel(*refs, count):
    layer_out, *grads, mean = refs[-5:]
    out_own, out_got = refs[:2]
    pairs, shares = refs[2:6], refs[6:-5]
    core, z, _, _ = place()
    mine = grads[0].shape[1] // 2
    width = mine // 2
    for pair in range(2):
        for source in range(2):
            start = (core ^ source) * mine + (z % 2 ^ pair) * width
            cols = pl.ds(pl.multiple_of(start, width), width)
            for i in range(3):
                grads[i][:, cols] = pairs[2 * pair + source][i]
    layer_out[...] = (out_own[...] + out_got[...].astype(jnp.float32)).astype(layer_out.dtype)
    width = shares[0].shape[1]
    for i in range(mean.shape[1] // width):
        mean[:, i * width : (i + 1) * width] = (shares[2 * i][...] + shares[2 * i + 1][...]) * (1.0 / count)


def chip_shards(queries, key_states, value_states, token_order, block_pattern, out_weight, out_grad):
    rows, width = queries.shape[1:]
    model = out_grad.shape[2]
    tokens, mine = 2 * rows, width // 2
    owned = out_weight.shape[0]
    bf16, f32 = jnp.bfloat16, jnp.float32
    in_vmem = pl.BlockSpec(memory_space=pltpu.VMEM)
    in_smem = pl.BlockSpec(memory_space=pltpu.SMEM)
    in_hbm = pl.BlockSpec(memory_space=pltpu.HBM)
    anywhere = pl.BlockSpec(memory_space=pl.ANY)
    done = []

    def call(kernel, name, args, outs, scratch=(), limit=8, specs=None, final=False):
        before = [a for a in done if not any(a is b for b in args)]
        results = pl.pallas_call(
            kernel,
            in_specs=list(specs or [in_vmem] * len(args)) + [anywhere] * len(before),
            out_specs=[in_vmem] * len(outs),
            out_shape=[jax.ShapeDtypeStruct(s, d) for s, d in outs],
            scratch_shapes=scratch,
            compiler_params=pltpu.CompilerParams(vmem_limit_bytes=limit << 20),
            cost_estimate=pl.CostEstimate(flops=10000000000, bytes_accessed=1, transcendentals=0),
            name=name,
        )(*args, *before)
        if not final:
            done[:] = results[:1]
        return results

    q_own, k_own, v_own, dy_own = queries[0], key_states[0], value_states[0], out_grad[0]
    q_in, k_in, v_in = (pltpu.with_memory_space_constraint(a, pltpu.HBM) for a in (q_own, k_own, v_own))
    pack, own = call(
        pack_kernel,
        "pack",
        (q_in, k_in, v_in),
        [((3, rows, mine), bf16)] * 2,
        specs=[in_hbm] * 3,
        scratch=[pltpu.SemaphoreType.DMA((6,))],
        final=True,
    )
    received = swap_core(pack)
    order_far = swap_core(token_order)
    dy_far = swap_core(dy_own)

    first, second = move(out_weight, gather_first), move(out_weight, gather_second)
    z_parts = ((out_weight, first), (first, second))
    chunks = 2

    rot_q, rot_k, rot_kt, values, attn, attn_t, lse, bias, cos, sin = call(
        forward_kernel,
        "forward",
        (block_pattern, token_order, order_far, own, received),
        [((mine, tokens), bf16), ((tokens, mine), bf16), ((mine, tokens), bf16)]
        + [((tokens, mine), bf16)] * 2
        + [((mine, tokens), bf16), ((mine // HD, tokens), f32), ((tokens // BLK, tokens), f32)]
        + [((HD // 4, tokens), f32)] * 2,
        limit=24,
        specs=[in_smem] + [in_vmem] * 4,
    )
    sums = SUM_CHUNKS
    cols = model // sums
    near, joined, weights, attn_grads, pairs = ([None] * chunks for _ in range(5))
    parts, z_sums, shares = [None] * sums, [None] * sums, [None] * sums
    result = {}

    def weight_grad(i):
        send, keep = call(
            functools.partial(weight_grad_kernel, chunk=i),
            "weight_grad",
            (attn_t, dy_own, dy_far),
            [((2, 2, owned, cols), bf16)] * 2,
            limit=16,
        )
        parts[i] = (keep, move(send, gather_far))

    def gather_near_step(i):
        (near[i],) = call(gather_pick_kernel, "gather_pick", z_parts[i], [((owned, model), bf16)])
        joined[i] = move(near[i], gather_near)

    def gather_far_step(i):
        (pair,) = call(pair_kernel, "pair", (near[i], joined[i]), [((2, owned, model), bf16)])
        weights[i] = pair, move(pair, gather_far)

    def second_sum(i):
        send, kept = call(
            second_sum_kernel,
            "second_sum",
            parts[i],
            [((2, owned, cols), bf16), ((2, owned, cols), f32)],
        )
        parts[i] = (kept, move(send, gather_near))

    def z_sum(i):
        to_first, to_second, own = call(
            z_sum_kernel,
            "z_sum",
            parts[i],
            [((owned, cols), bf16)] * 2 + [((owned, cols), f32)],
        )
        z_sums[i] = own, move(to_first, scatter_first), move(to_second, scatter_second)

    def share(i):
        (part,) = call(share_kernel, "share", z_sums[i], [((owned, cols), f32)])
        shares[i] = part, swap_core(part)

    def attn_grad(i):
        attn_grads[i] = call(
            functools.partial(attn_grad_kernel, pair=i),
            "attn_grad",
            (attn_t, dy_own, dy_far, *weights[i]),
            [((2 * HD, tokens), bf16), ((2, tokens), f32), ((2 * HD, model), bf16)],
            limit=16,
        )

    def projection():
        out_send, out_own = call(
            projection_kernel,
            "projection",
            (attn, attn_grads[0][2], attn_grads[1][2]),
            [((rows, model), bf16), ((rows, model), f32)],
            limit=16,
        )
        result["out"] = (out_own, swap_core(out_send))

    def backward(i):
        send, own = call(
            functools.partial(backward_kernel, pair=i),
            "backward",
            (rot_q, rot_k, rot_kt, values, *attn_grads[i][:2], lse, bias, cos, sin),
            [((3, rows, 2 * HD), bf16)] * 2,
            limit=24,
        )
        pairs[i] = own, swap_core(send)

    def finish():
        args = (*result["out"], *pairs[0], *pairs[1], *(a for s in shares for a in s))
        result["all"] = call(
            functools.partial(finish_kernel, count=lax.axis_size("dp")),
            "finish",
            args,
            [((rows, model), bf16)] + [((rows, width), bf16)] * 3 + [((owned, model), f32)],
            limit=24,
            final=True,
        )

    weight_grad(0)
    gather_near_step(0)
    weight_grad(1)
    gather_near_step(1)
    gather_far_step(0)
    second_sum(0)
    gather_far_step(1)
    second_sum(1)
    z_sum(0)
    z_sum(1)
    attn_grad(0)
    backward(0)
    share(0)
    attn_grad(1)
    backward(1)
    projection()
    share(1)
    finish()
    *sharded, weight_grad = result["all"]
    return (*[a[None] for a in sharded], weight_grad)


def solution(mesh):
    in_specs = (
        P("dp", "ctx", None),
        P("dp", "ctx", None),
        P("dp", "ctx", None),
        P("dp", "ctx"),
        P("dp", None, None),
        P("dp", None),
        P("dp", "ctx", None),
    )
    out_specs = (
        P("dp", "ctx", None),
        P("dp", "ctx", None),
        P("dp", "ctx", None),
        P("dp", "ctx", None),
        P("dp", None),
    )
    body = chip_shards if (mesh.shape["dp"], mesh.shape["ctx"]) == (16, 2) else shards
    return jax.shard_map(body, mesh=mesh, in_specs=in_specs, out_specs=out_specs, check_vma=False)
```

```python
import functools
import itertools
import math

import jax
import jax.numpy as jnp
import numpy as np
from jax import lax
from jax.experimental import pallas as pl
from jax.experimental.pallas import tpu as pltpu
from jax.sharding import PartitionSpec as P

H = 8
HD = 128
BLK = 128
KB = 4
SUM_CHUNKS = 2


def padded(shard, sides, width):
    for axis, dim in sides:
        devices, length = (lax.axis_size(axis), shard.shape[dim])
        up = [(i, (i + 1) % devices) for i in range(devices - 1)]
        down = [(j, i) for i, j in up]
        last = lax.slice_in_dim(shard, length - width, length, axis=dim)
        leading = lax.slice_in_dim(shard, 0, width, axis=dim)
        before = lax.ppermute(last, axis, up)
        after = lax.ppermute(leading, axis, down)
        shard = jnp.concatenate([before, shard, after], axis=dim)
    return shard


def from_behind(block, axis, distance):
    devices = range(lax.axis_size(axis))
    route = [(i - distance, i) for i in devices if i - distance in devices]
    return lax.ppermute(block, axis, route)


def rope_tables(positions):
    coords = jnp.stack(
        [positions % 8, positions // 8 % 8, positions // 64 % 4, positions // 256], axis=1
    ).astype(jnp.float32)
    per_axis = HD // 16
    frequency = 100.0 ** (-jnp.arange(per_axis, dtype=jnp.float32) / per_axis)
    angle = (coords[:, :, None] * frequency[None, None, :]).reshape(
        positions.shape[0], 4 * per_axis
    )
    return (jnp.cos(angle), jnp.sin(angle))


def rotate_heads(heads, cosine, sine_vals, direction):
    quarter = HD // 4
    first_part = heads[..., :quarter]
    second_part = heads[..., quarter : 2 * quarter]
    cos_rows = cosine[:, None, :]
    sin_rows = direction * sine_vals[:, None, :]
    return jnp.concatenate(
        [
            first_part * cos_rows - second_part * sin_rows,
            second_part * cos_rows + first_part * sin_rows,
            heads[..., 2 * quarter :],
        ],
        axis=-1,
    )


def attend_forward(query_blocks, key_sets, value_sets, key_mask, score_scale):
    scores = (
        jnp.einsum("nqhd,nkhd->nhqk", query_blocks, key_sets, preferred_element_type=jnp.float32)
        * score_scale
    )
    scores = jnp.where(key_mask[:, None, None, :], scores, -jnp.inf)
    row_peak = jnp.max(scores, axis=-1)
    row_total = jnp.sum(jnp.exp(scores - row_peak[..., None]), axis=-1)
    log_total = row_peak + jnp.log(row_total)
    soft_probs = jnp.exp(scores - log_total[..., None]).astype(jnp.bfloat16)
    block_out = jnp.einsum(
        "nhqk,nkhd->nqhd", soft_probs, value_sets, preferred_element_type=jnp.float32
    ).astype(jnp.bfloat16)
    return (block_out, log_total)


def attend_backward(
    query_blocks,
    key_sets,
    value_sets,
    key_mask,
    log_total,
    grad_dot,
    grad_blocks,
    score_scale,
    key_form,
):
    scores = (
        jnp.einsum(
            "nqhd," + key_form + "->nhqk",
            query_blocks,
            key_sets,
            preferred_element_type=jnp.float32,
        )
        * score_scale
    )
    scores = jnp.where(key_mask[:, None, None, :], scores, -jnp.inf)
    exact_probs = jnp.exp(scores - log_total[..., None])
    soft_probs = exact_probs.astype(jnp.bfloat16)
    value_part = jnp.einsum(
        "nhqk,nqhd->" + key_form, soft_probs, grad_blocks, preferred_element_type=jnp.float32
    )
    prob_grad = jnp.einsum(
        "nqhd," + key_form + "->nhqk", grad_blocks, value_sets, preferred_element_type=jnp.float32
    )
    score_grad = (exact_probs * (prob_grad - grad_dot[..., None]) * score_scale).astype(
        jnp.bfloat16
    )
    query_part = jnp.einsum(
        "nhqk," + key_form + "->nqhd", score_grad, key_sets, preferred_element_type=jnp.float32
    )
    key_part = jnp.einsum(
        "nhqk,nqhd->" + key_form, score_grad, query_blocks, preferred_element_type=jnp.float32
    )
    return (query_part, key_part, value_part)


def shards(queries, key_states, value_states, token_order, block_pattern, out_weight, out_grad):
    row_count = queries.shape[1]
    feature_width = queries.shape[2]
    local_blocks = row_count // BLK
    shard_index = lax.axis_index("ctx")
    score_scale = 1.0 / math.sqrt(HD)
    cosine, sine_vals = rope_tables(token_order[0])
    rot_query = rotate_heads(
        queries[0].astype(jnp.float32).reshape(row_count, H, HD), cosine, sine_vals, 1.0
    ).astype(jnp.bfloat16)
    rot_keys = rotate_heads(
        key_states[0].astype(jnp.float32).reshape(row_count, H, HD), cosine, sine_vals, 1.0
    ).astype(jnp.bfloat16)
    stacked = jnp.stack([rot_keys.reshape(row_count, feature_width), value_states[0]], axis=1)
    extended = padded(stacked, (("ctx", 0),), row_count)
    ext_blocks = extended.reshape(3 * local_blocks, BLK, 2, H, HD)
    pattern_rows = block_pattern[0]
    first_block = shard_index * local_blocks
    my_pattern = lax.dynamic_slice_in_dim(pattern_rows, first_block, local_blocks, 0)
    slot_valid = my_pattern >= 0
    slot_local = jnp.where(slot_valid, my_pattern - first_block + local_blocks, 0)
    gathered = jnp.take(ext_blocks, slot_local, axis=0)
    key_sets = gathered[:, :, :, 0].reshape(local_blocks, KB * BLK, H, HD)
    value_sets = gathered[:, :, :, 1].reshape(local_blocks, KB * BLK, H, HD)
    key_mask = jnp.repeat(slot_valid, BLK, axis=1)
    query_blocks = rot_query.reshape(local_blocks, BLK, H, HD)
    block_out, log_total = attend_forward(query_blocks, key_sets, value_sets, key_mask, score_scale)
    attn = block_out.reshape(row_count, feature_width)
    grad_rows = out_grad[0]
    forward_weight = lax.all_gather(out_weight, "dp", axis=0, tiled=True)
    layer_out = jnp.dot(attn, forward_weight, preferred_element_type=jnp.float32).astype(
        jnp.bfloat16
    )
    attn_grad = lax.dot_general(
        grad_rows,
        lax.all_gather(out_weight, "dp", axis=0, tiled=True),
        (((1,), (1,)), ((), ())),
        preferred_element_type=jnp.float32,
    ).astype(jnp.bfloat16)
    batch_count = lax.axis_size("dp")
    local_grad = lax.psum_scatter(
        lax.dot_general(
            attn, grad_rows, (((0,), (0,)), ((), ())), preferred_element_type=jnp.float32
        )
        / batch_count,
        "dp",
        scatter_dimension=0,
        tiled=True,
    )
    weight_grad = lax.psum(local_grad, "ctx")
    dot_rows = jnp.sum(
        (attn_grad.astype(jnp.float32) * attn.astype(jnp.float32)).reshape(row_count, H, HD),
        axis=-1,
    )
    grad_dot = dot_rows.reshape(local_blocks, BLK, H).transpose(0, 2, 1)
    grad_blocks = attn_grad.reshape(local_blocks, BLK, H, HD)
    query_part, key_part, value_part = attend_backward(
        query_blocks,
        key_sets,
        value_sets,
        key_mask,
        log_total,
        grad_dot,
        grad_blocks,
        score_scale,
        "nkhd",
    )
    query_grad = (
        rotate_heads(query_part.reshape(row_count, H, HD), cosine, sine_vals, -1.0)
        .reshape(row_count, feature_width)
        .astype(jnp.bfloat16)
    )
    keep = slot_valid.reshape(local_blocks * KB).astype(jnp.float32)[:, None, None, None, None]
    both_parts = (
        jnp.stack(
            [
                key_part.reshape(local_blocks * KB, BLK, H, HD),
                value_part.reshape(local_blocks * KB, BLK, H, HD),
            ],
            axis=2,
        )
        * keep
    )
    accumulated = (
        jnp.zeros((3 * local_blocks, BLK, 2, H, HD), jnp.float32)
        .at[slot_local.reshape(-1)]
        .add(both_parts)
    )
    accumulated = accumulated.reshape(3 * row_count, 2, feature_width)
    own_part = accumulated[row_count : 2 * row_count]
    from_right = from_behind(accumulated[:row_count], "ctx", -1)
    from_left = from_behind(accumulated[2 * row_count :], "ctx", 1)
    summed = own_part + from_right + from_left
    key_total = summed[:, 0]
    value_total = summed[:, 1]
    key_grad = (
        rotate_heads(key_total.reshape(row_count, H, HD), cosine, sine_vals, -1.0)
        .reshape(row_count, feature_width)
        .astype(jnp.bfloat16)
    )
    value_grad = value_total.astype(jnp.bfloat16)
    return (layer_out[None], query_grad[None], key_grad[None], value_grad[None], weight_grad)

def chip_moves(rule):
    pairs = []
    for z, y, x, core in itertools.product(range(4), range(2), range(2), range(2)):
        target = rule(z, y, x, core)
        if target is not None:
            tz, ty, tx, tcore = target
            pairs.append((((z * 2 + y) * 2 + x) * 2 + core, ((tz * 2 + ty) * 2 + tx) * 2 + tcore))
    return pairs


def swap_x(z, y, x, core):
    return (z, y, 1 - x, core)


def swap_y(z, y, x, core):
    return (z, 1 - y, x, core)


def move(array, rule):
    return lax.ppermute(array, ("dp", "ctx"), chip_moves(rule))


def swap_core(array):
    return lax.ppermute(array, "ctx", [(0, 1), (1, 0)])


def at_home(rule):
    return lambda z, y, x, core: rule(z, y, x, core) if z // 2 == core else (z, y, x, 1 - core)


def near_z(z, y, x, core):
    return (z ^ 1, y, x, core)


def far_z(z, y, x, core):
    return (z ^ 2, y, x, core)


def own_axis(z, y, x, core):
    return swap_x(z, y, x, core) if core == 0 else swap_y(z, y, x, core)


def other_axis(z, y, x, core):
    return swap_y(z, y, x, core) if core == 0 else swap_x(z, y, x, core)


def scatter_first(z, y, x, core):
    return (z ^ 1, y, x, 1 - core) if z // 2 == core else (z ^ 2, y, x, core)


def scatter_second(z, y, x, core):
    return (z, y, x, 1 - core) if z // 2 == core else (z ^ 3, y, x, core)


def scatter_first(z, y, x, core):
    return (z ^ 1, y, x, 1 - core) if z // 2 == core else (z ^ 2, y, x, core)


def scatter_second(z, y, x, core):
    return (z, y, x, 1 - core) if z // 2 == core else (z ^ 3, y, x, core)


def dot_nt(a, b):
    return lax.dot_general(a, b, (((1,), (1,)), ((), ())), preferred_element_type=jnp.float32)


def dot_nn(a, b):
    return jnp.dot(a, b, preferred_element_type=jnp.float32)


def rope_table(order):
    per_axis = HD // 16
    shape = (4 * per_axis, order.shape[1])
    row = lax.broadcasted_iota(jnp.int32, shape, 0)
    axis_of, step = row // per_axis, row % per_axis
    coords = jnp.where(
        axis_of == 0,
        order % 8,
        jnp.where(axis_of == 1, order // 8 % 8, jnp.where(axis_of == 2, order // 64 % 4, order // 256)),
    )
    frequency = jnp.zeros(shape, jnp.float32)
    for i in range(per_axis):
        frequency = jnp.where(step == i, jnp.float32(100.0 ** (-i / per_axis)), frequency)
    angle = coords.astype(jnp.float32) * frequency
    return jnp.cos(angle), jnp.sin(angle)


def rotate_rows(x, cos, sin):
    quarter = HD // 4
    f, g, rest = x[0:quarter], x[quarter : 2 * quarter], x[2 * quarter :]
    return jnp.concatenate([f * cos - g * sin, g * cos + f * sin, rest], axis=0).astype(jnp.bfloat16)


def place():
    dp = lax.axis_index("dp")
    return lax.axis_index("ctx"), dp // 4, dp // 2 % 2, dp % 2


def block_bias(pattern, core, bias):
    blocks = bias.shape[0]
    lane_block = lax.broadcasted_iota(jnp.int32, (1, bias.shape[1]), 1) // BLK
    for key_local in range(blocks):
        key_block = (key_local + 2 * core) % blocks
        row = jnp.full(lane_block.shape, -jnp.inf, jnp.float32)
        for query_local in range(blocks):
            query_block = (query_local + 2 * core) % blocks
            listed = jnp.int32(0)
            for slot in range(KB):
                listed = listed + jnp.where(pattern[0, query_block, slot] == key_block, 1, 0)
            row = jnp.where((lane_block == query_local) & (listed > 0), 0.0, row)
        bias[key_local : key_local + 1, :] = row


def scaled_scores(keys, queries_t, bias):
    scores = dot_nn(keys, queries_t) * (math.log2(math.e) / math.sqrt(HD))
    parts = [scores[b * BLK : (b + 1) * BLK, :] + bias[b : b + 1, :] for b in range(bias.shape[0])]
    return jnp.concatenate(parts, axis=0)


def pack_kernel(*refs):
    order, *inputs = refs[:4]
    out, own, sems = refs[-3:]
    rows, mine = own.shape[1:]
    copies = []
    for target, core in ((out, 1 - place()[0]), (own, place()[0])):
        there = pl.ds(pl.multiple_of(core * mine, mine), mine)
        for i, a in enumerate(inputs):
            copies.append(
                pltpu.make_async_copy(a.at[:, there], target.at[i, 0:rows, :], sems.at[len(copies)])
            )
            copies[-1].start()
    digits = jnp.concatenate([order[...] // 16, order[...] % 16] + [jnp.zeros_like(order)] * 14, axis=0)
    out[0, rows:, 0:rows] = digits.astype(jnp.float32).astype(jnp.bfloat16)
    for copy in copies:
        copy.wait()


def forward_kernel(pattern, near, own, received, *refs):
    rot_q, rot_k, rot_kt, values, attn, attn_t, lse, bias, cos_ref, sin_ref = refs[-10:]
    tokens = 2 * own.shape[1]
    step = BLK
    core, z, _, _ = place()
    block_bias(pattern, core, bias)
    rows = own.shape[1]
    digits = received[0, rows:, 0:rows].astype(jnp.float32).astype(jnp.int32)
    far = digits[0:1, :] * 16 + digits[1:2, :]
    cos, sin = rope_table(jnp.concatenate([near[...], far], axis=1))
    cos_ref[...] = cos
    sin_ref[...] = sin
    for head in range(rot_q.shape[0] // HD):
        cols = slice(head * HD, (head + 1) * HD)
        taken = (head // 2 ^ z % 2) * 2 + head % 2
        taken = pl.ds(pl.multiple_of(taken * HD, HD), HD)
        query, key, value = (
            jnp.concatenate([own[i, :, taken], received[i, 0:rows, taken]], axis=0) for i in range(3)
        )
        rot_q[cols, :] = rotate_rows(query.T.astype(jnp.float32), cos, sin)
        keys_t = rotate_rows(key.T.astype(jnp.float32), cos, sin)
        rot_kt[cols, :] = keys_t
        keys = keys_t.T
        rot_k[:, cols] = keys
        values[:, cols] = value
        value_t = value.T
        for part in range(tokens // step):
            at = slice(part * step, (part + 1) * step)
            scores = scaled_scores(keys, rot_q[cols, at], bias[:, at])
            peak = jnp.max(scores, axis=0, keepdims=True)
            raised = jnp.exp2(scores - peak)
            total = jnp.sum(raised, axis=0, keepdims=True)
            mixed = dot_nn(value_t, raised.astype(jnp.bfloat16)) * (1.0 / total)
            mixed = mixed.astype(jnp.bfloat16)
            attn_t[cols, at] = mixed
            attn[at, cols] = mixed.T
            lse[head : head + 1, at] = peak + jnp.log2(total)


def weight_grad_kernel(attn_t, own, other, *refs, chunk):
    send, keep = refs[-2:]
    core, _, y, x = place()
    piece, width = send.shape[2:]
    cols = slice(chunk * width, (chunk + 1) * width)
    tokens = jnp.concatenate([own[:, cols], other[:, cols]], axis=0)
    for block in range(attn_t.shape[0] // (2 * piece)):
        rows = slice(block * 2 * piece, (block + 1) * 2 * piece)
        part = dot_nn(attn_t[rows, :], tokens).astype(send.dtype)
        z_rel = block // 2
        for head_x in range(2):
            out = part[head_x * piece : (head_x + 1) * piece, :]
            first = jnp.where(core == 0, head_x ^ x, (block % 2) ^ y)
            sub = jnp.where(core == 0, (block % 2) ^ y, head_x ^ x)

            @pl.when(first == 1)
            def _():
                send[sub, z_rel] = out

            @pl.when(first == 0)
            def _():
                keep[sub, z_rel] = out


def attn_grad_kernel(attn_t, own, other, near, far, *refs, pair):
    grad_t, dots, weight = refs[-3:]
    core, _, y, x = place()
    piece = near.shape[1]
    for e3, ref in enumerate((near, far)):
        for e2 in range(2):
            y_at = jnp.where(core == 0, y ^ e2, y ^ e3)
            x_at = jnp.where(core == 0, x ^ e3, x ^ e2)
            start = (y_at * 2 + x_at) * piece
            weight[pl.ds(pl.multiple_of(start, piece), piece), :] = ref[e2]
    size = weight.shape[0]
    tokens = jnp.concatenate([own[...], other[...]], axis=0)
    rounded = dot_nt(weight[...], tokens).astype(grad_t.dtype)
    grad_t[...] = rounded
    product = rounded.astype(jnp.float32) * attn_t[pair * size : (pair + 1) * size, :].astype(jnp.float32)
    for head in range(size // HD):
        dots[head : head + 1, :] = jnp.sum(product[head * HD : (head + 1) * HD], axis=0, keepdims=True)


def projection_kernel(attn, low, high, *refs):
    out_send, out_own = refs[-2:]
    half = out_own.shape[0]
    for c in range(low.shape[1] // half):
        cols = slice(c * half, (c + 1) * half)
        part = dot_nn(attn[...], jnp.concatenate([low[:, cols], high[:, cols]], axis=0))
        out_send[:, cols] = part[half:].astype(out_send.dtype)
        out_own[:, cols] = part[:half]


def backward_kernel(rot_q, rot_k, rot_kt, values, grad_t, dots, lse, bias, cos_ref, sin_ref, *refs, pair):
    send, own = refs[-2:]
    tokens = rot_k.shape[0]
    half = tokens // 2
    step = 2 * BLK
    scale = 1.0 / math.sqrt(HD)
    cos, sin = cos_ref[...], -sin_ref[...]
    for at_head in range(2):
        head = pair * 2 + at_head
        cols = slice(head * HD, (head + 1) * HD)
        out_cols = slice(at_head * HD, (at_head + 1) * HD)
        keys, keys_t, value = rot_k[:, cols], rot_kt[cols, :], values[:, cols]
        key_sum = jnp.zeros((HD, tokens), jnp.float32)
        value_sum = jnp.zeros((HD, tokens), jnp.float32)
        query_parts = []
        for part in range(tokens // step):
            at = slice(part * step, (part + 1) * step)
            queries_t, grads_t = rot_q[cols, at], grad_t[out_cols, at]
            scores = scaled_scores(keys, queries_t, bias[:, at])
            exact = jnp.exp2(scores - lse[head : head + 1, at])
            prob_grad = dot_nn(value, grads_t)
            score_grad = (exact * (prob_grad - dots[at_head : at_head + 1, at])).astype(jnp.bfloat16)
            value_sum = value_sum + dot_nt(grads_t, exact.astype(jnp.bfloat16))
            key_sum = key_sum + dot_nt(queries_t, score_grad)
            query_parts.append(dot_nn(keys_t, score_grad))
        query_sum = jnp.concatenate(query_parts, axis=1)
        outs = (
            rotate_rows(query_sum * scale, cos, sin),
            rotate_rows(key_sum * scale, cos, sin),
            value_sum.astype(jnp.bfloat16),
        )
        for i, out in enumerate(outs):
            out = out.T
            own[i, :, out_cols] = out[0:half, :]
            send[i, :, out_cols] = out[half:, :]


def gather_pick_kernel(home0, home1, away0, away1, *refs):
    core, z, _, _ = place()
    low = refs[-1]

    @pl.when(z // 2 == core)
    def _():
        low[0] = home0[...]
        low[1] = home1[...]

    @pl.when(z // 2 != core)
    def _():
        low[0] = away0[...]
        low[1] = away1[...]


def copy_kernel(a, *refs):
    refs[-1][...] = a[...]


def second_sum_kernel(keep, got, *refs):
    send, kept = refs[-2:]
    send[...] = (keep[1].astype(jnp.float32) + got[1].astype(jnp.float32)).astype(send.dtype)
    kept[...] = keep[0].astype(jnp.float32) + got[0].astype(jnp.float32)


def z_sum_kernel(kept, got, *refs):
    to_first, to_second, own = refs[-3:]
    core, z, _, _ = place()
    at_home = z // 2 == core
    near = kept[0] + got[0].astype(jnp.float32)
    rest = kept[1] + got[1].astype(jnp.float32)
    own[...] = near
    to_first[...] = jnp.where(at_home, rest, near).astype(to_first.dtype)
    to_second[...] = rest.astype(to_second.dtype)


def share_kernel(own, first, second, *refs):
    core, z, _, _ = place()
    at_home = z // 2 == core
    total = own[...] + first[...].astype(jnp.float32) + second[...].astype(jnp.float32)
    refs[-1][...] = jnp.where(at_home, total, first[...].astype(jnp.float32))


def finish_kernel(*refs, count):
    layer_out, *grads, mean = refs[-5:]
    out_own, out_got = refs[:2]
    pairs, shares = refs[2:6], refs[6:-5]
    core, z, _, _ = place()
    mine = grads[0].shape[1] // 2
    width = mine // 2
    for pair in range(2):
        for source in range(2):
            start = (core ^ source) * mine + (z % 2 ^ pair) * width
            cols = pl.ds(pl.multiple_of(start, width), width)
            for i in range(3):
                grads[i][:, cols] = pairs[2 * pair + source][i]
    layer_out[...] = (out_own[...] + out_got[...].astype(jnp.float32)).astype(layer_out.dtype)
    width = shares[0].shape[1]
    for i in range(mean.shape[1] // width):
        mean[:, i * width : (i + 1) * width] = (shares[2 * i][...] + shares[2 * i + 1][...]) * (1.0 / count)


def chip_shards(queries, key_states, value_states, token_order, block_pattern, out_weight, out_grad):
    rows, width = queries.shape[1:]
    model = out_grad.shape[2]
    tokens, mine = 2 * rows, width // 2
    owned = out_weight.shape[0]
    bf16, f32 = jnp.bfloat16, jnp.float32
    in_vmem = pl.BlockSpec(memory_space=pltpu.VMEM)
    in_smem = pl.BlockSpec(memory_space=pltpu.SMEM)
    in_hbm = pl.BlockSpec(memory_space=pltpu.HBM)
    anywhere = pl.BlockSpec(memory_space=pl.ANY)
    done = []

    def call(kernel, name, args, outs, scratch=(), limit=8, specs=None, final=False):
        before = [a for a in done if not any(a is b for b in args)]
        results = pl.pallas_call(
            kernel,
            in_specs=list(specs or [in_vmem] * len(args)) + [anywhere] * len(before),
            out_specs=[in_vmem] * len(outs),
            out_shape=[jax.ShapeDtypeStruct(s, d) for s, d in outs],
            scratch_shapes=scratch,
            compiler_params=pltpu.CompilerParams(vmem_limit_bytes=limit << 20),
            cost_estimate=pl.CostEstimate(flops=10000000000, bytes_accessed=1, transcendentals=0),
            name=name,
        )(*args, *before)
        if not final:
            done[:] = results[:1]
        return results

    q_own, k_own, v_own, dy_own = queries[0], key_states[0], value_states[0], out_grad[0]
    q_in, k_in, v_in = (pltpu.with_memory_space_constraint(a, pltpu.HBM) for a in (q_own, k_own, v_own))
    pack, own = call(
        pack_kernel,
        "pack",
        (token_order, q_in, k_in, v_in),
        [((3, rows + 16, mine), bf16), ((3, rows, mine), bf16)],
        specs=[in_vmem] + [in_hbm] * 3,
        scratch=[pltpu.SemaphoreType.DMA((6,))],
        final=True,
    )
    received = swap_core(pack)
    dy_far = swap_core(dy_own)

    beyond = move(out_weight, at_home(far_z))
    beside = move(out_weight, other_axis)
    chunks = 2
    forward_results = []

    def forward():
        forward_results[:] = call(
            forward_kernel,
            "forward",
            (block_pattern, token_order, own, received),
            [((mine, tokens), bf16), ((tokens, mine), bf16), ((mine, tokens), bf16)]
            + [((tokens, mine), bf16)] * 2
            + [((mine, tokens), bf16), ((mine // HD, tokens), f32), ((tokens // BLK, tokens), f32)]
            + [((HD // 4, tokens), f32)] * 2,
            limit=24,
            specs=[in_smem] + [in_vmem] * 3,
        )

    sums = SUM_CHUNKS
    cols = model // sums
    weights, attn_grads, pairs = ([None] * chunks for _ in range(3))
    parts, z_sums, shares = [None] * sums, [None] * sums, [None] * sums
    result = {}

    def weight_grad(i):
        send, keep = call(
            functools.partial(weight_grad_kernel, chunk=i),
            "weight_grad",
            (forward_results[5], dy_own, dy_far),
            [((2, 2, owned, cols), bf16)] * 2,
            limit=16,
        )
        parts[i] = (keep, move(send, own_axis))

    def gather_beside():
        (copied,) = call(copy_kernel, "copy", (beside,), [((owned, model), bf16)])
        result["beside"] = move(copied, at_home(far_z))

    def gather_pick():
        args = (out_weight, beside, beyond, result["beside"])
        (low,) = call(gather_pick_kernel, "gather_pick", args, [((2, owned, model), bf16)])
        result["high"] = move(low, near_z)
        weights[0] = low, move(low, own_axis)

    def gather_last():
        (high,) = call(copy_kernel, "copy", (result["high"],), [((2, owned, model), bf16)])
        weights[1] = high, move(high, own_axis)

    def second_sum(i):
        send, kept = call(
            second_sum_kernel,
            "second_sum",
            parts[i],
            [((2, owned, cols), bf16), ((2, owned, cols), f32)],
        )
        parts[i] = (kept, move(send, other_axis))

    def z_sum(i):
        to_first, to_second, own = call(
            z_sum_kernel,
            "z_sum",
            parts[i],
            [((owned, cols), bf16)] * 2 + [((owned, cols), f32)],
        )
        z_sums[i] = own, move(to_first, scatter_first), move(to_second, scatter_second)

    def share(i):
        (part,) = call(share_kernel, "share", z_sums[i], [((owned, cols), f32)])
        shares[i] = part, swap_core(part)

    def attn_grad(i):
        attn_grads[i] = call(
            functools.partial(attn_grad_kernel, pair=i),
            "attn_grad",
            (forward_results[5], dy_own, dy_far, *weights[i]),
            [((2 * HD, tokens), bf16), ((2, tokens), f32), ((2 * HD, model), bf16)],
            limit=16,
        )

    def projection():
        out_send, out_own = call(
            projection_kernel,
            "projection",
            (forward_results[4], attn_grads[0][2], attn_grads[1][2]),
            [((rows, model), bf16), ((rows, model), f32)],
            limit=16,
        )
        result["out"] = (out_own, swap_core(out_send))

    def backward(i):
        send, own = call(
            functools.partial(backward_kernel, pair=i),
            "backward",
            (*forward_results[:4], *attn_grads[i][:2], *forward_results[6:]),
            [((3, rows, 2 * HD), bf16)] * 2,
            limit=24,
        )
        pairs[i] = own, swap_core(send)

    def finish():
        args = (*result["out"], *pairs[0], *pairs[1], *(a for s in shares for a in s))
        result["all"] = call(
            functools.partial(finish_kernel, count=lax.axis_size("dp")),
            "finish",
            args,
            [((rows, model), bf16)] + [((rows, width), bf16)] * 3 + [((owned, model), f32)],
            limit=24,
            final=True,
        )

    forward()
    weight_grad(0)
    gather_beside()
    weight_grad(1)
    gather_pick()
    second_sum(0)
    second_sum(1)
    z_sum(0)
    gather_last()
    z_sum(1)
    attn_grad(0)
    backward(0)
    share(0)
    attn_grad(1)
    projection()
    backward(1)
    share(1)
    finish()
    *sharded, weight_grad = result["all"]
    return (*[a[None] for a in sharded], weight_grad)


def solution(mesh):
    in_specs = (
        P("dp", "ctx", None),
        P("dp", "ctx", None),
        P("dp", "ctx", None),
        P("dp", "ctx"),
        P("dp", None, None),
        P("dp", None),
        P("dp", "ctx", None),
    )
    out_specs = (
        P("dp", "ctx", None),
        P("dp", "ctx", None),
        P("dp", "ctx", None),
        P("dp", "ctx", None),
        P("dp", None),
    )
    body = chip_shards if (mesh.shape["dp"], mesh.shape["ctx"]) == (16, 2) else shards
    return jax.shard_map(body, mesh=mesh, in_specs=in_specs, out_specs=out_specs, check_vma=False)
```

```python
import functools
import itertools
import math

import jax
import jax.numpy as jnp
import numpy as np
from jax import lax
from jax.experimental import pallas as pl
from jax.experimental.pallas import tpu as pltpu
from jax.sharding import PartitionSpec as P

H = 8
HD = 128
BLK = 128
KB = 4
SUM_CHUNKS = 2
KERNEL_COST = 10**10


def padded(shard, sides, width):
    for axis, dim in sides:
        devices, length = (lax.axis_size(axis), shard.shape[dim])
        up = [(i, (i + 1) % devices) for i in range(devices - 1)]
        down = [(j, i) for i, j in up]
        last = lax.slice_in_dim(shard, length - width, length, axis=dim)
        leading = lax.slice_in_dim(shard, 0, width, axis=dim)
        before = lax.ppermute(last, axis, up)
        after = lax.ppermute(leading, axis, down)
        shard = jnp.concatenate([before, shard, after], axis=dim)
    return shard


def from_behind(block, axis, distance):
    devices = range(lax.axis_size(axis))
    route = [(i - distance, i) for i in devices if i - distance in devices]
    return lax.ppermute(block, axis, route)


def rope_tables(positions):
    coords = jnp.stack(
        [positions % 8, positions // 8 % 8, positions // 64 % 4, positions // 256], axis=1
    ).astype(jnp.float32)
    per_axis = HD // 16
    frequency = 100.0 ** (-jnp.arange(per_axis, dtype=jnp.float32) / per_axis)
    angle = (coords[:, :, None] * frequency[None, None, :]).reshape(
        positions.shape[0], 4 * per_axis
    )
    return (jnp.cos(angle), jnp.sin(angle))


def rotate_heads(heads, cosine, sine_vals, direction):
    quarter = HD // 4
    first_part = heads[..., :quarter]
    second_part = heads[..., quarter : 2 * quarter]
    cos_rows = cosine[:, None, :]
    sin_rows = direction * sine_vals[:, None, :]
    return jnp.concatenate(
        [
            first_part * cos_rows - second_part * sin_rows,
            second_part * cos_rows + first_part * sin_rows,
            heads[..., 2 * quarter :],
        ],
        axis=-1,
    )


def attend_forward(query_blocks, key_sets, value_sets, key_mask, score_scale):
    scores = (
        jnp.einsum("nqhd,nkhd->nhqk", query_blocks, key_sets, preferred_element_type=jnp.float32)
        * score_scale
    )
    scores = jnp.where(key_mask[:, None, None, :], scores, -jnp.inf)
    row_peak = jnp.max(scores, axis=-1)
    row_total = jnp.sum(jnp.exp(scores - row_peak[..., None]), axis=-1)
    log_total = row_peak + jnp.log(row_total)
    soft_probs = jnp.exp(scores - log_total[..., None]).astype(jnp.bfloat16)
    block_out = jnp.einsum(
        "nhqk,nkhd->nqhd", soft_probs, value_sets, preferred_element_type=jnp.float32
    ).astype(jnp.bfloat16)
    return (block_out, log_total)


def attend_backward(
    query_blocks,
    key_sets,
    value_sets,
    key_mask,
    log_total,
    grad_dot,
    grad_blocks,
    score_scale,
    key_form,
):
    scores = (
        jnp.einsum(
            "nqhd," + key_form + "->nhqk",
            query_blocks,
            key_sets,
            preferred_element_type=jnp.float32,
        )
        * score_scale
    )
    scores = jnp.where(key_mask[:, None, None, :], scores, -jnp.inf)
    exact_probs = jnp.exp(scores - log_total[..., None])
    soft_probs = exact_probs.astype(jnp.bfloat16)
    value_part = jnp.einsum(
        "nhqk,nqhd->" + key_form, soft_probs, grad_blocks, preferred_element_type=jnp.float32
    )
    prob_grad = jnp.einsum(
        "nqhd," + key_form + "->nhqk", grad_blocks, value_sets, preferred_element_type=jnp.float32
    )
    score_grad = (exact_probs * (prob_grad - grad_dot[..., None]) * score_scale).astype(
        jnp.bfloat16
    )
    query_part = jnp.einsum(
        "nhqk," + key_form + "->nqhd", score_grad, key_sets, preferred_element_type=jnp.float32
    )
    key_part = jnp.einsum(
        "nhqk,nqhd->" + key_form, score_grad, query_blocks, preferred_element_type=jnp.float32
    )
    return (query_part, key_part, value_part)


def shards(queries, key_states, value_states, token_order, block_pattern, out_weight, out_grad):
    row_count = queries.shape[1]
    feature_width = queries.shape[2]
    local_blocks = row_count // BLK
    shard_index = lax.axis_index("ctx")
    score_scale = 1.0 / math.sqrt(HD)
    cosine, sine_vals = rope_tables(token_order[0])
    rot_query = rotate_heads(
        queries[0].astype(jnp.float32).reshape(row_count, H, HD), cosine, sine_vals, 1.0
    ).astype(jnp.bfloat16)
    rot_keys = rotate_heads(
        key_states[0].astype(jnp.float32).reshape(row_count, H, HD), cosine, sine_vals, 1.0
    ).astype(jnp.bfloat16)
    stacked = jnp.stack([rot_keys.reshape(row_count, feature_width), value_states[0]], axis=1)
    extended = padded(stacked, (("ctx", 0),), row_count)
    ext_blocks = extended.reshape(3 * local_blocks, BLK, 2, H, HD)
    pattern_rows = block_pattern[0]
    first_block = shard_index * local_blocks
    my_pattern = lax.dynamic_slice_in_dim(pattern_rows, first_block, local_blocks, 0)
    slot_valid = my_pattern >= 0
    slot_local = jnp.where(slot_valid, my_pattern - first_block + local_blocks, 0)
    gathered = jnp.take(ext_blocks, slot_local, axis=0)
    key_sets = gathered[:, :, :, 0].reshape(local_blocks, KB * BLK, H, HD)
    value_sets = gathered[:, :, :, 1].reshape(local_blocks, KB * BLK, H, HD)
    key_mask = jnp.repeat(slot_valid, BLK, axis=1)
    query_blocks = rot_query.reshape(local_blocks, BLK, H, HD)
    block_out, log_total = attend_forward(query_blocks, key_sets, value_sets, key_mask, score_scale)
    attn = block_out.reshape(row_count, feature_width)
    grad_rows = out_grad[0]
    forward_weight = lax.all_gather(out_weight, "dp", axis=0, tiled=True)
    layer_out = jnp.dot(attn, forward_weight, preferred_element_type=jnp.float32).astype(
        jnp.bfloat16
    )
    attn_grad = lax.dot_general(
        grad_rows,
        lax.all_gather(out_weight, "dp", axis=0, tiled=True),
        (((1,), (1,)), ((), ())),
        preferred_element_type=jnp.float32,
    ).astype(jnp.bfloat16)
    batch_count = lax.axis_size("dp")
    local_grad = lax.psum_scatter(
        lax.dot_general(
            attn, grad_rows, (((0,), (0,)), ((), ())), preferred_element_type=jnp.float32
        )
        / batch_count,
        "dp",
        scatter_dimension=0,
        tiled=True,
    )
    weight_grad = lax.psum(local_grad, "ctx")
    dot_rows = jnp.sum(
        (attn_grad.astype(jnp.float32) * attn.astype(jnp.float32)).reshape(row_count, H, HD),
        axis=-1,
    )
    grad_dot = dot_rows.reshape(local_blocks, BLK, H).transpose(0, 2, 1)
    grad_blocks = attn_grad.reshape(local_blocks, BLK, H, HD)
    query_part, key_part, value_part = attend_backward(
        query_blocks,
        key_sets,
        value_sets,
        key_mask,
        log_total,
        grad_dot,
        grad_blocks,
        score_scale,
        "nkhd",
    )
    query_grad = (
        rotate_heads(query_part.reshape(row_count, H, HD), cosine, sine_vals, -1.0)
        .reshape(row_count, feature_width)
        .astype(jnp.bfloat16)
    )
    keep = slot_valid.reshape(local_blocks * KB).astype(jnp.float32)[:, None, None, None, None]
    both_parts = (
        jnp.stack(
            [
                key_part.reshape(local_blocks * KB, BLK, H, HD),
                value_part.reshape(local_blocks * KB, BLK, H, HD),
            ],
            axis=2,
        )
        * keep
    )
    accumulated = (
        jnp.zeros((3 * local_blocks, BLK, 2, H, HD), jnp.float32)
        .at[slot_local.reshape(-1)]
        .add(both_parts)
    )
    accumulated = accumulated.reshape(3 * row_count, 2, feature_width)
    own_part = accumulated[row_count : 2 * row_count]
    from_right = from_behind(accumulated[:row_count], "ctx", -1)
    from_left = from_behind(accumulated[2 * row_count :], "ctx", 1)
    summed = own_part + from_right + from_left
    key_total = summed[:, 0]
    value_total = summed[:, 1]
    key_grad = (
        rotate_heads(key_total.reshape(row_count, H, HD), cosine, sine_vals, -1.0)
        .reshape(row_count, feature_width)
        .astype(jnp.bfloat16)
    )
    value_grad = value_total.astype(jnp.bfloat16)
    return (layer_out[None], query_grad[None], key_grad[None], value_grad[None], weight_grad)

def chip_moves(rule):
    pairs = []
    for z, y, x, core in itertools.product(range(4), range(2), range(2), range(2)):
        target = rule(z, y, x, core)
        if target is not None:
            tz, ty, tx, tcore = target
            pairs.append((((z * 2 + y) * 2 + x) * 2 + core, ((tz * 2 + ty) * 2 + tx) * 2 + tcore))
    return pairs


def swap_x(z, y, x, core):
    return (z, y, 1 - x, core)


def swap_y(z, y, x, core):
    return (z, 1 - y, x, core)


def move(array, rule):
    return lax.ppermute(array, ("dp", "ctx"), chip_moves(rule))


def swap_core(array):
    return lax.ppermute(array, "ctx", [(0, 1), (1, 0)])


def at_home(rule):
    return lambda z, y, x, core: rule(z, y, x, core) if z // 2 == core else (z, y, x, 1 - core)


def near_z(z, y, x, core):
    return (z ^ 1, y, x, core)


def far_z(z, y, x, core):
    return (z ^ 2, y, x, core)


def own_axis(z, y, x, core):
    return swap_x(z, y, x, core) if core == 0 else swap_y(z, y, x, core)


def other_axis(z, y, x, core):
    return swap_y(z, y, x, core) if core == 0 else swap_x(z, y, x, core)


def scatter_first(z, y, x, core):
    return (z ^ 1, y, x, 1 - core) if z // 2 == core else (z ^ 2, y, x, core)


def scatter_second(z, y, x, core):
    return (z, y, x, 1 - core) if z // 2 == core else (z ^ 3, y, x, core)


def scatter_first(z, y, x, core):
    return (z ^ 1, y, x, 1 - core) if z // 2 == core else (z ^ 2, y, x, core)


def scatter_second(z, y, x, core):
    return (z, y, x, 1 - core) if z // 2 == core else (z ^ 3, y, x, core)


def dot_nt(a, b):
    return lax.dot_general(a, b, (((1,), (1,)), ((), ())), preferred_element_type=jnp.float32)


def dot_nn(a, b):
    return jnp.dot(a, b, preferred_element_type=jnp.float32)


def rope_table(order):
    per_axis = HD // 16
    shape = (4 * per_axis, order.shape[1])
    row = lax.broadcasted_iota(jnp.int32, shape, 0)
    axis_of, step = row // per_axis, row % per_axis
    coords = jnp.where(
        axis_of == 0,
        order % 8,
        jnp.where(axis_of == 1, order // 8 % 8, jnp.where(axis_of == 2, order // 64 % 4, order // 256)),
    )
    frequency = jnp.zeros(shape, jnp.float32)
    for i in range(per_axis):
        frequency = jnp.where(step == i, jnp.float32(100.0 ** (-i / per_axis)), frequency)
    angle = coords.astype(jnp.float32) * frequency
    return jnp.cos(angle), jnp.sin(angle)


def rotate_rows(x, cos, sin):
    quarter = HD // 4
    f, g, rest = x[0:quarter], x[quarter : 2 * quarter], x[2 * quarter :]
    return jnp.concatenate([f * cos - g * sin, g * cos + f * sin, rest], axis=0).astype(jnp.bfloat16)


def place():
    dp = lax.axis_index("dp")
    return lax.axis_index("ctx"), dp // 4, dp // 2 % 2, dp % 2


def block_bias(pattern, core, bias):
    blocks = bias.shape[0]
    lane_block = lax.broadcasted_iota(jnp.int32, (1, bias.shape[1]), 1) // BLK
    for key_local in range(blocks):
        key_block = (key_local + 2 * core) % blocks
        row = jnp.full(lane_block.shape, -jnp.inf, jnp.float32)
        for query_local in range(blocks):
            query_block = (query_local + 2 * core) % blocks
            listed = jnp.int32(0)
            for slot in range(KB):
                listed = listed + jnp.where(pattern[0, query_block, slot] == key_block, 1, 0)
            row = jnp.where((lane_block == query_local) & (listed > 0), 0.0, row)
        bias[key_local : key_local + 1, :] = row


def scaled_scores(keys, queries_t, bias):
    scores = dot_nn(keys, queries_t) * (math.log2(math.e) / math.sqrt(HD))
    parts = [scores[b * BLK : (b + 1) * BLK, :] + bias[b : b + 1, :] for b in range(bias.shape[0])]
    return jnp.concatenate(parts, axis=0)


def pack_kernel(*refs):
    order, *inputs = refs[:4]
    out, own, sems = refs[-3:]
    rows, mine = own.shape[1:]
    copies = []
    for target, core in ((out, 1 - place()[0]), (own, place()[0])):
        there = pl.ds(pl.multiple_of(core * mine, mine), mine)
        for i, a in enumerate(inputs):
            copies.append(
                pltpu.make_async_copy(a.at[:, there], target.at[i, 0:rows, :], sems.at[len(copies)])
            )
            copies[-1].start()
    digits = jnp.concatenate([order[...] // 16, order[...] % 16] + [jnp.zeros_like(order)] * 14, axis=0)
    out[0, rows:, 0:rows] = digits.astype(jnp.float32).astype(jnp.bfloat16)
    for copy in copies:
        copy.wait()


def forward_kernel(pattern, near, own, received, *refs):
    rot_q, rot_k, rot_kt, values, attn, attn_t, lse, bias, cos_ref, sin_ref = refs[-10:]
    tokens = 2 * own.shape[1]
    step = BLK
    core, z, _, _ = place()
    block_bias(pattern, core, bias)
    rows = own.shape[1]
    digits = received[0, rows:, 0:rows].astype(jnp.float32).astype(jnp.int32)
    far = digits[0:1, :] * 16 + digits[1:2, :]
    cos, sin = rope_table(jnp.concatenate([near[...], far], axis=1))
    cos_ref[...] = cos
    sin_ref[...] = sin
    for head in range(rot_q.shape[0] // HD):
        cols = slice(head * HD, (head + 1) * HD)
        taken = (head // 2 ^ z % 2) * 2 + head % 2
        taken = pl.ds(pl.multiple_of(taken * HD, HD), HD)
        query, key, value = (
            jnp.concatenate([own[i, :, taken], received[i, 0:rows, taken]], axis=0) for i in range(3)
        )
        rot_q[cols, :] = rotate_rows(query.T.astype(jnp.float32), cos, sin)
        keys_t = rotate_rows(key.T.astype(jnp.float32), cos, sin)
        rot_kt[cols, :] = keys_t
        keys = keys_t.T
        rot_k[:, cols] = keys
        values[:, cols] = value
        value_t = value.T
        for part in range(tokens // step):
            at = slice(part * step, (part + 1) * step)
            scores = scaled_scores(keys, rot_q[cols, at], bias[:, at])
            peak = jnp.max(scores, axis=0, keepdims=True)
            raised = jnp.exp2(scores - peak)
            total = jnp.sum(raised, axis=0, keepdims=True)
            mixed = dot_nn(value_t, raised.astype(jnp.bfloat16)) * (1.0 / total)
            mixed = mixed.astype(jnp.bfloat16)
            attn_t[cols, at] = mixed
            attn[at, cols] = mixed.T
            lse[head : head + 1, at] = peak + jnp.log2(total)


def weight_grad_kernel(attn_t, own, other, *refs, chunk):
    send, keep = refs[-2:]
    core, _, y, x = place()
    piece, width = send.shape[2:]
    cols = slice(chunk * width, (chunk + 1) * width)
    tokens = jnp.concatenate([own[:, cols], other[:, cols]], axis=0)
    for block in range(attn_t.shape[0] // (2 * piece)):
        rows = slice(block * 2 * piece, (block + 1) * 2 * piece)
        part = dot_nn(attn_t[rows, :], tokens).astype(send.dtype)
        z_rel = block // 2
        for head_x in range(2):
            out = part[head_x * piece : (head_x + 1) * piece, :]
            first = jnp.where(core == 0, head_x ^ x, (block % 2) ^ y)
            sub = jnp.where(core == 0, (block % 2) ^ y, head_x ^ x)

            @pl.when(first == 1)
            def _():
                send[sub, z_rel] = out

            @pl.when(first == 0)
            def _():
                keep[sub, z_rel] = out


def attn_grad_kernel(attn_t, own, other, near, far, *refs, pair):
    grad_t, dots, weight = refs[-3:]
    core, _, y, x = place()
    piece = near.shape[1]
    for e3, ref in enumerate((near, far)):
        for e2 in range(2):
            y_at = jnp.where(core == 0, y ^ e2, y ^ e3)
            x_at = jnp.where(core == 0, x ^ e3, x ^ e2)
            start = (y_at * 2 + x_at) * piece
            weight[pl.ds(pl.multiple_of(start, piece), piece), :] = ref[e2]
    size = weight.shape[0]
    tokens = jnp.concatenate([own[...], other[...]], axis=0)
    rounded = dot_nt(weight[...], tokens).astype(grad_t.dtype)
    grad_t[...] = rounded
    product = rounded.astype(jnp.float32) * attn_t[pair * size : (pair + 1) * size, :].astype(jnp.float32)
    for head in range(size // HD):
        dots[head : head + 1, :] = jnp.sum(product[head * HD : (head + 1) * HD], axis=0, keepdims=True)


def projection_kernel(attn, low, high, *refs):
    out_send, out_own = refs[-2:]
    half = out_own.shape[0]
    for c in range(low.shape[1] // half):
        cols = slice(c * half, (c + 1) * half)
        part = dot_nn(attn[...], jnp.concatenate([low[:, cols], high[:, cols]], axis=0))
        out_send[:, cols] = part[half:].astype(out_send.dtype)
        out_own[:, cols] = part[:half]


def backward_kernel(rot_q, rot_k, rot_kt, values, grad_t, dots, lse, bias, cos_ref, sin_ref, *refs, pair):
    send, own = refs[-2:]
    tokens = rot_k.shape[0]
    half = tokens // 2
    step = 2 * BLK
    scale = 1.0 / math.sqrt(HD)
    cos, sin = cos_ref[...], -sin_ref[...]
    for at_head in range(2):
        head = pair * 2 + at_head
        cols = slice(head * HD, (head + 1) * HD)
        out_cols = slice(at_head * HD, (at_head + 1) * HD)
        keys, keys_t, value = rot_k[:, cols], rot_kt[cols, :], values[:, cols]
        key_sum = jnp.zeros((HD, tokens), jnp.float32)
        value_sum = jnp.zeros((HD, tokens), jnp.float32)
        query_parts = []
        for part in range(tokens // step):
            at = slice(part * step, (part + 1) * step)
            queries_t, grads_t = rot_q[cols, at], grad_t[out_cols, at]
            scores = scaled_scores(keys, queries_t, bias[:, at])
            exact = jnp.exp2(scores - lse[head : head + 1, at])
            prob_grad = dot_nn(value, grads_t)
            score_grad = (exact * (prob_grad - dots[at_head : at_head + 1, at])).astype(jnp.bfloat16)
            value_sum = value_sum + dot_nt(grads_t, exact.astype(jnp.bfloat16))
            key_sum = key_sum + dot_nt(queries_t, score_grad)
            query_parts.append(dot_nn(keys_t, score_grad))
        query_sum = jnp.concatenate(query_parts, axis=1)
        outs = (
            rotate_rows(query_sum * scale, cos, sin),
            rotate_rows(key_sum * scale, cos, sin),
            value_sum.astype(jnp.bfloat16),
        )
        for i, out in enumerate(outs):
            out = out.T
            own[i, :, out_cols] = out[0:half, :]
            send[i, :, out_cols] = out[half:, :]


def gather_pick_kernel(home, away, *refs):
    core, z, _, _ = place()
    low = refs[-1]

    @pl.when(z // 2 == core)
    def _():
        low[...] = home[...]

    @pl.when(z // 2 != core)
    def _():
        low[...] = away[...]


def pair_kernel(a, b, *refs):
    refs[-1][0] = a[...]
    refs[-1][1] = b[...]


def copy_kernel(a, *refs):
    refs[-1][...] = a[...]


def second_sum_kernel(keep, got, *refs):
    send, kept = refs[-2:]
    send[...] = (keep[1].astype(jnp.float32) + got[1].astype(jnp.float32)).astype(send.dtype)
    kept[...] = keep[0].astype(jnp.float32) + got[0].astype(jnp.float32)


def z_sum_kernel(kept, got, *refs):
    to_first, to_second, own = refs[-3:]
    core, z, _, _ = place()
    at_home = z // 2 == core
    near = kept[0] + got[0].astype(jnp.float32)
    rest = kept[1] + got[1].astype(jnp.float32)
    own[...] = near
    to_first[...] = jnp.where(at_home, rest, near).astype(to_first.dtype)
    to_second[...] = rest.astype(to_second.dtype)


def share_kernel(own, first, second, *refs):
    core, z, _, _ = place()
    at_home = z // 2 == core
    total = own[...] + first[...].astype(jnp.float32) + second[...].astype(jnp.float32)
    refs[-1][...] = jnp.where(at_home, total, first[...].astype(jnp.float32))


def finish_kernel(*refs, count):
    layer_out, *grads, mean, layer_rows, mean_rows, sems = refs[-8:]
    out_own, out_got = refs[:2]
    pairs, shares = refs[2:6], refs[6:-8]
    core, z, _, _ = place()
    mine = grads[0].shape[1] // 2
    width = mine // 2
    copies = []

    def send(source, target):
        copies.append(pltpu.make_async_copy(source, target, sems.at[len(copies)]))
        copies[-1].start()

    for pair in range(2):
        for source in range(2):
            start = (core ^ source) * mine + (z % 2 ^ pair) * width
            cols = pl.ds(pl.multiple_of(start, width), width)
            for i in range(3):
                send(pairs[2 * pair + source].at[i], grads[i].at[:, cols])
    parts = 2
    size = layer_rows.shape[0] // parts
    for part in range(parts):
        rows = slice(part * size, (part + 1) * size)
        total = out_own[rows, :] + out_got[rows, :].astype(jnp.float32)
        layer_rows[rows, :] = total.astype(layer_rows.dtype)
        send(layer_rows.at[rows, :], layer_out.at[rows, :])
    width = shares[0].shape[1]
    for i in range(mean.shape[1] // width):
        total = shares[2 * i][...] + shares[2 * i + 1][...]
        mean_rows[:, i * width : (i + 1) * width] = total * (1.0 / count)
    send(mean_rows, mean)
    for copy in copies:
        copy.wait()


def chip_shards(queries, key_states, value_states, token_order, block_pattern, out_weight, out_grad):
    rows, width = queries.shape[1:]
    model = out_grad.shape[2]
    tokens, mine = 2 * rows, width // 2
    owned = out_weight.shape[0]
    bf16, f32 = jnp.bfloat16, jnp.float32
    in_vmem = pl.BlockSpec(memory_space=pltpu.VMEM)
    in_smem = pl.BlockSpec(memory_space=pltpu.SMEM)
    in_hbm = pl.BlockSpec(memory_space=pltpu.HBM)
    anywhere = pl.BlockSpec(memory_space=pl.ANY)
    done = []

    def call(kernel, name, args, outs, scratch=(), limit=8, specs=None, final=False, out_space=pltpu.VMEM):
        before = [a for a in done if not any(a is b for b in args)]
        results = pl.pallas_call(
            kernel,
            in_specs=list(specs or [in_vmem] * len(args)) + [anywhere] * len(before),
            out_specs=[pl.BlockSpec(memory_space=out_space)] * len(outs),
            out_shape=[out_space(s, d) if out_space is pltpu.HBM else jax.ShapeDtypeStruct(s, d) for s, d in outs],
            scratch_shapes=scratch,
            compiler_params=pltpu.CompilerParams(vmem_limit_bytes=limit << 20),
            cost_estimate=pl.CostEstimate(flops=KERNEL_COST, bytes_accessed=1, transcendentals=0),
            name=name,
        )(*args, *before)
        if not final:
            done[:] = results[:1]
        return results

    q_own, k_own, v_own, dy_own = queries[0], key_states[0], value_states[0], out_grad[0]
    q_in, k_in, v_in = (pltpu.with_memory_space_constraint(a, pltpu.HBM) for a in (q_own, k_own, v_own))
    pack, own = call(
        pack_kernel,
        "pack",
        (token_order, q_in, k_in, v_in),
        [((3, rows + 16, mine), bf16), ((3, rows, mine), bf16)],
        specs=[in_vmem] + [in_hbm] * 3,
        scratch=[pltpu.SemaphoreType.DMA((6,))],
        final=True,
    )
    received = swap_core(pack)
    dy_far = swap_core(dy_own)

    beyond = move(out_weight, at_home(far_z))
    beside = move(out_weight, other_axis)
    chunks = 2
    forward_results = []

    def forward():
        forward_results[:] = call(
            forward_kernel,
            "forward",
            (block_pattern, token_order, own, received),
            [((mine, tokens), bf16), ((tokens, mine), bf16), ((mine, tokens), bf16)]
            + [((tokens, mine), bf16)] * 2
            + [((mine, tokens), bf16), ((mine // HD, tokens), f32), ((tokens // BLK, tokens), f32)]
            + [((HD // 4, tokens), f32)] * 2,
            limit=24,
            specs=[in_smem] + [in_vmem] * 3,
        )

    sums = SUM_CHUNKS
    cols = model // sums
    weights, attn_grads, pairs = ([None] * chunks for _ in range(3))
    parts, z_sums, shares = [None] * sums, [None] * sums, [None] * sums
    result = {}

    def weight_grad(i):
        send, keep = call(
            functools.partial(weight_grad_kernel, chunk=i),
            "weight_grad",
            (forward_results[5], dy_own, dy_far),
            [((2, 2, owned, cols), bf16)] * 2,
            limit=16,
        )
        parts[i] = (keep, move(send, own_axis))

    def gather_beside():
        (copied,) = call(copy_kernel, "copy", (beside,), [((owned, model), bf16)])
        result["beside"] = move(copied, at_home(far_z))

    def gather_pick(i):
        args = ((out_weight, beyond), (beside, result["beside"]))[i]
        (low,) = call(gather_pick_kernel, "gather_pick", args, [((owned, model), bf16)])
        result["low", i] = low, move(low, near_z)

    def gather_own(i):
        args = result["low", 0][i], result["low", 1][i]
        (pair,) = call(pair_kernel, "pair", args, [((2, owned, model), bf16)])
        weights[i] = pair, move(pair, own_axis)

    def second_sum(i):
        send, kept = call(
            second_sum_kernel,
            "second_sum",
            parts[i],
            [((2, owned, cols), bf16), ((2, owned, cols), f32)],
        )
        parts[i] = (kept, move(send, other_axis))

    def z_sum(i):
        to_first, to_second, own = call(
            z_sum_kernel,
            "z_sum",
            parts[i],
            [((owned, cols), bf16)] * 2 + [((owned, cols), f32)],
        )
        z_sums[i] = own, move(to_first, scatter_first), move(to_second, scatter_second)

    def share(i):
        (part,) = call(share_kernel, "share", z_sums[i], [((owned, cols), f32)])
        shares[i] = part, swap_core(part)

    def attn_grad(i):
        attn_grads[i] = call(
            functools.partial(attn_grad_kernel, pair=i),
            "attn_grad",
            (forward_results[5], dy_own, dy_far, *weights[i]),
            [((2 * HD, tokens), bf16), ((2, tokens), f32), ((2 * HD, model), bf16)],
            limit=16,
        )

    def projection():
        out_send, out_own = call(
            projection_kernel,
            "projection",
            (forward_results[4], attn_grads[0][2], attn_grads[1][2]),
            [((rows, model), bf16), ((rows, model), f32)],
            limit=16,
        )
        result["out"] = (out_own, swap_core(out_send))

    def backward(i):
        send, own = call(
            functools.partial(backward_kernel, pair=i),
            "backward",
            (*forward_results[:4], *attn_grads[i][:2], *forward_results[6:]),
            [((3, rows, 2 * HD), bf16)] * 2,
            limit=24,
        )
        pairs[i] = own, swap_core(send)

    def finish():
        args = (*result["out"], *pairs[0], *pairs[1], *(a for s in shares for a in s))
        result["all"] = call(
            functools.partial(finish_kernel, count=lax.axis_size("dp")),
            "finish",
            args,
            [((rows, model), bf16)] + [((rows, width), bf16)] * 3 + [((owned, model), f32)],
            scratch=[
                pltpu.VMEM((rows, model), bf16),
                pltpu.VMEM((owned, model), f32),
                pltpu.SemaphoreType.DMA((15,)),
            ],
            limit=24,
            final=True,
            out_space=pltpu.HBM,
        )

    forward()
    weight_grad(0)
    gather_beside()
    weight_grad(1)
    gather_pick(0)
    gather_pick(1)
    second_sum(0)
    gather_own(0)
    second_sum(1)
    z_sum(0)
    gather_own(1)
    z_sum(1)
    attn_grad(0)
    backward(0)
    share(0)
    attn_grad(1)
    projection()
    backward(1)
    share(1)
    finish()
    *sharded, weight_grad = result["all"]
    return (*[a[None] for a in sharded], weight_grad)


def solution(mesh):
    in_specs = (
        P("dp", "ctx", None),
        P("dp", "ctx", None),
        P("dp", "ctx", None),
        P("dp", "ctx"),
        P("dp", None, None),
        P("dp", None),
        P("dp", "ctx", None),
    )
    out_specs = (
        P("dp", "ctx", None),
        P("dp", "ctx", None),
        P("dp", "ctx", None),
        P("dp", "ctx", None),
        P("dp", None),
    )
    body = chip_shards if (mesh.shape["dp"], mesh.shape["ctx"]) == (16, 2) else shards
    return jax.shard_map(body, mesh=mesh, in_specs=in_specs, out_specs=out_specs, check_vma=False)
```

```python
import functools
import itertools
import math

import jax
import jax.numpy as jnp
import numpy as np
from jax import lax
from jax.experimental import pallas as pl
from jax.experimental.pallas import tpu as pltpu
from jax.sharding import PartitionSpec as P

H = 8
HD = 128
BLK = 128
KB = 4
SUM_CHUNKS = 2
KERNEL_COST = 10**10


def padded(shard, sides, width):
    for axis, dim in sides:
        devices, length = (lax.axis_size(axis), shard.shape[dim])
        up = [(i, (i + 1) % devices) for i in range(devices - 1)]
        down = [(j, i) for i, j in up]
        last = lax.slice_in_dim(shard, length - width, length, axis=dim)
        leading = lax.slice_in_dim(shard, 0, width, axis=dim)
        before = lax.ppermute(last, axis, up)
        after = lax.ppermute(leading, axis, down)
        shard = jnp.concatenate([before, shard, after], axis=dim)
    return shard


def from_behind(block, axis, distance):
    devices = range(lax.axis_size(axis))
    route = [(i - distance, i) for i in devices if i - distance in devices]
    return lax.ppermute(block, axis, route)


def rope_tables(positions):
    coords = jnp.stack(
        [positions % 8, positions // 8 % 8, positions // 64 % 4, positions // 256], axis=1
    ).astype(jnp.float32)
    per_axis = HD // 16
    frequency = 100.0 ** (-jnp.arange(per_axis, dtype=jnp.float32) / per_axis)
    angle = (coords[:, :, None] * frequency[None, None, :]).reshape(
        positions.shape[0], 4 * per_axis
    )
    return (jnp.cos(angle), jnp.sin(angle))


def rotate_heads(heads, cosine, sine_vals, direction):
    quarter = HD // 4
    first_part = heads[..., :quarter]
    second_part = heads[..., quarter : 2 * quarter]
    cos_rows = cosine[:, None, :]
    sin_rows = direction * sine_vals[:, None, :]
    return jnp.concatenate(
        [
            first_part * cos_rows - second_part * sin_rows,
            second_part * cos_rows + first_part * sin_rows,
            heads[..., 2 * quarter :],
        ],
        axis=-1,
    )


def attend_forward(query_blocks, key_sets, value_sets, key_mask, score_scale):
    scores = (
        jnp.einsum("nqhd,nkhd->nhqk", query_blocks, key_sets, preferred_element_type=jnp.float32)
        * score_scale
    )
    scores = jnp.where(key_mask[:, None, None, :], scores, -jnp.inf)
    row_peak = jnp.max(scores, axis=-1)
    row_total = jnp.sum(jnp.exp(scores - row_peak[..., None]), axis=-1)
    log_total = row_peak + jnp.log(row_total)
    soft_probs = jnp.exp(scores - log_total[..., None]).astype(jnp.bfloat16)
    block_out = jnp.einsum(
        "nhqk,nkhd->nqhd", soft_probs, value_sets, preferred_element_type=jnp.float32
    ).astype(jnp.bfloat16)
    return (block_out, log_total)


def attend_backward(
    query_blocks,
    key_sets,
    value_sets,
    key_mask,
    log_total,
    grad_dot,
    grad_blocks,
    score_scale,
    key_form,
):
    scores = (
        jnp.einsum(
            "nqhd," + key_form + "->nhqk",
            query_blocks,
            key_sets,
            preferred_element_type=jnp.float32,
        )
        * score_scale
    )
    scores = jnp.where(key_mask[:, None, None, :], scores, -jnp.inf)
    exact_probs = jnp.exp(scores - log_total[..., None])
    soft_probs = exact_probs.astype(jnp.bfloat16)
    value_part = jnp.einsum(
        "nhqk,nqhd->" + key_form, soft_probs, grad_blocks, preferred_element_type=jnp.float32
    )
    prob_grad = jnp.einsum(
        "nqhd," + key_form + "->nhqk", grad_blocks, value_sets, preferred_element_type=jnp.float32
    )
    score_grad = (exact_probs * (prob_grad - grad_dot[..., None]) * score_scale).astype(
        jnp.bfloat16
    )
    query_part = jnp.einsum(
        "nhqk," + key_form + "->nqhd", score_grad, key_sets, preferred_element_type=jnp.float32
    )
    key_part = jnp.einsum(
        "nhqk,nqhd->" + key_form, score_grad, query_blocks, preferred_element_type=jnp.float32
    )
    return (query_part, key_part, value_part)


def shards(queries, key_states, value_states, token_order, block_pattern, out_weight, out_grad):
    row_count = queries.shape[1]
    feature_width = queries.shape[2]
    local_blocks = row_count // BLK
    shard_index = lax.axis_index("ctx")
    score_scale = 1.0 / math.sqrt(HD)
    cosine, sine_vals = rope_tables(token_order[0])
    rot_query = rotate_heads(
        queries[0].astype(jnp.float32).reshape(row_count, H, HD), cosine, sine_vals, 1.0
    ).astype(jnp.bfloat16)
    rot_keys = rotate_heads(
        key_states[0].astype(jnp.float32).reshape(row_count, H, HD), cosine, sine_vals, 1.0
    ).astype(jnp.bfloat16)
    stacked = jnp.stack([rot_keys.reshape(row_count, feature_width), value_states[0]], axis=1)
    extended = padded(stacked, (("ctx", 0),), row_count)
    ext_blocks = extended.reshape(3 * local_blocks, BLK, 2, H, HD)
    pattern_rows = block_pattern[0]
    first_block = shard_index * local_blocks
    my_pattern = lax.dynamic_slice_in_dim(pattern_rows, first_block, local_blocks, 0)
    slot_valid = my_pattern >= 0
    slot_local = jnp.where(slot_valid, my_pattern - first_block + local_blocks, 0)
    gathered = jnp.take(ext_blocks, slot_local, axis=0)
    key_sets = gathered[:, :, :, 0].reshape(local_blocks, KB * BLK, H, HD)
    value_sets = gathered[:, :, :, 1].reshape(local_blocks, KB * BLK, H, HD)
    key_mask = jnp.repeat(slot_valid, BLK, axis=1)
    query_blocks = rot_query.reshape(local_blocks, BLK, H, HD)
    block_out, log_total = attend_forward(query_blocks, key_sets, value_sets, key_mask, score_scale)
    attn = block_out.reshape(row_count, feature_width)
    grad_rows = out_grad[0]
    forward_weight = lax.all_gather(out_weight, "dp", axis=0, tiled=True)
    layer_out = jnp.dot(attn, forward_weight, preferred_element_type=jnp.float32).astype(
        jnp.bfloat16
    )
    attn_grad = lax.dot_general(
        grad_rows,
        lax.all_gather(out_weight, "dp", axis=0, tiled=True),
        (((1,), (1,)), ((), ())),
        preferred_element_type=jnp.float32,
    ).astype(jnp.bfloat16)
    batch_count = lax.axis_size("dp")
    local_grad = lax.psum_scatter(
        lax.dot_general(
            attn, grad_rows, (((0,), (0,)), ((), ())), preferred_element_type=jnp.float32
        )
        / batch_count,
        "dp",
        scatter_dimension=0,
        tiled=True,
    )
    weight_grad = lax.psum(local_grad, "ctx")
    dot_rows = jnp.sum(
        (attn_grad.astype(jnp.float32) * attn.astype(jnp.float32)).reshape(row_count, H, HD),
        axis=-1,
    )
    grad_dot = dot_rows.reshape(local_blocks, BLK, H).transpose(0, 2, 1)
    grad_blocks = attn_grad.reshape(local_blocks, BLK, H, HD)
    query_part, key_part, value_part = attend_backward(
        query_blocks,
        key_sets,
        value_sets,
        key_mask,
        log_total,
        grad_dot,
        grad_blocks,
        score_scale,
        "nkhd",
    )
    query_grad = (
        rotate_heads(query_part.reshape(row_count, H, HD), cosine, sine_vals, -1.0)
        .reshape(row_count, feature_width)
        .astype(jnp.bfloat16)
    )
    keep = slot_valid.reshape(local_blocks * KB).astype(jnp.float32)[:, None, None, None, None]
    both_parts = (
        jnp.stack(
            [
                key_part.reshape(local_blocks * KB, BLK, H, HD),
                value_part.reshape(local_blocks * KB, BLK, H, HD),
            ],
            axis=2,
        )
        * keep
    )
    accumulated = (
        jnp.zeros((3 * local_blocks, BLK, 2, H, HD), jnp.float32)
        .at[slot_local.reshape(-1)]
        .add(both_parts)
    )
    accumulated = accumulated.reshape(3 * row_count, 2, feature_width)
    own_part = accumulated[row_count : 2 * row_count]
    from_right = from_behind(accumulated[:row_count], "ctx", -1)
    from_left = from_behind(accumulated[2 * row_count :], "ctx", 1)
    summed = own_part + from_right + from_left
    key_total = summed[:, 0]
    value_total = summed[:, 1]
    key_grad = (
        rotate_heads(key_total.reshape(row_count, H, HD), cosine, sine_vals, -1.0)
        .reshape(row_count, feature_width)
        .astype(jnp.bfloat16)
    )
    value_grad = value_total.astype(jnp.bfloat16)
    return (layer_out[None], query_grad[None], key_grad[None], value_grad[None], weight_grad)

def chip_moves(rule):
    pairs = []
    for z, y, x, core in itertools.product(range(4), range(2), range(2), range(2)):
        target = rule(z, y, x, core)
        if target is not None:
            tz, ty, tx, tcore = target
            pairs.append((((z * 2 + y) * 2 + x) * 2 + core, ((tz * 2 + ty) * 2 + tx) * 2 + tcore))
    return pairs


def swap_x(z, y, x, core):
    return (z, y, 1 - x, core)


def swap_y(z, y, x, core):
    return (z, 1 - y, x, core)


def move(array, rule):
    return lax.ppermute(array, ("dp", "ctx"), chip_moves(rule))


def swap_core(array):
    return lax.ppermute(array, "ctx", [(0, 1), (1, 0)])


def at_home(rule):
    return lambda z, y, x, core: rule(z, y, x, core) if z // 2 == core else (z, y, x, 1 - core)


def near_z(z, y, x, core):
    return (z ^ 1, y, x, core)


def far_z(z, y, x, core):
    return (z ^ 2, y, x, core)


def own_axis(z, y, x, core):
    return swap_x(z, y, x, core) if core == 0 else swap_y(z, y, x, core)


def other_axis(z, y, x, core):
    return swap_y(z, y, x, core) if core == 0 else swap_x(z, y, x, core)


def scatter_first(z, y, x, core):
    return (z ^ 1, y, x, 1 - core) if z // 2 == core else (z ^ 2, y, x, core)


def scatter_second(z, y, x, core):
    return (z, y, x, 1 - core) if z // 2 == core else (z ^ 3, y, x, core)


def scatter_first(z, y, x, core):
    return (z ^ 1, y, x, 1 - core) if z // 2 == core else (z ^ 2, y, x, core)


def scatter_second(z, y, x, core):
    return (z, y, x, 1 - core) if z // 2 == core else (z ^ 3, y, x, core)


def dot_nt(a, b):
    return lax.dot_general(a, b, (((1,), (1,)), ((), ())), preferred_element_type=jnp.float32)


def dot_nn(a, b):
    return jnp.dot(a, b, preferred_element_type=jnp.float32)


def rope_table(order):
    per_axis = HD // 16
    shape = (4 * per_axis, order.shape[1])
    row = lax.broadcasted_iota(jnp.int32, shape, 0)
    axis_of, step = row // per_axis, row % per_axis
    coords = jnp.where(
        axis_of == 0,
        order % 8,
        jnp.where(axis_of == 1, order // 8 % 8, jnp.where(axis_of == 2, order // 64 % 4, order // 256)),
    )
    frequency = jnp.zeros(shape, jnp.float32)
    for i in range(per_axis):
        frequency = jnp.where(step == i, jnp.float32(100.0 ** (-i / per_axis)), frequency)
    angle = coords.astype(jnp.float32) * frequency
    return jnp.cos(angle), jnp.sin(angle)


def rotate_rows(x, cos, sin):
    quarter = HD // 4
    f, g, rest = x[0:quarter], x[quarter : 2 * quarter], x[2 * quarter :]
    return jnp.concatenate([f * cos - g * sin, g * cos + f * sin, rest], axis=0).astype(jnp.bfloat16)


def place():
    dp = lax.axis_index("dp")
    return lax.axis_index("ctx"), dp // 4, dp // 2 % 2, dp % 2


def block_bias(pattern, core, bias):
    blocks = bias.shape[0]
    lane_block = lax.broadcasted_iota(jnp.int32, (1, bias.shape[1]), 1) // BLK
    for key_local in range(blocks):
        key_block = (key_local + 2 * core) % blocks
        row = jnp.full(lane_block.shape, -jnp.inf, jnp.float32)
        for query_local in range(blocks):
            query_block = (query_local + 2 * core) % blocks
            listed = jnp.int32(0)
            for slot in range(KB):
                listed = listed + jnp.where(pattern[0, query_block, slot] == key_block, 1, 0)
            row = jnp.where((lane_block == query_local) & (listed > 0), 0.0, row)
        bias[key_local : key_local + 1, :] = row


def scaled_scores(keys, queries_t, bias):
    scores = dot_nn(keys, queries_t) * (math.log2(math.e) / math.sqrt(HD))
    parts = [scores[b * BLK : (b + 1) * BLK, :] + bias[b : b + 1, :] for b in range(bias.shape[0])]
    return jnp.concatenate(parts, axis=0)


def pack_kernel(*refs):
    order, *inputs = refs[:4]
    out, own, sems = refs[-3:]
    rows, mine = own.shape[1:]
    copies = []
    for target, core in ((out, 1 - place()[0]), (own, place()[0])):
        there = pl.ds(pl.multiple_of(core * mine, mine), mine)
        for i, a in enumerate(inputs):
            copies.append(
                pltpu.make_async_copy(a.at[:, there], target.at[i, 0:rows, :], sems.at[len(copies)])
            )
            copies[-1].start()
    digits = jnp.concatenate([order[...] // 16, order[...] % 16] + [jnp.zeros_like(order)] * 14, axis=0)
    out[0, rows:, 0:rows] = digits.astype(jnp.float32).astype(jnp.bfloat16)
    for copy in copies:
        copy.wait()


def forward_kernel(pattern, near, own, received, *refs):
    rot_q, rot_k, rot_kt, values, attn, attn_t, lse, bias, cos_ref, sin_ref = refs[-10:]
    tokens = 2 * own.shape[1]
    step = BLK
    core, z, _, _ = place()
    block_bias(pattern, core, bias)
    rows = own.shape[1]
    digits = received[0, rows:, 0:rows].astype(jnp.float32).astype(jnp.int32)
    far = digits[0:1, :] * 16 + digits[1:2, :]
    cos, sin = rope_table(jnp.concatenate([near[...], far], axis=1))
    cos_ref[...] = cos
    sin_ref[...] = sin
    for head in range(rot_q.shape[0] // HD):
        cols = slice(head * HD, (head + 1) * HD)
        taken = (head // 2 ^ z % 2) * 2 + head % 2
        taken = pl.ds(pl.multiple_of(taken * HD, HD), HD)
        query, key, value = (
            jnp.concatenate([own[i, :, taken], received[i, 0:rows, taken]], axis=0) for i in range(3)
        )
        rot_q[cols, :] = rotate_rows(query.T.astype(jnp.float32), cos, sin)
        keys_t = rotate_rows(key.T.astype(jnp.float32), cos, sin)
        rot_kt[cols, :] = keys_t
        keys = keys_t.T
        rot_k[:, cols] = keys
        values[:, cols] = value
        value_t = value.T
        for part in range(tokens // step):
            at = slice(part * step, (part + 1) * step)
            scores = scaled_scores(keys, rot_q[cols, at], bias[:, at])
            peak = jnp.max(scores, axis=0, keepdims=True)
            raised = jnp.exp2(scores - peak)
            total = jnp.sum(raised, axis=0, keepdims=True)
            mixed = dot_nn(value_t, raised.astype(jnp.bfloat16)) * (1.0 / total)
            mixed = mixed.astype(jnp.bfloat16)
            attn_t[cols, at] = mixed
            attn[at, cols] = mixed.T
            lse[head : head + 1, at] = peak + jnp.log2(total)


def weight_grad_kernel(attn_t, own, other, *refs, chunk):
    send, keep = refs[-2:]
    core, _, y, x = place()
    piece, width = send.shape[2:]
    cols = slice(chunk * width, (chunk + 1) * width)
    tokens = jnp.concatenate([own[:, cols], other[:, cols]], axis=0)
    whole = dot_nn(attn_t[...], tokens).astype(send.dtype)
    for block in range(attn_t.shape[0] // (2 * piece)):
        part = whole[block * 2 * piece : (block + 1) * 2 * piece, :]
        z_rel = block // 2
        for head_x in range(2):
            out = part[head_x * piece : (head_x + 1) * piece, :]
            first = jnp.where(core == 0, head_x ^ x, (block % 2) ^ y)
            sub = jnp.where(core == 0, (block % 2) ^ y, head_x ^ x)

            @pl.when(first == 1)
            def _():
                send[sub, z_rel] = out

            @pl.when(first == 0)
            def _():
                keep[sub, z_rel] = out


def attn_grad_kernel(attn_t, own, other, near, far, *refs, pair):
    grad_t, dots, weight = refs[-3:]
    core, _, y, x = place()
    piece = near.shape[1]
    for e3, ref in enumerate((near, far)):
        for e2 in range(2):
            y_at = jnp.where(core == 0, y ^ e2, y ^ e3)
            x_at = jnp.where(core == 0, x ^ e3, x ^ e2)
            start = (y_at * 2 + x_at) * piece
            weight[pl.ds(pl.multiple_of(start, piece), piece), :] = ref[e2]
    size = weight.shape[0]
    tokens = jnp.concatenate([own[...], other[...]], axis=0)
    rounded = dot_nt(weight[...], tokens).astype(grad_t.dtype)
    grad_t[...] = rounded
    product = rounded.astype(jnp.float32) * attn_t[pair * size : (pair + 1) * size, :].astype(jnp.float32)
    for head in range(size // HD):
        dots[head : head + 1, :] = jnp.sum(product[head * HD : (head + 1) * HD], axis=0, keepdims=True)


def projection_kernel(attn, low, high, *refs):
    out_send, out_own = refs[-2:]
    half = out_own.shape[0]
    for c in range(low.shape[1] // half):
        cols = slice(c * half, (c + 1) * half)
        part = dot_nn(attn[...], jnp.concatenate([low[:, cols], high[:, cols]], axis=0))
        out_send[:, cols] = part[half:].astype(out_send.dtype)
        out_own[:, cols] = part[:half]


def backward_kernel(rot_q, rot_k, rot_kt, values, grad_t, dots, lse, bias, cos_ref, sin_ref, *refs, pair):
    send, own = refs[-2:]
    tokens = rot_k.shape[0]
    half = tokens // 2
    step = 2 * BLK
    scale = 1.0 / math.sqrt(HD)
    cos, sin = cos_ref[...], -sin_ref[...]
    for at_head in range(2):
        head = pair * 2 + at_head
        cols = slice(head * HD, (head + 1) * HD)
        out_cols = slice(at_head * HD, (at_head + 1) * HD)
        keys, keys_t, value = rot_k[:, cols], rot_kt[cols, :], values[:, cols]
        key_sum = jnp.zeros((HD, tokens), jnp.float32)
        value_sum = jnp.zeros((HD, tokens), jnp.float32)
        query_parts = []
        for part in range(tokens // step):
            at = slice(part * step, (part + 1) * step)
            queries_t, grads_t = rot_q[cols, at], grad_t[out_cols, at]
            scores = scaled_scores(keys, queries_t, bias[:, at])
            exact = jnp.exp2(scores - lse[head : head + 1, at])
            prob_grad = dot_nn(value, grads_t)
            score_grad = (exact * (prob_grad - dots[at_head : at_head + 1, at])).astype(jnp.bfloat16)
            value_sum = value_sum + dot_nt(grads_t, exact.astype(jnp.bfloat16))
            key_sum = key_sum + dot_nt(queries_t, score_grad)
            query_parts.append(dot_nn(keys_t, score_grad))
        query_sum = jnp.concatenate(query_parts, axis=1)
        outs = (
            rotate_rows(query_sum * scale, cos, sin),
            rotate_rows(key_sum * scale, cos, sin),
            value_sum.astype(jnp.bfloat16),
        )
        for i, out in enumerate(outs):
            out = out.T
            own[i, :, out_cols] = out[0:half, :]
            send[i, :, out_cols] = out[half:, :]


def gather_pick_kernel(home0, home1, away0, away1, *refs):
    core, z, _, _ = place()
    low = refs[-1]

    @pl.when(z // 2 == core)
    def _():
        low[0] = home0[...]
        low[1] = home1[...]

    @pl.when(z // 2 != core)
    def _():
        low[0] = away0[...]
        low[1] = away1[...]


def copy_kernel(a, *refs):
    refs[-1][...] = a[...]


def second_sum_kernel(keep, got, *refs):
    send, kept = refs[-2:]
    send[...] = (keep[1].astype(jnp.float32) + got[1].astype(jnp.float32)).astype(send.dtype)
    kept[...] = keep[0].astype(jnp.float32) + got[0].astype(jnp.float32)


def z_sum_kernel(kept, got, *refs):
    to_first, to_second, own = refs[-3:]
    core, z, _, _ = place()
    at_home = z // 2 == core
    near = kept[0] + got[0].astype(jnp.float32)
    rest = kept[1] + got[1].astype(jnp.float32)
    own[...] = near
    to_first[...] = jnp.where(at_home, rest, near).astype(to_first.dtype)
    to_second[...] = rest.astype(to_second.dtype)


def share_kernel(own, first, second, *refs):
    core, z, _, _ = place()
    at_home = z // 2 == core
    total = own[...] + first[...].astype(jnp.float32) + second[...].astype(jnp.float32)
    refs[-1][...] = jnp.where(at_home, total, first[...].astype(jnp.float32))


def finish_kernel(*refs, count):
    layer_out, *grads, mean, layer_rows, mean_rows, sems = refs[-8:]
    out_own, out_got = refs[:2]
    pairs, shares = refs[2:6], refs[6:-8]
    core, z, _, _ = place()
    mine = grads[0].shape[1] // 2
    width = mine // 2
    copies = []

    def send(source, target):
        copies.append(pltpu.make_async_copy(source, target, sems.at[len(copies)]))
        copies[-1].start()

    for pair in range(2):
        for source in range(2):
            start = (core ^ source) * mine + (z % 2 ^ pair) * width
            cols = pl.ds(pl.multiple_of(start, width), width)
            for i in range(3):
                send(pairs[2 * pair + source].at[i], grads[i].at[:, cols])
    parts = 2
    size = layer_rows.shape[0] // parts
    for part in range(parts):
        rows = slice(part * size, (part + 1) * size)
        total = out_own[rows, :] + out_got[rows, :].astype(jnp.float32)
        layer_rows[rows, :] = total.astype(layer_rows.dtype)
        send(layer_rows.at[rows, :], layer_out.at[rows, :])
    width = shares[0].shape[1]
    for i in range(mean.shape[1] // width):
        total = shares[2 * i][...] + shares[2 * i + 1][...]
        mean_rows[:, i * width : (i + 1) * width] = total * (1.0 / count)
    send(mean_rows, mean)
    for copy in copies:
        copy.wait()


def chip_shards(queries, key_states, value_states, token_order, block_pattern, out_weight, out_grad):
    rows, width = queries.shape[1:]
    model = out_grad.shape[2]
    tokens, mine = 2 * rows, width // 2
    owned = out_weight.shape[0]
    bf16, f32 = jnp.bfloat16, jnp.float32
    in_vmem = pl.BlockSpec(memory_space=pltpu.VMEM)
    in_smem = pl.BlockSpec(memory_space=pltpu.SMEM)
    in_hbm = pl.BlockSpec(memory_space=pltpu.HBM)
    anywhere = pl.BlockSpec(memory_space=pl.ANY)
    done = []

    def call(kernel, name, args, outs, scratch=(), limit=8, specs=None, final=False, out_space=pltpu.VMEM):
        before = [a for a in done if not any(a is b for b in args)]
        results = pl.pallas_call(
            kernel,
            in_specs=list(specs or [in_vmem] * len(args)) + [anywhere] * len(before),
            out_specs=[pl.BlockSpec(memory_space=out_space)] * len(outs),
            out_shape=[out_space(s, d) if out_space is pltpu.HBM else jax.ShapeDtypeStruct(s, d) for s, d in outs],
            scratch_shapes=scratch,
            compiler_params=pltpu.CompilerParams(vmem_limit_bytes=limit << 20),
            cost_estimate=pl.CostEstimate(flops=KERNEL_COST, bytes_accessed=1, transcendentals=0),
            name=name,
        )(*args, *before)
        if not final:
            done[:] = results[:1]
        return results

    q_own, k_own, v_own, dy_own = queries[0], key_states[0], value_states[0], out_grad[0]
    q_in, k_in, v_in = (pltpu.with_memory_space_constraint(a, pltpu.HBM) for a in (q_own, k_own, v_own))
    pack, own = call(
        pack_kernel,
        "pack",
        (token_order, q_in, k_in, v_in),
        [((3, rows + 16, mine), bf16), ((3, rows, mine), bf16)],
        specs=[in_vmem] + [in_hbm] * 3,
        scratch=[pltpu.SemaphoreType.DMA((6,))],
        final=True,
    )
    received = swap_core(pack)
    dy_far = swap_core(dy_own)

    beyond = move(out_weight, at_home(far_z))
    beside = move(out_weight, other_axis)
    chunks = 2
    forward_results = []

    def forward():
        forward_results[:] = call(
            forward_kernel,
            "forward",
            (block_pattern, token_order, own, received),
            [((mine, tokens), bf16), ((tokens, mine), bf16), ((mine, tokens), bf16)]
            + [((tokens, mine), bf16)] * 2
            + [((mine, tokens), bf16), ((mine // HD, tokens), f32), ((tokens // BLK, tokens), f32)]
            + [((HD // 4, tokens), f32)] * 2,
            limit=24,
            specs=[in_smem] + [in_vmem] * 3,
        )

    sums = SUM_CHUNKS
    cols = model // sums
    weights, attn_grads, pairs = ([None] * chunks for _ in range(3))
    parts, z_sums, shares = [None] * sums, [None] * sums, [None] * sums
    result = {}

    def weight_grad(i):
        send, keep = call(
            functools.partial(weight_grad_kernel, chunk=i),
            "weight_grad",
            (forward_results[5], dy_own, dy_far),
            [((2, 2, owned, cols), bf16)] * 2,
            limit=16,
        )
        parts[i] = (keep, move(send, own_axis))

    def gather_beside():
        (copied,) = call(copy_kernel, "copy", (beside,), [((owned, model), bf16)])
        result["beside"] = move(copied, at_home(far_z))

    def gather_pick():
        args = (out_weight, beside, beyond, result["beside"])
        (low,) = call(gather_pick_kernel, "gather_pick", args, [((2, owned, model), bf16)])
        result["high"] = move(low, near_z)
        weights[0] = low, move(low, own_axis)

    def gather_last():
        (high,) = call(copy_kernel, "copy", (result["high"],), [((2, owned, model), bf16)])
        weights[1] = high, move(high, own_axis)

    def second_sum(i):
        send, kept = call(
            second_sum_kernel,
            "second_sum",
            parts[i],
            [((2, owned, cols), bf16), ((2, owned, cols), f32)],
        )
        parts[i] = (kept, move(send, other_axis))

    def z_sum(i):
        to_first, to_second, own = call(
            z_sum_kernel,
            "z_sum",
            parts[i],
            [((owned, cols), bf16)] * 2 + [((owned, cols), f32)],
        )
        z_sums[i] = own, move(to_first, scatter_first), move(to_second, scatter_second)

    def share(i):
        (part,) = call(share_kernel, "share", z_sums[i], [((owned, cols), f32)])
        shares[i] = part, swap_core(part)

    def attn_grad(i):
        attn_grads[i] = call(
            functools.partial(attn_grad_kernel, pair=i),
            "attn_grad",
            (forward_results[5], dy_own, dy_far, *weights[i]),
            [((2 * HD, tokens), bf16), ((2, tokens), f32), ((2 * HD, model), bf16)],
            limit=16,
        )

    def projection():
        out_send, out_own = call(
            projection_kernel,
            "projection",
            (forward_results[4], attn_grads[0][2], attn_grads[1][2]),
            [((rows, model), bf16), ((rows, model), f32)],
            limit=16,
        )
        result["out"] = (out_own, swap_core(out_send))

    def backward(i):
        send, own = call(
            functools.partial(backward_kernel, pair=i),
            "backward",
            (*forward_results[:4], *attn_grads[i][:2], *forward_results[6:]),
            [((3, rows, 2 * HD), bf16)] * 2,
            limit=24,
        )
        pairs[i] = own, swap_core(send)

    def finish():
        args = (*result["out"], *pairs[0], *pairs[1], *(a for s in shares for a in s))
        result["all"] = call(
            functools.partial(finish_kernel, count=lax.axis_size("dp")),
            "finish",
            args,
            [((rows, model), bf16)] + [((rows, width), bf16)] * 3 + [((owned, model), f32)],
            scratch=[
                pltpu.VMEM((rows, model), bf16),
                pltpu.VMEM((owned, model), f32),
                pltpu.SemaphoreType.DMA((15,)),
            ],
            limit=24,
            final=True,
            out_space=pltpu.HBM,
        )

    forward()
    weight_grad(0)
    gather_beside()
    weight_grad(1)
    gather_pick()
    second_sum(0)
    second_sum(1)
    z_sum(0)
    gather_last()
    z_sum(1)
    attn_grad(0)
    backward(0)
    share(0)
    attn_grad(1)
    projection()
    backward(1)
    share(1)
    finish()
    *sharded, weight_grad = result["all"]
    return (*[a[None] for a in sharded], weight_grad)


def solution(mesh):
    in_specs = (
        P("dp", "ctx", None),
        P("dp", "ctx", None),
        P("dp", "ctx", None),
        P("dp", "ctx"),
        P("dp", None, None),
        P("dp", None),
        P("dp", "ctx", None),
    )
    out_specs = (
        P("dp", "ctx", None),
        P("dp", "ctx", None),
        P("dp", "ctx", None),
        P("dp", "ctx", None),
        P("dp", None),
    )
    body = chip_shards if (mesh.shape["dp"], mesh.shape["ctx"]) == (16, 2) else shards
    return jax.shard_map(body, mesh=mesh, in_specs=in_specs, out_specs=out_specs, check_vma=False)
```

```python
import functools
import itertools
import math

import jax
import jax.numpy as jnp
import numpy as np
from jax import lax
from jax.experimental import pallas as pl
from jax.experimental.pallas import tpu as pltpu
from jax.sharding import PartitionSpec as P

H = 8
HD = 128
BLK = 128
KB = 4
SUM_CHUNKS = 2
KERNEL_COST = 10**10


def padded(shard, sides, width):
    for axis, dim in sides:
        devices, length = (lax.axis_size(axis), shard.shape[dim])
        up = [(i, (i + 1) % devices) for i in range(devices - 1)]
        down = [(j, i) for i, j in up]
        last = lax.slice_in_dim(shard, length - width, length, axis=dim)
        leading = lax.slice_in_dim(shard, 0, width, axis=dim)
        before = lax.ppermute(last, axis, up)
        after = lax.ppermute(leading, axis, down)
        shard = jnp.concatenate([before, shard, after], axis=dim)
    return shard


def from_behind(block, axis, distance):
    devices = range(lax.axis_size(axis))
    route = [(i - distance, i) for i in devices if i - distance in devices]
    return lax.ppermute(block, axis, route)


def rope_tables(positions):
    coords = jnp.stack(
        [positions % 8, positions // 8 % 8, positions // 64 % 4, positions // 256], axis=1
    ).astype(jnp.float32)
    per_axis = HD // 16
    frequency = 100.0 ** (-jnp.arange(per_axis, dtype=jnp.float32) / per_axis)
    angle = (coords[:, :, None] * frequency[None, None, :]).reshape(
        positions.shape[0], 4 * per_axis
    )
    return (jnp.cos(angle), jnp.sin(angle))


def rotate_heads(heads, cosine, sine_vals, direction):
    quarter = HD // 4
    first_part = heads[..., :quarter]
    second_part = heads[..., quarter : 2 * quarter]
    cos_rows = cosine[:, None, :]
    sin_rows = direction * sine_vals[:, None, :]
    return jnp.concatenate(
        [
            first_part * cos_rows - second_part * sin_rows,
            second_part * cos_rows + first_part * sin_rows,
            heads[..., 2 * quarter :],
        ],
        axis=-1,
    )


def attend_forward(query_blocks, key_sets, value_sets, key_mask, score_scale):
    scores = (
        jnp.einsum("nqhd,nkhd->nhqk", query_blocks, key_sets, preferred_element_type=jnp.float32)
        * score_scale
    )
    scores = jnp.where(key_mask[:, None, None, :], scores, -jnp.inf)
    row_peak = jnp.max(scores, axis=-1)
    row_total = jnp.sum(jnp.exp(scores - row_peak[..., None]), axis=-1)
    log_total = row_peak + jnp.log(row_total)
    soft_probs = jnp.exp(scores - log_total[..., None]).astype(jnp.bfloat16)
    block_out = jnp.einsum(
        "nhqk,nkhd->nqhd", soft_probs, value_sets, preferred_element_type=jnp.float32
    ).astype(jnp.bfloat16)
    return (block_out, log_total)


def attend_backward(
    query_blocks,
    key_sets,
    value_sets,
    key_mask,
    log_total,
    grad_dot,
    grad_blocks,
    score_scale,
    key_form,
):
    scores = (
        jnp.einsum(
            "nqhd," + key_form + "->nhqk",
            query_blocks,
            key_sets,
            preferred_element_type=jnp.float32,
        )
        * score_scale
    )
    scores = jnp.where(key_mask[:, None, None, :], scores, -jnp.inf)
    exact_probs = jnp.exp(scores - log_total[..., None])
    soft_probs = exact_probs.astype(jnp.bfloat16)
    value_part = jnp.einsum(
        "nhqk,nqhd->" + key_form, soft_probs, grad_blocks, preferred_element_type=jnp.float32
    )
    prob_grad = jnp.einsum(
        "nqhd," + key_form + "->nhqk", grad_blocks, value_sets, preferred_element_type=jnp.float32
    )
    score_grad = (exact_probs * (prob_grad - grad_dot[..., None]) * score_scale).astype(
        jnp.bfloat16
    )
    query_part = jnp.einsum(
        "nhqk," + key_form + "->nqhd", score_grad, key_sets, preferred_element_type=jnp.float32
    )
    key_part = jnp.einsum(
        "nhqk,nqhd->" + key_form, score_grad, query_blocks, preferred_element_type=jnp.float32
    )
    return (query_part, key_part, value_part)


def shards(queries, key_states, value_states, token_order, block_pattern, out_weight, out_grad):
    row_count = queries.shape[1]
    feature_width = queries.shape[2]
    local_blocks = row_count // BLK
    shard_index = lax.axis_index("ctx")
    score_scale = 1.0 / math.sqrt(HD)
    cosine, sine_vals = rope_tables(token_order[0])
    rot_query = rotate_heads(
        queries[0].astype(jnp.float32).reshape(row_count, H, HD), cosine, sine_vals, 1.0
    ).astype(jnp.bfloat16)
    rot_keys = rotate_heads(
        key_states[0].astype(jnp.float32).reshape(row_count, H, HD), cosine, sine_vals, 1.0
    ).astype(jnp.bfloat16)
    stacked = jnp.stack([rot_keys.reshape(row_count, feature_width), value_states[0]], axis=1)
    extended = padded(stacked, (("ctx", 0),), row_count)
    ext_blocks = extended.reshape(3 * local_blocks, BLK, 2, H, HD)
    pattern_rows = block_pattern[0]
    first_block = shard_index * local_blocks
    my_pattern = lax.dynamic_slice_in_dim(pattern_rows, first_block, local_blocks, 0)
    slot_valid = my_pattern >= 0
    slot_local = jnp.where(slot_valid, my_pattern - first_block + local_blocks, 0)
    gathered = jnp.take(ext_blocks, slot_local, axis=0)
    key_sets = gathered[:, :, :, 0].reshape(local_blocks, KB * BLK, H, HD)
    value_sets = gathered[:, :, :, 1].reshape(local_blocks, KB * BLK, H, HD)
    key_mask = jnp.repeat(slot_valid, BLK, axis=1)
    query_blocks = rot_query.reshape(local_blocks, BLK, H, HD)
    block_out, log_total = attend_forward(query_blocks, key_sets, value_sets, key_mask, score_scale)
    attn = block_out.reshape(row_count, feature_width)
    grad_rows = out_grad[0]
    forward_weight = lax.all_gather(out_weight, "dp", axis=0, tiled=True)
    layer_out = jnp.dot(attn, forward_weight, preferred_element_type=jnp.float32).astype(
        jnp.bfloat16
    )
    attn_grad = lax.dot_general(
        grad_rows,
        lax.all_gather(out_weight, "dp", axis=0, tiled=True),
        (((1,), (1,)), ((), ())),
        preferred_element_type=jnp.float32,
    ).astype(jnp.bfloat16)
    batch_count = lax.axis_size("dp")
    local_grad = lax.psum_scatter(
        lax.dot_general(
            attn, grad_rows, (((0,), (0,)), ((), ())), preferred_element_type=jnp.float32
        )
        / batch_count,
        "dp",
        scatter_dimension=0,
        tiled=True,
    )
    weight_grad = lax.psum(local_grad, "ctx")
    dot_rows = jnp.sum(
        (attn_grad.astype(jnp.float32) * attn.astype(jnp.float32)).reshape(row_count, H, HD),
        axis=-1,
    )
    grad_dot = dot_rows.reshape(local_blocks, BLK, H).transpose(0, 2, 1)
    grad_blocks = attn_grad.reshape(local_blocks, BLK, H, HD)
    query_part, key_part, value_part = attend_backward(
        query_blocks,
        key_sets,
        value_sets,
        key_mask,
        log_total,
        grad_dot,
        grad_blocks,
        score_scale,
        "nkhd",
    )
    query_grad = (
        rotate_heads(query_part.reshape(row_count, H, HD), cosine, sine_vals, -1.0)
        .reshape(row_count, feature_width)
        .astype(jnp.bfloat16)
    )
    keep = slot_valid.reshape(local_blocks * KB).astype(jnp.float32)[:, None, None, None, None]
    both_parts = (
        jnp.stack(
            [
                key_part.reshape(local_blocks * KB, BLK, H, HD),
                value_part.reshape(local_blocks * KB, BLK, H, HD),
            ],
            axis=2,
        )
        * keep
    )
    accumulated = (
        jnp.zeros((3 * local_blocks, BLK, 2, H, HD), jnp.float32)
        .at[slot_local.reshape(-1)]
        .add(both_parts)
    )
    accumulated = accumulated.reshape(3 * row_count, 2, feature_width)
    own_part = accumulated[row_count : 2 * row_count]
    from_right = from_behind(accumulated[:row_count], "ctx", -1)
    from_left = from_behind(accumulated[2 * row_count :], "ctx", 1)
    summed = own_part + from_right + from_left
    key_total = summed[:, 0]
    value_total = summed[:, 1]
    key_grad = (
        rotate_heads(key_total.reshape(row_count, H, HD), cosine, sine_vals, -1.0)
        .reshape(row_count, feature_width)
        .astype(jnp.bfloat16)
    )
    value_grad = value_total.astype(jnp.bfloat16)
    return (layer_out[None], query_grad[None], key_grad[None], value_grad[None], weight_grad)

def chip_moves(rule):
    pairs = []
    for z, y, x, core in itertools.product(range(4), range(2), range(2), range(2)):
        target = rule(z, y, x, core)
        if target is not None:
            tz, ty, tx, tcore = target
            pairs.append((((z * 2 + y) * 2 + x) * 2 + core, ((tz * 2 + ty) * 2 + tx) * 2 + tcore))
    return pairs


def swap_x(z, y, x, core):
    return (z, y, 1 - x, core)


def swap_y(z, y, x, core):
    return (z, 1 - y, x, core)


def move(array, rule):
    return lax.ppermute(array, ("dp", "ctx"), chip_moves(rule))


def swap_core(array):
    return lax.ppermute(array, "ctx", [(0, 1), (1, 0)])


def at_home(rule):
    return lambda z, y, x, core: rule(z, y, x, core) if z // 2 == core else (z, y, x, 1 - core)


def near_z(z, y, x, core):
    return (z ^ 1, y, x, core)


def far_z(z, y, x, core):
    return (z ^ 2, y, x, core)


def own_axis(z, y, x, core):
    return swap_x(z, y, x, core) if core == 0 else swap_y(z, y, x, core)


def other_axis(z, y, x, core):
    return swap_y(z, y, x, core) if core == 0 else swap_x(z, y, x, core)


def scatter_first(z, y, x, core):
    return (z ^ 1, y, x, 1 - core) if z // 2 == core else (z ^ 2, y, x, core)


def scatter_second(z, y, x, core):
    return (z, y, x, 1 - core) if z // 2 == core else (z ^ 3, y, x, core)


def scatter_first(z, y, x, core):
    return (z ^ 1, y, x, 1 - core) if z // 2 == core else (z ^ 2, y, x, core)


def scatter_second(z, y, x, core):
    return (z, y, x, 1 - core) if z // 2 == core else (z ^ 3, y, x, core)


def dot_nt(a, b):
    return lax.dot_general(a, b, (((1,), (1,)), ((), ())), preferred_element_type=jnp.float32)


def dot_nn(a, b):
    return jnp.dot(a, b, preferred_element_type=jnp.float32)


def rope_table(order):
    per_axis = HD // 16
    shape = (4 * per_axis, order.shape[1])
    row = lax.broadcasted_iota(jnp.int32, shape, 0)
    axis_of, step = row // per_axis, row % per_axis
    coords = jnp.where(
        axis_of == 0,
        order % 8,
        jnp.where(axis_of == 1, order // 8 % 8, jnp.where(axis_of == 2, order // 64 % 4, order // 256)),
    )
    frequency = jnp.zeros(shape, jnp.float32)
    for i in range(per_axis):
        frequency = jnp.where(step == i, jnp.float32(100.0 ** (-i / per_axis)), frequency)
    angle = coords.astype(jnp.float32) * frequency
    return jnp.cos(angle), jnp.sin(angle)


def rotate_rows(x, cos, sin):
    quarter = HD // 4
    f, g, rest = x[0:quarter], x[quarter : 2 * quarter], x[2 * quarter :]
    return jnp.concatenate([f * cos - g * sin, g * cos + f * sin, rest], axis=0).astype(jnp.bfloat16)


def place():
    dp = lax.axis_index("dp")
    return lax.axis_index("ctx"), dp // 4, dp // 2 % 2, dp % 2


def block_bias(pattern, core, bias):
    blocks = bias.shape[0]
    lane_block = lax.broadcasted_iota(jnp.int32, (1, bias.shape[1]), 1) // BLK
    for key_local in range(blocks):
        key_block = (key_local + 2 * core) % blocks
        row = jnp.full(lane_block.shape, -jnp.inf, jnp.float32)
        for query_local in range(blocks):
            query_block = (query_local + 2 * core) % blocks
            listed = jnp.int32(0)
            for slot in range(KB):
                listed = listed + jnp.where(pattern[0, query_block, slot] == key_block, 1, 0)
            row = jnp.where((lane_block == query_local) & (listed > 0), 0.0, row)
        bias[key_local : key_local + 1, :] = row


def scaled_scores(keys, queries_t, bias):
    scores = dot_nn(keys, queries_t) * (math.log2(math.e) / math.sqrt(HD))
    parts = [scores[b * BLK : (b + 1) * BLK, :] + bias[b : b + 1, :] for b in range(bias.shape[0])]
    return jnp.concatenate(parts, axis=0)


def pack_kernel(*refs):
    order, *inputs = refs[:4]
    out, own, sems = refs[-3:]
    rows, mine = own.shape[1:]
    copies = []
    for target, core in ((out, 1 - place()[0]), (own, place()[0])):
        there = pl.ds(pl.multiple_of(core * mine, mine), mine)
        for i, a in enumerate(inputs):
            copies.append(
                pltpu.make_async_copy(a.at[:, there], target.at[i, 0:rows, :], sems.at[len(copies)])
            )
            copies[-1].start()
    digits = jnp.concatenate([order[...] // 16, order[...] % 16] + [jnp.zeros_like(order)] * 14, axis=0)
    out[0, rows:, 0:rows] = digits.astype(jnp.float32).astype(jnp.bfloat16)
    for copy in copies:
        copy.wait()


def forward_kernel(pattern, near, own, received, *refs):
    rot_q, rot_k, rot_kt, values, attn, attn_t, lse, bias, cos_ref, sin_ref = refs[-10:]
    tokens = 2 * own.shape[1]
    step = BLK
    core, z, _, _ = place()
    block_bias(pattern, core, bias)
    rows = own.shape[1]
    digits = received[0, rows:, 0:rows].astype(jnp.float32).astype(jnp.int32)
    far = digits[0:1, :] * 16 + digits[1:2, :]
    cos, sin = rope_table(jnp.concatenate([near[...], far], axis=1))
    cos_ref[...] = cos
    sin_ref[...] = sin
    for head in range(rot_q.shape[0] // HD):
        cols = slice(head * HD, (head + 1) * HD)
        taken = (head // 2 ^ z % 2) * 2 + head % 2
        taken = pl.ds(pl.multiple_of(taken * HD, HD), HD)
        query, key, value = (
            jnp.concatenate([own[i, :, taken], received[i, 0:rows, taken]], axis=0) for i in range(3)
        )
        rot_q[cols, :] = rotate_rows(query.T.astype(jnp.float32), cos, sin)
        keys_t = rotate_rows(key.T.astype(jnp.float32), cos, sin)
        rot_kt[cols, :] = keys_t
        keys = keys_t.T
        rot_k[:, cols] = keys
        values[:, cols] = value
        value_t = value.T
        for part in range(tokens // step):
            at = slice(part * step, (part + 1) * step)
            scores = scaled_scores(keys, rot_q[cols, at], bias[:, at])
            peak = jnp.max(scores, axis=0, keepdims=True)
            raised = jnp.exp2(scores - peak)
            total = jnp.sum(raised, axis=0, keepdims=True)
            mixed = dot_nn(value_t, raised.astype(jnp.bfloat16)) * (1.0 / total)
            mixed = mixed.astype(jnp.bfloat16)
            attn_t[cols, at] = mixed
            attn[at, cols] = mixed.T
            lse[head : head + 1, at] = peak + jnp.log2(total)


def weight_grad_kernel(attn_t, own, other, *refs, chunk):
    send, keep = refs[-2:]
    core, _, y, x = place()
    piece, width = send.shape[2:]
    cols = slice(chunk * width, (chunk + 1) * width)
    tokens = jnp.concatenate([own[:, cols], other[:, cols]], axis=0)
    whole = dot_nn(attn_t[...], tokens).astype(send.dtype)
    for block in range(attn_t.shape[0] // (2 * piece)):
        part = whole[block * 2 * piece : (block + 1) * 2 * piece, :]
        z_rel = block // 2
        for head_x in range(2):
            out = part[head_x * piece : (head_x + 1) * piece, :]
            first = jnp.where(core == 0, head_x ^ x, (block % 2) ^ y)
            sub = jnp.where(core == 0, (block % 2) ^ y, head_x ^ x)

            @pl.when(first == 1)
            def _():
                send[sub, z_rel] = out

            @pl.when(first == 0)
            def _():
                keep[sub, z_rel] = out


def attn_grad_kernel(attn_t, own, other, near, far, *refs, pair):
    grad_t, dots, weight = refs[-3:]
    core, _, y, x = place()
    piece = near.shape[1]
    for e3, ref in enumerate((near, far)):
        for e2 in range(2):
            y_at = jnp.where(core == 0, y ^ e2, y ^ e3)
            x_at = jnp.where(core == 0, x ^ e3, x ^ e2)
            start = (y_at * 2 + x_at) * piece
            weight[pl.ds(pl.multiple_of(start, piece), piece), :] = ref[e2]
    size = weight.shape[0]
    tokens = jnp.concatenate([own[...], other[...]], axis=0)
    rounded = dot_nt(weight[...], tokens).astype(grad_t.dtype)
    grad_t[...] = rounded
    product = rounded.astype(jnp.float32) * attn_t[pair * size : (pair + 1) * size, :].astype(jnp.float32)
    for head in range(size // HD):
        dots[head : head + 1, :] = jnp.sum(product[head * HD : (head + 1) * HD], axis=0, keepdims=True)


def projection_kernel(attn, low, high, *refs):
    out_send, out_own = refs[-2:]
    half = out_own.shape[0]
    for c in range(low.shape[1] // half):
        cols = slice(c * half, (c + 1) * half)
        part = dot_nn(attn[...], jnp.concatenate([low[:, cols], high[:, cols]], axis=0))
        out_send[:, cols] = part[half:].astype(out_send.dtype)
        out_own[:, cols] = part[:half]


def backward_kernel(rot_q, rot_k, rot_kt, values, grad_t, dots, lse, bias, cos_ref, sin_ref, *refs, pair):
    send, own = refs[-2:]
    tokens = rot_k.shape[0]
    half = tokens // 2
    step = 4 * BLK
    scale = 1.0 / math.sqrt(HD)
    cos, sin = cos_ref[...], -sin_ref[...]
    for at_head in range(2):
        head = pair * 2 + at_head
        cols = slice(head * HD, (head + 1) * HD)
        out_cols = slice(at_head * HD, (at_head + 1) * HD)
        keys, keys_t, value = rot_k[:, cols], rot_kt[cols, :], values[:, cols]
        key_sum = jnp.zeros((HD, tokens), jnp.float32)
        value_sum = jnp.zeros((HD, tokens), jnp.float32)
        query_parts = []
        for part in range(tokens // step):
            at = slice(part * step, (part + 1) * step)
            queries_t, grads_t = rot_q[cols, at], grad_t[out_cols, at]
            scores = scaled_scores(keys, queries_t, bias[:, at])
            exact = jnp.exp2(scores - lse[head : head + 1, at])
            prob_grad = dot_nn(value, grads_t)
            score_grad = (exact * (prob_grad - dots[at_head : at_head + 1, at])).astype(jnp.bfloat16)
            value_sum = value_sum + dot_nt(grads_t, exact.astype(jnp.bfloat16))
            key_sum = key_sum + dot_nt(queries_t, score_grad)
            query_parts.append(dot_nn(keys_t, score_grad))
        query_sum = jnp.concatenate(query_parts, axis=1)
        outs = (
            rotate_rows(query_sum * scale, cos, sin),
            rotate_rows(key_sum * scale, cos, sin),
            value_sum.astype(jnp.bfloat16),
        )
        for i, out in enumerate(outs):
            out = out.T
            own[i, :, out_cols] = out[0:half, :]
            send[i, :, out_cols] = out[half:, :]


def gather_pick_kernel(home0, home1, away0, away1, *refs):
    core, z, _, _ = place()
    low = refs[-1]

    @pl.when(z // 2 == core)
    def _():
        low[0] = home0[...]
        low[1] = home1[...]

    @pl.when(z // 2 != core)
    def _():
        low[0] = away0[...]
        low[1] = away1[...]


def copy_kernel(a, *refs):
    refs[-1][...] = a[...]


def second_sum_kernel(keep, got, *refs):
    send, kept = refs[-2:]
    send[...] = (keep[1].astype(jnp.float32) + got[1].astype(jnp.float32)).astype(send.dtype)
    kept[...] = keep[0].astype(jnp.float32) + got[0].astype(jnp.float32)


def z_sum_kernel(kept, got, *refs):
    to_first, to_second, own = refs[-3:]
    core, z, _, _ = place()
    at_home = z // 2 == core
    near = kept[0] + got[0].astype(jnp.float32)
    rest = kept[1] + got[1].astype(jnp.float32)
    own[...] = near
    to_first[...] = jnp.where(at_home, rest, near).astype(to_first.dtype)
    to_second[...] = rest.astype(to_second.dtype)


def share_kernel(own, first, second, *refs):
    core, z, _, _ = place()
    at_home = z // 2 == core
    total = own[...] + first[...].astype(jnp.float32) + second[...].astype(jnp.float32)
    refs[-1][...] = jnp.where(at_home, total, first[...].astype(jnp.float32))


def finish_kernel(*refs, count):
    layer_out, *grads, mean, layer_rows, mean_rows, sems = refs[-8:]
    out_own, out_got = refs[:2]
    pairs, shares = refs[2:6], refs[6:-8]
    core, z, _, _ = place()
    mine = grads[0].shape[1] // 2
    width = mine // 2
    copies = []

    def send(source, target):
        copies.append(pltpu.make_async_copy(source, target, sems.at[len(copies)]))
        copies[-1].start()

    for pair in range(2):
        for source in range(2):
            start = (core ^ source) * mine + (z % 2 ^ pair) * width
            cols = pl.ds(pl.multiple_of(start, width), width)
            for i in range(3):
                send(pairs[2 * pair + source].at[i], grads[i].at[:, cols])
    parts = 2
    size = layer_rows.shape[0] // parts
    for part in range(parts):
        rows = slice(part * size, (part + 1) * size)
        total = out_own[rows, :] + out_got[rows, :].astype(jnp.float32)
        layer_rows[rows, :] = total.astype(layer_rows.dtype)
        send(layer_rows.at[rows, :], layer_out.at[rows, :])
    width = shares[0].shape[1]
    for i in range(mean.shape[1] // width):
        total = shares[2 * i][...] + shares[2 * i + 1][...]
        mean_rows[:, i * width : (i + 1) * width] = total * (1.0 / count)
    send(mean_rows, mean)
    for copy in copies:
        copy.wait()


def chip_shards(queries, key_states, value_states, token_order, block_pattern, out_weight, out_grad):
    rows, width = queries.shape[1:]
    model = out_grad.shape[2]
    tokens, mine = 2 * rows, width // 2
    owned = out_weight.shape[0]
    bf16, f32 = jnp.bfloat16, jnp.float32
    in_vmem = pl.BlockSpec(memory_space=pltpu.VMEM)
    in_smem = pl.BlockSpec(memory_space=pltpu.SMEM)
    in_hbm = pl.BlockSpec(memory_space=pltpu.HBM)
    anywhere = pl.BlockSpec(memory_space=pl.ANY)
    done = []

    def call(kernel, name, args, outs, scratch=(), limit=8, specs=None, final=False, out_space=pltpu.VMEM):
        before = [a for a in done if not any(a is b for b in args)]
        results = pl.pallas_call(
            kernel,
            in_specs=list(specs or [in_vmem] * len(args)) + [anywhere] * len(before),
            out_specs=[pl.BlockSpec(memory_space=out_space)] * len(outs),
            out_shape=[out_space(s, d) if out_space is pltpu.HBM else jax.ShapeDtypeStruct(s, d) for s, d in outs],
            scratch_shapes=scratch,
            compiler_params=pltpu.CompilerParams(vmem_limit_bytes=limit << 20),
            cost_estimate=pl.CostEstimate(flops=KERNEL_COST, bytes_accessed=1, transcendentals=0),
            name=name,
        )(*args, *before)
        if not final:
            done[:] = results[:1]
        return results

    q_own, k_own, v_own, dy_own = queries[0], key_states[0], value_states[0], out_grad[0]
    q_in, k_in, v_in = (pltpu.with_memory_space_constraint(a, pltpu.HBM) for a in (q_own, k_own, v_own))
    pack, own = call(
        pack_kernel,
        "pack",
        (token_order, q_in, k_in, v_in),
        [((3, rows + 16, mine), bf16), ((3, rows, mine), bf16)],
        specs=[in_vmem] + [in_hbm] * 3,
        scratch=[pltpu.SemaphoreType.DMA((6,))],
        final=True,
    )
    received = swap_core(pack)
    dy_far = swap_core(dy_own)

    beyond = move(out_weight, at_home(far_z))
    beside = move(out_weight, other_axis)
    chunks = 2
    forward_results = []

    def forward():
        forward_results[:] = call(
            forward_kernel,
            "forward",
            (block_pattern, token_order, own, received),
            [((mine, tokens), bf16), ((tokens, mine), bf16), ((mine, tokens), bf16)]
            + [((tokens, mine), bf16)] * 2
            + [((mine, tokens), bf16), ((mine // HD, tokens), f32), ((tokens // BLK, tokens), f32)]
            + [((HD // 4, tokens), f32)] * 2,
            limit=24,
            specs=[in_smem] + [in_vmem] * 3,
        )

    sums = SUM_CHUNKS
    cols = model // sums
    weights, attn_grads, pairs = ([None] * chunks for _ in range(3))
    parts, z_sums, shares = [None] * sums, [None] * sums, [None] * sums
    result = {}

    def weight_grad(i):
        send, keep = call(
            functools.partial(weight_grad_kernel, chunk=i),
            "weight_grad",
            (forward_results[5], dy_own, dy_far),
            [((2, 2, owned, cols), bf16)] * 2,
            limit=16,
        )
        parts[i] = (keep, move(send, own_axis))

    def gather_beside():
        (copied,) = call(copy_kernel, "copy", (beside,), [((owned, model), bf16)])
        result["beside"] = move(copied, at_home(far_z))

    def gather_pick():
        args = (out_weight, beside, beyond, result["beside"])
        (low,) = call(gather_pick_kernel, "gather_pick", args, [((2, owned, model), bf16)])
        result["high"] = move(low, near_z)
        weights[0] = low, move(low, own_axis)

    def gather_last():
        (high,) = call(copy_kernel, "copy", (result["high"],), [((2, owned, model), bf16)])
        weights[1] = high, move(high, own_axis)

    def second_sum(i):
        send, kept = call(
            second_sum_kernel,
            "second_sum",
            parts[i],
            [((2, owned, cols), bf16), ((2, owned, cols), f32)],
        )
        parts[i] = (kept, move(send, other_axis))

    def z_sum(i):
        to_first, to_second, own = call(
            z_sum_kernel,
            "z_sum",
            parts[i],
            [((owned, cols), bf16)] * 2 + [((owned, cols), f32)],
        )
        z_sums[i] = own, move(to_first, scatter_first), move(to_second, scatter_second)

    def share(i):
        (part,) = call(share_kernel, "share", z_sums[i], [((owned, cols), f32)])
        shares[i] = part, swap_core(part)

    def attn_grad(i):
        attn_grads[i] = call(
            functools.partial(attn_grad_kernel, pair=i),
            "attn_grad",
            (forward_results[5], dy_own, dy_far, *weights[i]),
            [((2 * HD, tokens), bf16), ((2, tokens), f32), ((2 * HD, model), bf16)],
            limit=16,
        )

    def projection():
        out_send, out_own = call(
            projection_kernel,
            "projection",
            (forward_results[4], attn_grads[0][2], attn_grads[1][2]),
            [((rows, model), bf16), ((rows, model), f32)],
            limit=16,
        )
        result["out"] = (out_own, swap_core(out_send))

    def backward(i):
        send, own = call(
            functools.partial(backward_kernel, pair=i),
            "backward",
            (*forward_results[:4], *attn_grads[i][:2], *forward_results[6:]),
            [((3, rows, 2 * HD), bf16)] * 2,
            limit=24,
        )
        pairs[i] = own, swap_core(send)

    def finish():
        args = (*result["out"], *pairs[0], *pairs[1], *(a for s in shares for a in s))
        result["all"] = call(
            functools.partial(finish_kernel, count=lax.axis_size("dp")),
            "finish",
            args,
            [((rows, model), bf16)] + [((rows, width), bf16)] * 3 + [((owned, model), f32)],
            scratch=[
                pltpu.VMEM((rows, model), bf16),
                pltpu.VMEM((owned, model), f32),
                pltpu.SemaphoreType.DMA((15,)),
            ],
            limit=24,
            final=True,
            out_space=pltpu.HBM,
        )

    forward()
    weight_grad(0)
    gather_beside()
    weight_grad(1)
    gather_pick()
    second_sum(0)
    second_sum(1)
    z_sum(0)
    gather_last()
    z_sum(1)
    attn_grad(0)
    backward(0)
    share(0)
    attn_grad(1)
    projection()
    backward(1)
    share(1)
    finish()
    *sharded, weight_grad = result["all"]
    return (*[a[None] for a in sharded], weight_grad)


def solution(mesh):
    in_specs = (
        P("dp", "ctx", None),
        P("dp", "ctx", None),
        P("dp", "ctx", None),
        P("dp", "ctx"),
        P("dp", None, None),
        P("dp", None),
        P("dp", "ctx", None),
    )
    out_specs = (
        P("dp", "ctx", None),
        P("dp", "ctx", None),
        P("dp", "ctx", None),
        P("dp", "ctx", None),
        P("dp", None),
    )
    body = chip_shards if (mesh.shape["dp"], mesh.shape["ctx"]) == (16, 2) else shards
    return jax.shard_map(body, mesh=mesh, in_specs=in_specs, out_specs=out_specs, check_vma=False)
```
